32 devices in a mesh: region: 4 (over z), dev: 8 (over y, x, core).
Axes of the slice: x: 2, y: 2, z: 4, core: 2. Of those that a mesh axis runs over, the one named last changes fastest.
Arguments:
- basis_values: bfloat16 [384, 4, 256, 128], P(('region', 'dev')), may hold values from -6 to 6
- density_rows: bfloat16 [96, 4, 128, 128], P(('region', 'dev')), may hold values from -0.013671875 to 0.013671875
- block_mask: int32 [96, 4], P(('region', 'dev')), may hold values 0 or 1
- window_start: int32 [32], P(('region', 'dev')), may hold values from 0 to 23
- batch_offsets: int32 [32, 12], P(('region', 'dev')), may hold values from 0 to 4, as said below
- batch_sizes: int32 [32, 12], P(('region', 'dev')), may hold values from 1 to 256, 1920 in all within a row
- atom_near: int32 [384, 6], P(('region', 'dev')), may hold values from 0 to 383
- harmonics: bfloat16 [384, 6, 25, 256], P(('region', 'dev')), may hold values from -6 to 6
- partition: float32 [384, 6, 256], P(('region', 'dev')), may hold values from 0.002 to 0.05
- radius: float32 [384, 6, 256], P(('region', 'dev')), may hold values from 0 to 15
- radial_table: float32 [25, 16], replicated, may hold values from -1.5 to 1.5
Outputs:
- density: float32 [384, 256], P(('region', 'dev'))
- moments: float32 [25, 512], P(None, ('region', 'dev'))
- potential: float32 [384, 256], P(('region', 'dev'))
The draws below stay inside these ranges and needn't reach their ends.
Inputs may be any that keep to these rules, and one draw needn't show every extreme that they name: The blocks of a batch are positions batch_offsets to batch_offsets + 3 of its device's window of 8 consecutive blocks.
All inputs are finite; a program needn't handle non-finite values. No bound on the sum of `block_mask` on one device may be relied on, other than what follows from the above.
Results may differ from the reference program's by a relative error of at most 0.0029.
Values may be sent and summed in bfloat16 or wider, within the bound.
No kernel may reach another device: no remote copies, remote signals or barrier semaphores. Data moves between devices by JAX's collectives and lax.ppermute only.
A program may use at most 64 MiB of HBM per device.

```python
import math
import jax
import jax.numpy as jnp
import numpy as np
from jax import lax

BS = 128
PTS = 256
NNB = 4
KB = 4
BLK_DEV = 3
LM = 25
NR = 16
NAT = 6
ATOM_DEV = 16
BATCH_DEV = 12
WIN = 8
NB = 24
ATOMS = 512
NBT = 384
TOTAL_DEV = 1920
N_REGION = 4
N_DEV = 8


def draw_batch_offsets(key, part):
    row_total = N_REGION * N_DEV
    top_value = WIN - NNB
    drawn = jax.random.randint(jax.random.fold_in(key, 11), (row_total, BATCH_DEV), 0, top_value + 1)
    low_position = jax.random.randint(jax.random.fold_in(key, 12), (row_total, 1), 0, BATCH_DEV)
    step_value = jax.random.randint(jax.random.fold_in(key, 13), (row_total, 1), 1, BATCH_DEV)
    high_position = (low_position + step_value) % BATCH_DEV
    column = jnp.arange(BATCH_DEV)[None, :]
    drawn = jnp.where(column == low_position, 0, drawn)
    drawn = jnp.where(column == high_position, top_value, drawn)
    return drawn.astype(jnp.int32)


def set_ends(result, rng, least, high):
    longest = result.shape.index(max(result.shape))
    spots = []
    for shift in (0, 1):
        where = [jax.random.randint(jax.random.fold_in(rng, axis), (), 0, length) for axis, length in enumerate(result.shape)]
        where[longest] = (where[longest] + shift) % result.shape[longest]
        spots.append(tuple(where))
    return result.at[spots[0]].set(least).at[spots[1]].set(high)


def block_levels(rng, extent, pieces, least, high):
    factor_of = 1.0
    for position, blocks in pieces:
        draws = jax.random.uniform(jax.random.fold_in(jax.random.fold_in(rng, 6), position), (blocks,), jnp.float32, least / len(pieces), high / len(pieces))
        factor_of = factor_of * jnp.repeat(jnp.exp(draws), extent[position] // blocks).reshape((-1,) + (1,) * (len(extent) - 1 - position))
    return factor_of


def split_up(count, total, most, slope):
    weights = [(1 << 20) // math.isqrt(rank ** slope) + 1 for rank in range(2, count + 1)]
    rest, counts = total - most - (count - 1), [1] * (count - 1)
    while rest > 0:
        movable = [i for i in range(count - 1) if counts[i] < most]
        mass, left = sum([weights[i] for i in movable]), rest
        for i in movable:
            extra = min(most - counts[i], max(1, left * weights[i] // mass), rest)
            counts[i] = counts[i] + extra
            rest = rest - extra
    return np.array([most] + counts)


def ragged_sizes(stream_key, amount, total, bound, slope):
    if amount == 2:
        one = jax.random.randint(stream_key, (), max(1, total - bound), min(bound, total - 1) + 1)
        return jnp.stack([one, total - one])
    lengths = jnp.asarray(split_up(amount, total, bound, slope), jnp.int32)
    twos = (amount - 1) // 2
    source_of, receiver = lengths[1:1 + 2 * twos:2], lengths[2:2 + 2 * twos:2]
    margin = jnp.minimum(source_of - 1, bound - receiver)
    moved = jax.random.randint(jax.random.fold_in(stream_key, 1), (twos,), 0, 1 << 20) % (margin + 1)
    lengths = lengths.at[1:1 + 2 * twos:2].set(source_of - moved).at[2:2 + 2 * twos:2].set(receiver + moved)
    return lengths[jax.random.permutation(jax.random.fold_in(stream_key, 2), amount)]


def scatter_about(key, dims, scale, reach, cuts=(), held_as=jnp.bfloat16):
    level = block_levels(key, dims, cuts, -0.22, 0.18) if cuts else 1.0
    values = jax.random.normal(key, dims, jnp.float32) * scale * level
    return jnp.minimum(jnp.maximum(values, -reach), reach).astype(held_as)


def setup_inputs(seed: int = 0) -> dict:
    key_of = jax.random.split(jax.random.key(seed), 12)
    return {
        "basis_values": scatter_about(key_of[0], (NBT, NNB, PTS, BS), 1.0, 6.0, ((0, 32),)),
        "density_rows": scatter_about(key_of[1], (N_REGION * NB, KB, BS, BS), (12 * BS * BS) ** -0.5, 0.013671875, ((0, 32),)),
        "block_mask": set_ends((jax.random.randint(key_of[2], (N_REGION * NB, KB), 0, 4) < 3).astype(jnp.int32), jax.random.fold_in(key_of[2], 1), 0, 1),
        "window_start": set_ends(jax.random.randint(key_of[3], (N_REGION * N_DEV,), 0, BLK_DEV * N_DEV), jax.random.fold_in(key_of[3], 1), 0, (BLK_DEV * N_DEV) - 1).astype(jnp.int32),
        "batch_offsets": draw_batch_offsets(jax.random.fold_in(key_of[11], 71), 0),
        "batch_sizes": jax.vmap(lambda own: ragged_sizes(own, BATCH_DEV, TOTAL_DEV, PTS, 2))(jax.random.split(key_of[5], (N_REGION * N_DEV))).reshape((N_REGION * N_DEV, BATCH_DEV)).astype(jnp.int32),
        "atom_near": set_ends(jax.random.randint(key_of[6], (NBT, NAT), 0, 3 * ATOM_DEV * N_DEV), jax.random.fold_in(key_of[6], 1), 0, (3 * ATOM_DEV * N_DEV) - 1).astype(jnp.int32),
        "harmonics": scatter_about(key_of[7], (NBT, NAT, LM, PTS), 1.0, 6.0, ((0, 32),)),
        "partition": jnp.clip(jnp.exp(math.log(0.05) - 3.218876 * jax.random.uniform(key_of[8], (NBT, NAT, PTS), jnp.float32) ** block_levels(key_of[8], (NBT, NAT, PTS), ((0, 32),), -0.2, 0.2)), 0.002, 0.05),
        "radius": jnp.clip(15.0 * jax.random.uniform(key_of[9], (NBT, NAT, PTS), jnp.float32) ** block_levels(key_of[9], (NBT, NAT, PTS), ((0, 32),), -0.2, 0.2), 0.0, 15.0),
        "radial_table": scatter_about(key_of[10], (LM, NR), 0.1, 1.5, (), jnp.float32),
    }


def spline_basis(radii_row, knot_count):
    knot_points = jnp.arange(knot_count).astype(jnp.float32)
    distance = jnp.abs(radii_row[..., None, :] - knot_points[:, None])
    inner_part = 2.0 / 3.0 - distance * distance + 0.5 * distance * distance * distance
    remote = 2.0 - distance
    outer_part = remote * remote * remote / 6.0
    return jnp.where(distance < 1.0, inner_part, jnp.where(distance < 2.0, outer_part, 0.0))


def batch_density(values, row_blocks):
    block_total = values.shape[0]
    band_width = row_blocks.shape[1]
    leading = jnp.zeros((1,) + values.shape[1:], values.dtype)
    trailing = jnp.zeros((band_width - 2,) + values.shape[1:], values.dtype)
    padded = jnp.concatenate([leading, values, trailing], axis=0)
    stacked = jnp.stack([padded[column:column + block_total] for column in range(band_width)], axis=2)
    mixed_rows = jnp.einsum("jpkf,jkgf->jpg", stacked.astype(jnp.float32), row_blocks.astype(jnp.float32), precision=lax.Precision.HIGHEST)
    return jnp.sum(values.astype(jnp.float32) * mixed_rows, axis=(0, 2))


def reference(basis_values, density_rows, block_mask, window_start, batch_offsets, batch_sizes, atom_near, harmonics, partition, radius, radial_table):
    block_count = BLK_DEV * N_DEV
    atom_region = ATOM_DEV * N_DEV
    masked = density_rows * block_mask.astype(jnp.bfloat16)[:, :, None, None]
    batch_total = basis_values.shape[0]
    device_of = jnp.arange(batch_total, dtype=jnp.int32) // BATCH_DEV
    region_of = device_of // N_DEV
    first_block = window_start[device_of] + batch_offsets.reshape(-1)
    alive_mask = (jnp.arange(PTS, dtype=jnp.int32)[None, :] < batch_sizes.reshape(-1)[:, None]).astype(jnp.float32)

    def one_density(batch_item):
        values, start_block, region_index = batch_item
        spatial = (start_block + jnp.arange(NNB, dtype=jnp.int32)) % block_count
        stored = region_index * block_count + (spatial % N_DEV) * BLK_DEV + spatial // N_DEV
        row_blocks = jnp.take(masked, stored.astype(jnp.int32), axis=0)
        return batch_density(values, row_blocks)

    density = lax.map(one_density, (basis_values, first_block, region_of)) * alive_mask

    def one_terms(batch_item):
        weights, dens_row, harmonic = batch_item
        return jnp.einsum("ip,ilp->il", weights * dens_row[None, :], harmonic.astype(jnp.float32), precision=lax.Precision.HIGHEST)

    moment_terms = lax.map(one_terms, (partition, density, harmonics))
    near_region = (region_of[:, None] + atom_near // atom_region - 1) % N_REGION
    target = (near_region * atom_region + atom_near % atom_region).astype(jnp.int32)
    summed = jax.ops.segment_sum(moment_terms.reshape(-1, moment_terms.shape[-1]), target.reshape(-1), num_segments=ATOMS)
    moments = summed.T
    spline_table = (summed[:, :, None] * radial_table[None, :, :]).astype(jnp.bfloat16)

    def one_potential(batch_item):
        selected, harmonic, radii_row = batch_item
        rows_here = jnp.take(spline_table, selected, axis=0).astype(jnp.float32)
        spline = spline_basis(radii_row, NR)
        radial = jnp.einsum("ilr,irp->ilp", rows_here, spline, precision=lax.Precision.HIGHEST)
        return jnp.sum(harmonic.astype(jnp.float32) * radial, axis=(0, 1))

    potential = lax.map(one_potential, (target, harmonics, radius)) * alive_mask
    return (density, moments, potential)
```

```python
import functools
import jax
import jax.numpy as jnp
from jax import lax
from jax.experimental import pallas as pl
from jax.experimental.pallas import tpu as pltpu
from jax.sharding import PartitionSpec as P

LANES = 128
ROWS = 32
SLOT = 8
NT = (((1,), (1,)), ((), ()))
NN = (((1,), (0,)), ((), ()))
VMEM = pl.BlockSpec(memory_space=pltpu.VMEM)
SMEM = pl.BlockSpec(memory_space=pltpu.SMEM)
PARAMS = pltpu.CompilerParams(vmem_limit_bytes=40 * 1024 * 1024)


def dot(a, b, dims=NN):
    return lax.dot_general(a, b, dims, preferred_element_type=jnp.float32)


def split2(x):
    hi = x.astype(jnp.bfloat16)
    lo = (x - hi.astype(jnp.float32)).astype(jnp.bfloat16)
    return hi, lo


def split3(x):
    hi, mid = split2(x)
    rest = x - hi.astype(jnp.float32) - mid.astype(jnp.float32)
    return hi, mid, rest.astype(jnp.bfloat16)


def cubic(distance):
    inner = 2.0 / 3.0 - distance * distance + 0.5 * distance * distance * distance
    remote = 2.0 - distance
    outer = remote * remote * remote * (1.0 / 6.0)
    return jnp.where(distance < 1.0, inner, jnp.where(distance < 2.0, outer, 0.0))


def pre_kernel(harm_ref, radius_ref, table_ref, g_ref, hpad_ref):
    batches, near, comps, points = harm_ref.shape
    knots = table_ref.shape[1]
    hpad_ref[...] = jnp.zeros(hpad_ref.shape, hpad_ref.dtype)
    r_hi, r_lo = split2(table_ref[...])
    coeffs = jnp.concatenate([r_hi, r_hi, r_lo], axis=1)
    knot = lax.broadcasted_iota(jnp.int32, (knots, points), 0).astype(jnp.float32)

    def body(b, carry):
        rows = radius_ref[b]
        for i in range(near):
            spline = cubic(jnp.abs(rows[i : i + 1, :] - knot))
            s_hi, s_lo = split2(spline)
            radial = dot(coeffs, jnp.concatenate([s_hi, s_lo, s_hi], axis=0))
            h = harm_ref[b, i]
            g_ref[b * near + i] = radial * h.astype(jnp.float32)
            hpad_ref[b * near + i, 0:comps, :] = h
        return carry

    lax.fori_loop(0, batches, body, 0)


def density_kernel(
    start_ref, offset_ref, size_ref, basis_ref, blocks_ref, part_ref, hpad_ref, atom_ref,
    dens_ref, terms_ref, w_ref,
):
    batches, near_blocks, points, width = basis_ref.shape
    owners = blocks_ref.shape[0]
    near = part_ref.shape[1]
    w_ref[...] = jnp.zeros(w_ref.shape, w_ref.dtype)
    lane = lax.broadcasted_iota(jnp.int32, (1, points), 1)
    ones = jnp.ones((8, 3 * width), jnp.bfloat16)
    zero = jnp.zeros((width, width), jnp.bfloat16)

    def body(b, carry):
        first = start_ref[0] + offset_ref[0, b]
        spot = [lax.rem(first + j, owners) for j in range(near_blocks)]
        phi = [basis_ref[b, j] for j in range(near_blocks)]

        def block(j, q):
            k = q - j + 1
            return blocks_ref[spot[j], k] if 0 <= k < 4 else zero

        total = jnp.zeros((points, width), jnp.float32)
        for q0, js in ((0, (0, 1, 2)), (2, (0, 1, 2, 3))):
            left = jnp.concatenate([phi[j] for j in js], axis=1)
            right = jnp.concatenate(
                [jnp.concatenate([block(j, q0), block(j, q0 + 1)], axis=1) for j in js], axis=0
            )
            mixed = dot(left, right)
            total = total + mixed[:, :width] * phi[q0].astype(jnp.float32)
            total = total + mixed[:, width:] * phi[q0 + 1].astype(jnp.float32)
        summed = dot(ones, jnp.concatenate(split3(total), axis=1), NT)[0:1]
        alive = lane < size_ref[0, b]
        row = jnp.where(alive, summed, 0.0)
        dens_ref[pl.ds(b, 1), :] = row
        w_ref[b, 0:near, :] = part_ref[b] * row
        return carry

    lax.fori_loop(0, batches, body, 0)
    weights = w_ref[...].reshape(LANES, points)
    columns = jnp.concatenate(split2(weights), axis=0)
    slot = lax.broadcasted_iota(jnp.int32, (1, 2 * LANES), 1) % LANES
    terms = jnp.zeros((ROWS, 2 * LANES), jnp.float32)
    for b in range(batches):
        rows = hpad_ref[b * near : (b + 1) * near].reshape(near * ROWS, points)
        cross = dot(rows, columns, NT)
        for i in range(near):
            terms = terms + jnp.where(
                slot == b * SLOT + i, cross[i * ROWS : (i + 1) * ROWS], 0.0
            )
    result = terms[:, :LANES] + terms[:, LANES:]
    row_id = lax.broadcasted_iota(jnp.int32, (ROWS, LANES), 0)
    comps = ROWS - 7
    terms_ref[...] = jnp.where(row_id == comps, atom_ref[...].astype(jnp.float32), result)


def scatter_kernel(comps, atoms, *refs):
    outs = refs[-5:]
    pieces = refs[:-5]
    row_id = lax.broadcasted_iota(jnp.int32, (3 * atoms, LANES), 0)
    total = jnp.zeros((3 * ROWS, 3 * atoms), jnp.float32)
    for m in range(0, len(pieces), 2):
        left, right = [], []
        for piece in pieces[m : m + 2]:
            values = piece[...]
            chosen = values[comps : comps + 1, :].astype(jnp.int32)
            right.append((row_id == chosen).astype(jnp.float32).astype(jnp.bfloat16))
            left.append(jnp.concatenate(split3(values), axis=0))
        total = total + dot(jnp.concatenate(left, axis=1), jnp.concatenate(right, axis=1), NT)
    sums = total[:ROWS] + total[ROWS : 2 * ROWS] + total[2 * ROWS :]
    own, ahead1, back1, ahead2, back2 = outs
    own[...] = sums
    ahead1[...] = sums[:, atoms:]
    back1[...] = sums[:, : 2 * atoms]
    ahead2[...] = sums[:, 2 * atoms :]
    back2[...] = sums[:, :atoms]


def potential_kernel(
    comps, atoms, size_ref, own_ref, a1_ref, b1_ref, a2_ref, b2_ref, atom_ref, g_ref,
    mom_ref, pot_ref,
):
    batches, points = pot_ref.shape
    near = g_ref.shape[0] // batches
    own = own_ref[...]
    before = a2_ref[...] + a1_ref[:, :atoms] + own[:, :atoms]
    here = a1_ref[:, atoms:] + own[:, atoms : 2 * atoms] + b1_ref[:, :atoms]
    after = own[:, 2 * atoms :] + b1_ref[:, atoms:] + b2_ref[...]
    mom_ref[...] = here[:comps]
    moments = jnp.concatenate([before, here, after], axis=1)
    row_id = lax.broadcasted_iota(jnp.int32, (3 * atoms, LANES), 0)
    pick = (row_id == atom_ref[...]).astype(jnp.float32).astype(jnp.bfloat16)
    got = dot(jnp.concatenate(split3(moments), axis=0), pick)
    chosen = got[:ROWS] + got[ROWS : 2 * ROWS] + got[2 * ROWS :]
    chosen = chosen[:comps]
    lane = lax.broadcasted_iota(jnp.int32, (1, points), 1)
    for b in range(batches):
        total = jnp.zeros((comps, points), jnp.float32)
        for i in range(near):
            column = chosen[:, b * SLOT + i : b * SLOT + i + 1]
            total = total + column * g_ref[b * near + i]
        row = jnp.sum(total, axis=0, keepdims=True)
        pot_ref[b : b + 1, :] = jnp.where(lane < size_ref[0, b], row, 0.0)


def shifted(value, axis, step):
    count = lax.axis_size(axis)
    return lax.ppermute(value, axis, [(i, (i + step) % count) for i in range(count)])


def per_device(
    basis_values,
    density_rows,
    block_mask,
    window_start,
    batch_offsets,
    batch_sizes,
    atom_near,
    harmonics,
    partition,
    radius,
    radial_table,
):
    dev_count = lax.axis_size("dev")
    blocks_dev = density_rows.shape[0]
    block_count = blocks_dev * dev_count
    batches, near, comps, points = harmonics.shape
    atoms = 16 * dev_count

    first_block = window_start[0]
    peer_index = jnp.arange(dev_count, dtype=jnp.int32)
    ahead_count = (peer_index - first_block) % dev_count
    wanted = (first_block + ahead_count) % block_count // dev_count
    requested = lax.all_to_all(wanted[:, None], "dev", split_axis=0, concat_axis=0, tiled=True)[:, 0]
    masked = density_rows * block_mask.astype(jnp.bfloat16)[:, :, None, None]
    served = jnp.take(masked, requested, axis=0, mode="clip")
    replies = lax.all_to_all(served, "dev", split_axis=0, concat_axis=0, tiled=True)

    f32, bf16 = jnp.float32, jnp.bfloat16
    g, hpad = pl.pallas_call(
        pre_kernel,
        out_shape=(
            jax.ShapeDtypeStruct((batches * near, comps, points), f32),
            jax.ShapeDtypeStruct((batches * near, ROWS, points), bf16),
        ),
        in_specs=[VMEM] * 3,
        out_specs=(VMEM, VMEM),
        compiler_params=PARAMS,
        cost_estimate=pl.CostEstimate(flops=400_000_000, bytes_accessed=6_000_000, transcendentals=0),
        name="pre",
    )(harmonics, radius, radial_table)

    atom_rows = jnp.pad(atom_near, ((0, LANES // SLOT - batches), (0, SLOT - near)), constant_values=-1)
    atom_rows = atom_rows.reshape(1, LANES)

    density, terms = pl.pallas_call(
        density_kernel,
        out_shape=(
            jax.ShapeDtypeStruct((batches, points), f32),
            jax.ShapeDtypeStruct((ROWS, LANES), f32),
        ),
        in_specs=[SMEM] * 3 + [VMEM] * 5,
        out_specs=(VMEM, VMEM),
        scratch_shapes=[pltpu.VMEM((LANES // SLOT, SLOT, points), f32)],
        compiler_params=PARAMS,
        cost_estimate=pl.CostEstimate(flops=2_000_000_000, bytes_accessed=6_000_000, transcendentals=0),
        name="density",
    )(window_start, batch_offsets, batch_sizes, basis_values, replies, partition, hpad, atom_rows)

    pieces = [terms] + [
        lax.ppermute(terms, "dev", [(i, i ^ m) for i in range(dev_count)]) for m in range(1, dev_count)
    ]
    own, ahead1, back1, ahead2, back2 = pl.pallas_call(
        functools.partial(scatter_kernel, comps, atoms),
        out_shape=tuple(
            jax.ShapeDtypeStruct((ROWS, n * atoms), f32) for n in (3, 2, 2, 1, 1)
        ),
        in_specs=[VMEM] * len(pieces),
        out_specs=(VMEM,) * 5,
        compiler_params=PARAMS,
        name="scatter",
    )(*pieces)
    ahead2 = shifted(ahead2, "region", 2)
    back2 = shifted(back2, "region", -2)
    ahead1 = shifted(ahead1, "region", 1)
    back1 = shifted(back1, "region", -1)

    region_moments, potential = pl.pallas_call(
        functools.partial(potential_kernel, comps, atoms),
        out_shape=(
            jax.ShapeDtypeStruct((comps, atoms), f32),
            jax.ShapeDtypeStruct((batches, points), f32),
        ),
        in_specs=[SMEM] + [VMEM] * 7,
        out_specs=(VMEM, VMEM),
        compiler_params=PARAMS,
        name="potential",
    )(batch_sizes, own, ahead1, back1, ahead2, back2, atom_rows, g)
    moments = lax.dynamic_slice_in_dim(region_moments, lax.axis_index("dev") * 16, 16, 1)
    return (density, moments, potential)


def solution(mesh):
    both = ("region", "dev")
    placed = (
        P(both, None, None, None),
        P(both, None, None, None),
        P(both, None),
        P(both),
        P(both, None),
        P(both, None),
        P(both, None),
        P(both, None, None, None),
        P(both, None, None),
        P(both, None, None),
        P(),
    )
    return jax.shard_map(
        per_device,
        mesh=mesh,
        in_specs=placed,
        out_specs=(P(both, None), P(None, both), P(both, None)),
        check_vma=False,
    )
```

```python
import functools
import jax
import jax.numpy as jnp
from jax import lax
from jax.experimental import pallas as pl
from jax.experimental.pallas import tpu as pltpu
from jax.sharding import PartitionSpec as P

LANES = 128
ROWS = 32
SLOT = 8
NT = (((1,), (1,)), ((), ()))
NN = (((1,), (0,)), ((), ()))
VMEM = pl.BlockSpec(memory_space=pltpu.VMEM)
SMEM = pl.BlockSpec(memory_space=pltpu.SMEM)
PARAMS = pltpu.CompilerParams(vmem_limit_bytes=16 * 1024 * 1024)


def dot(a, b, dims=NN):
    return lax.dot_general(a, b, dims, preferred_element_type=jnp.float32)


def split2(x):
    hi = x.astype(jnp.bfloat16)
    lo = (x - hi.astype(jnp.float32)).astype(jnp.bfloat16)
    return hi, lo


def split3(x):
    hi, mid = split2(x)
    rest = x - hi.astype(jnp.float32) - mid.astype(jnp.float32)
    return hi, mid, rest.astype(jnp.bfloat16)


def cubic(distance):
    inner = 2.0 / 3.0 - distance * distance + 0.5 * distance * distance * distance
    remote = 2.0 - distance
    outer = remote * remote * remote * (1.0 / 6.0)
    return jnp.where(distance < 1.0, inner, jnp.where(distance < 2.0, outer, 0.0))


def pre_kernel(harm_ref, radius_ref, table_ref, g_ref, hpad_ref):
    batches, near, comps, points = harm_ref.shape
    knots = table_ref.shape[1]
    hpad_ref[...] = jnp.zeros(hpad_ref.shape, hpad_ref.dtype)
    r_hi, r_lo = split2(table_ref[...])
    coeffs = jnp.concatenate([r_hi, r_hi, r_lo], axis=1)
    knot = lax.broadcasted_iota(jnp.int32, (knots, points), 0).astype(jnp.float32)

    def body(b, carry):
        rows = radius_ref[b]
        for i in range(near):
            spline = cubic(jnp.abs(rows[i : i + 1, :] - knot))
            s_hi, s_lo = split2(spline)
            radial = dot(coeffs, jnp.concatenate([s_hi, s_lo, s_hi], axis=0))
            h = harm_ref[b, i]
            g_ref[b * near + i] = radial * h.astype(jnp.float32)
            hpad_ref[b * near + i, 0:comps, :] = h
        return carry

    lax.fori_loop(0, batches, body, 0)


def density_kernel(
    rows_dev, start_ref, offset_ref, size_ref, basis_ref, blocks_ref, part_ref, hpad_ref, atom_ref,
    dens_ref, terms_ref, w_ref,
):
    batches, near_blocks, points, width = basis_ref.shape
    stored = blocks_ref.shape[0]
    owners = stored // rows_dev
    near = part_ref.shape[1]
    w_ref[...] = jnp.zeros(w_ref.shape, w_ref.dtype)
    lane = lax.broadcasted_iota(jnp.int32, (1, points), 1)
    ones = jnp.ones((8, 3 * width), jnp.bfloat16)
    zero = jnp.zeros((width, width), jnp.bfloat16)

    def body(b, carry):
        first = start_ref[0] + offset_ref[0, b]
        spot = []
        for j in range(near_blocks):
            index = lax.rem(first + j, stored)
            spot.append(lax.rem(index, owners) * rows_dev + index // owners)
        phi = [basis_ref[b, j] for j in range(near_blocks)]

        def block(j, q):
            k = q - j + 1
            return blocks_ref[spot[j], k] if 0 <= k < 4 else zero

        total = jnp.zeros((points, width), jnp.float32)
        for q0, js in ((0, (0, 1, 2)), (2, (0, 1, 2, 3))):
            left = jnp.concatenate([phi[j] for j in js], axis=1)
            right = jnp.concatenate(
                [jnp.concatenate([block(j, q0), block(j, q0 + 1)], axis=1) for j in js], axis=0
            )
            mixed = dot(left, right)
            total = total + mixed[:, :width] * phi[q0].astype(jnp.float32)
            total = total + mixed[:, width:] * phi[q0 + 1].astype(jnp.float32)
        summed = dot(ones, jnp.concatenate(split3(total), axis=1), NT)[0:1]
        alive = lane < size_ref[0, b]
        row = jnp.where(alive, summed, 0.0)
        dens_ref[pl.ds(b, 1), :] = row
        w_ref[b, 0:near, :] = part_ref[b] * row
        return carry

    lax.fori_loop(0, batches, body, 0)
    weights = w_ref[...].reshape(LANES, points)
    columns = jnp.concatenate(split2(weights), axis=0)
    slot = lax.broadcasted_iota(jnp.int32, (1, 2 * LANES), 1) % LANES
    terms = jnp.zeros((ROWS, 2 * LANES), jnp.float32)
    for b in range(batches):
        rows = hpad_ref[b * near : (b + 1) * near].reshape(near * ROWS, points)
        cross = dot(rows, columns, NT)
        for i in range(near):
            terms = terms + jnp.where(
                slot == b * SLOT + i, cross[i * ROWS : (i + 1) * ROWS], 0.0
            )
    result = terms[:, :LANES] + terms[:, LANES:]
    row_id = lax.broadcasted_iota(jnp.int32, (ROWS, LANES), 0)
    comps = ROWS - 7
    terms_ref[...] = jnp.where(row_id == comps, atom_ref[...].astype(jnp.float32), result)


def scatter_kernel(comps, atoms, *refs):
    outs = refs[-5:]
    pieces = refs[:-5]
    row_id = lax.broadcasted_iota(jnp.int32, (3 * atoms, LANES), 0)
    total = jnp.zeros((3 * ROWS, 3 * atoms), jnp.float32)
    for m in range(0, len(pieces), 2):
        left, right = [], []
        for piece in pieces[m : m + 2]:
            values = piece[...]
            chosen = values[comps : comps + 1, :].astype(jnp.int32)
            right.append((row_id == chosen).astype(jnp.float32).astype(jnp.bfloat16))
            left.append(jnp.concatenate(split3(values), axis=0))
        total = total + dot(jnp.concatenate(left, axis=1), jnp.concatenate(right, axis=1), NT)
    sums = total[:ROWS] + total[ROWS : 2 * ROWS] + total[2 * ROWS :]
    own, ahead1, back1, ahead2, back2 = outs
    own[...] = sums
    ahead1[...] = sums[:, atoms:]
    back1[...] = sums[:, : 2 * atoms]
    ahead2[...] = sums[:, 2 * atoms :]
    back2[...] = sums[:, :atoms]


def potential_kernel(
    comps, atoms, size_ref, own_ref, a1_ref, b1_ref, a2_ref, b2_ref, atom_ref, g_ref,
    mom_ref, pot_ref,
):
    batches, points = pot_ref.shape
    near = g_ref.shape[0] // batches
    own = own_ref[...]
    before = a2_ref[...] + a1_ref[:, :atoms] + own[:, :atoms]
    here = a1_ref[:, atoms:] + own[:, atoms : 2 * atoms] + b1_ref[:, :atoms]
    after = own[:, 2 * atoms :] + b1_ref[:, atoms:] + b2_ref[...]
    mom_ref[...] = here[:comps]
    moments = jnp.concatenate([before, here, after], axis=1)
    row_id = lax.broadcasted_iota(jnp.int32, (3 * atoms, LANES), 0)
    pick = (row_id == atom_ref[...]).astype(jnp.float32).astype(jnp.bfloat16)
    got = dot(jnp.concatenate(split3(moments), axis=0), pick)
    chosen = got[:ROWS] + got[ROWS : 2 * ROWS] + got[2 * ROWS :]
    chosen = chosen[:comps]
    lane = lax.broadcasted_iota(jnp.int32, (1, points), 1)
    for b in range(batches):
        total = jnp.zeros((comps, points), jnp.float32)
        for i in range(near):
            column = chosen[:, b * SLOT + i : b * SLOT + i + 1]
            total = total + column * g_ref[b * near + i]
        row = jnp.sum(total, axis=0, keepdims=True)
        pot_ref[b : b + 1, :] = jnp.where(lane < size_ref[0, b], row, 0.0)


def shifted(value, axis, step):
    count = lax.axis_size(axis)
    return lax.ppermute(value, axis, [(i, (i + step) % count) for i in range(count)])


def per_device(
    basis_values,
    density_rows,
    block_mask,
    window_start,
    batch_offsets,
    batch_sizes,
    atom_near,
    harmonics,
    partition,
    radius,
    radial_table,
):
    dev_count = lax.axis_size("dev")
    blocks_dev = density_rows.shape[0]
    batches, near, comps, points = harmonics.shape
    atoms = 16 * dev_count

    masked = density_rows * block_mask.astype(jnp.bfloat16)[:, :, None, None]
    gathered = lax.all_gather(masked, "dev", axis=0, tiled=True)

    f32, bf16 = jnp.float32, jnp.bfloat16
    g, hpad = pl.pallas_call(
        pre_kernel,
        out_shape=(
            jax.ShapeDtypeStruct((batches * near, comps, points), f32),
            jax.ShapeDtypeStruct((batches * near, ROWS, points), bf16),
        ),
        in_specs=[VMEM] * 3,
        out_specs=(VMEM, VMEM),
        compiler_params=PARAMS,
        cost_estimate=pl.CostEstimate(flops=400_000_000, bytes_accessed=6_000_000, transcendentals=0),
        name="pre",
    )(harmonics, radius, radial_table)

    atom_rows = jnp.pad(atom_near, ((0, LANES // SLOT - batches), (0, SLOT - near)), constant_values=-1)
    atom_rows = atom_rows.reshape(1, LANES)

    density, terms = pl.pallas_call(
        functools.partial(density_kernel, blocks_dev),
        out_shape=(
            jax.ShapeDtypeStruct((batches, points), f32),
            jax.ShapeDtypeStruct((ROWS, LANES), f32),
        ),
        in_specs=[SMEM] * 3 + [VMEM] * 5,
        out_specs=(VMEM, VMEM),
        scratch_shapes=[pltpu.VMEM((LANES // SLOT, SLOT, points), f32)],
        compiler_params=PARAMS,
        cost_estimate=pl.CostEstimate(flops=2_000_000_000, bytes_accessed=6_000_000, transcendentals=0),
        name="density",
    )(window_start, batch_offsets, batch_sizes, basis_values, gathered, partition, hpad, atom_rows)

    pieces = [terms] + [
        lax.ppermute(terms, "dev", [(i, i ^ m) for i in range(dev_count)]) for m in range(1, dev_count)
    ]
    own, ahead1, back1, ahead2, back2 = pl.pallas_call(
        functools.partial(scatter_kernel, comps, atoms),
        out_shape=tuple(
            jax.ShapeDtypeStruct((ROWS, n * atoms), f32) for n in (3, 2, 2, 1, 1)
        ),
        in_specs=[VMEM] * len(pieces),
        out_specs=(VMEM,) * 5,
        compiler_params=PARAMS,
        name="scatter",
    )(*pieces)
    ahead2 = shifted(ahead2, "region", 2)
    back2 = shifted(back2, "region", -2)
    ahead1 = shifted(ahead1, "region", 1)
    back1 = shifted(back1, "region", -1)

    region_moments, potential = pl.pallas_call(
        functools.partial(potential_kernel, comps, atoms),
        out_shape=(
            jax.ShapeDtypeStruct((comps, atoms), f32),
            jax.ShapeDtypeStruct((batches, points), f32),
        ),
        in_specs=[SMEM] + [VMEM] * 7,
        out_specs=(VMEM, VMEM),
        compiler_params=PARAMS,
        name="potential",
    )(batch_sizes, own, ahead1, back1, ahead2, back2, atom_rows, g)
    moments = lax.dynamic_slice_in_dim(region_moments, lax.axis_index("dev") * 16, 16, 1)
    return (density, moments, potential)


def solution(mesh):
    both = ("region", "dev")
    placed = (
        P(both, None, None, None),
        P(both, None, None, None),
        P(both, None),
        P(both),
        P(both, None),
        P(both, None),
        P(both, None),
        P(both, None, None, None),
        P(both, None, None),
        P(both, None, None),
        P(),
    )
    return jax.shard_map(
        per_device,
        mesh=mesh,
        in_specs=placed,
        out_specs=(P(both, None), P(None, both), P(both, None)),
        check_vma=False,
    )
```

```python
import functools
import jax
import jax.numpy as jnp
from jax import lax
from jax.experimental import pallas as pl
from jax.experimental.pallas import tpu as pltpu
from jax.sharding import PartitionSpec as P

LANES = 128
ROWS = 32
SLOT = 8
NT = (((1,), (1,)), ((), ()))
NN = (((1,), (0,)), ((), ()))
VMEM = pl.BlockSpec(memory_space=pltpu.VMEM)
SMEM = pl.BlockSpec(memory_space=pltpu.SMEM)
ANY = pl.BlockSpec(memory_space=pl.ANY)
PARAMS = pltpu.CompilerParams(vmem_limit_bytes=16 * 1024 * 1024)


def dot(a, b, dims=NN):
    return lax.dot_general(a, b, dims, preferred_element_type=jnp.float32)


def split2(x):
    hi = x.astype(jnp.bfloat16)
    lo = (x - hi.astype(jnp.float32)).astype(jnp.bfloat16)
    return hi, lo


def split3(x):
    hi, mid = split2(x)
    rest = x - hi.astype(jnp.float32) - mid.astype(jnp.float32)
    return hi, mid, rest.astype(jnp.bfloat16)


def cubic(distance):
    inner = 2.0 / 3.0 - distance * distance + 0.5 * distance * distance * distance
    remote = 2.0 - distance
    outer = remote * remote * remote * (1.0 / 6.0)
    return jnp.where(distance < 1.0, inner, jnp.where(distance < 2.0, outer, 0.0))


def select_kernel(dev_count, starts_ref, mask_ref, rows_ref, *outs):
    me = lax.axis_index("dev")
    stored, band = rows_ref.shape[0], rows_ref.shape[1]
    for m, out in enumerate(outs):
        start = starts_ref[m]
        ahead = lax.rem(me - start + stored * dev_count, dev_count)
        held = lax.rem(start + ahead, stored * dev_count) // dev_count
        for k in range(band):
            factor = mask_ref[held, k].astype(jnp.float32)
            out[k] = (rows_ref[held, k].astype(jnp.float32) * factor).astype(jnp.bfloat16)


def pre_kernel(basis_ref, harm_ref, radius_ref, table_ref, g_ref, hpad_ref, phit_ref, basis, sem):
    batches, near, comps, points = harm_ref.shape
    near_blocks = basis.shape[1]
    knots = table_ref.shape[1]
    copy = pltpu.make_async_copy(basis_ref, basis, sem)
    copy.start()
    hpad_ref[...] = jnp.zeros(hpad_ref.shape, hpad_ref.dtype)
    r_hi, r_lo = split2(table_ref[...])
    coeffs = jnp.concatenate([r_hi, r_hi, r_lo], axis=1)
    knot = lax.broadcasted_iota(jnp.int32, (knots, points), 0).astype(jnp.float32)

    def body(b, carry):
        rows = radius_ref[b]
        for i in range(near):
            spline = cubic(jnp.abs(rows[i : i + 1, :] - knot))
            s_hi, s_lo = split2(spline)
            radial = dot(coeffs, jnp.concatenate([s_hi, s_lo, s_hi], axis=0))
            h = harm_ref[b, i]
            g_ref[b * near + i] = radial * h.astype(jnp.float32)
            hpad_ref[b * near + i, 0:comps, :] = h
        return carry

    lax.fori_loop(0, batches, body, 0)
    copy.wait()

    def turn(b, carry):
        for j in range(near_blocks):
            phit_ref[b, j] = basis[b, j].T
        return carry

    lax.fori_loop(0, batches, turn, 0)


def density_kernel(start_ref, offset_ref, size_ref, atom_ref, phit_ref, part_ref, hpad_ref, *refs):
    dens_ref, terms_ref, window_ref, w_ref = refs[-4:]
    pieces = refs[:-4]
    owners = len(pieces)
    batches, near_blocks, width, points = phit_ref.shape
    near = part_ref.shape[1]
    me = lax.axis_index("dev")
    for m, piece in enumerate(pieces):
        spot = lax.rem(lax.bitwise_xor(me, m) - start_ref[0] + 3 * owners, owners)
        window_ref[spot] = piece[...]
    w_ref[...] = jnp.zeros(w_ref.shape, w_ref.dtype)
    lane = lax.broadcasted_iota(jnp.int32, (1, points), 1)
    zero = jnp.zeros((width, width), jnp.bfloat16)

    def body(b, carry):
        first = offset_ref[0, b]
        total = jnp.zeros((width, points), jnp.float32)
        for q, js in ((0, (0, 1, 2)), (2, (0, 1, 2, 3))):
            left = []
            for j in js:
                pair = [
                    window_ref[first + j, f - j + 1] if 0 <= f - j + 1 < 4 else zero
                    for f in (q, q + 1)
                ]
                left.append(jnp.concatenate(pair, axis=1))
            right = jnp.concatenate([phit_ref[b, q], phit_ref[b, q + 1]], axis=0)
            mixed = dot(jnp.concatenate(left, axis=0), right)
            for at, j in enumerate(js):
                part = mixed[at * width : (at + 1) * width]
                total = total + part * phit_ref[b, j].astype(jnp.float32)
        summed = jnp.sum(total, axis=0, keepdims=True)
        alive = lane < size_ref[0, b]
        row = jnp.where(alive, summed, 0.0)
        dens_ref[pl.ds(b, 1), :] = row
        w_ref[b, 0:near, :] = part_ref[b] * row
        return carry

    lax.fori_loop(0, batches, body, 0, unroll=2)
    weights = w_ref[...].reshape(LANES, points)
    columns = jnp.concatenate(split2(weights), axis=0)
    slot = lax.broadcasted_iota(jnp.int32, (1, 2 * LANES), 1) % LANES
    cross = dot(hpad_ref[...].reshape(batches * near * ROWS, points), columns, NT)
    terms = jnp.zeros((ROWS, 2 * LANES), jnp.float32)
    for b in range(batches):
        for i in range(near):
            at = (b * near + i) * ROWS
            terms = terms + jnp.where(slot == b * SLOT + i, cross[at : at + ROWS], 0.0)
    result = terms[:, :LANES] + terms[:, LANES:]
    row_id = lax.broadcasted_iota(jnp.int32, (ROWS, LANES), 0)
    comps = ROWS - 7
    terms_ref[...] = jnp.where(row_id == comps, atom_ref[...].astype(jnp.float32), result)


def scatter_kernel(comps, atoms, flip, *refs):
    outs = refs[-4:]
    pieces = refs[:-4]
    row_id = lax.broadcasted_iota(jnp.int32, (3 * atoms, LANES), 0)
    total = jnp.zeros((3 * ROWS, 3 * atoms), jnp.float32)
    for piece in pieces:
        left, right = [], []
        for part in range(piece.shape[0]):
            values = piece[part]
            chosen = values[comps : comps + 1, :].astype(jnp.int32)
            right.append((row_id == chosen).astype(jnp.float32).astype(jnp.bfloat16))
            left.append(jnp.concatenate(split3(values), axis=0))
        total = total + dot(jnp.concatenate(left, axis=1), jnp.concatenate(right, axis=1), NT)
    sums = total[:ROWS] + total[ROWS : 2 * ROWS] + total[2 * ROWS :]
    own, near_a, near_b, far = outs
    own[...] = sums
    ahead, back = sums[:, atoms:], sums[:, : 2 * atoms]
    if flip:
        odd = lax.rem(lax.axis_index("region"), 2) == 1
        near_a[...] = jnp.where(odd, back, ahead)
        near_b[...] = jnp.where(odd, ahead, back)
    else:
        near_a[...] = ahead
        near_b[...] = back
    far[:, :atoms] = sums[:, :atoms]
    far[:, atoms:] = sums[:, 2 * atoms :]


def potential_kernel(
    comps, atoms, flip, size_ref, own_ref, near_a_ref, near_b_ref, fa_ref, fb_ref, atom_ref, g_ref,
    mom_ref, pot_ref,
):
    batches, points = pot_ref.shape
    near = g_ref.shape[0] // batches
    own = own_ref[...]
    near_a, near_b = near_a_ref[...], near_b_ref[...]
    if flip:
        odd = lax.rem(lax.axis_index("region"), 2) == 1
        low = jnp.where(odd, near_a, near_b)
        high = jnp.where(odd, near_b, near_a)
    else:
        low, high = near_a, near_b
    before = fa_ref[:, atoms:] + low[:, :atoms] + own[:, :atoms]
    here = low[:, atoms:] + own[:, atoms : 2 * atoms] + high[:, :atoms]
    after = own[:, 2 * atoms :] + high[:, atoms:] + fb_ref[:, :atoms]

    mine = mom_ref.shape[0]
    want = lax.broadcasted_iota(jnp.int32, (mine, atoms), 0) + lax.axis_index("dev") * mine
    keep = want == lax.broadcasted_iota(jnp.int32, (mine, atoms), 1)
    keep = keep.astype(jnp.float32).astype(jnp.bfloat16)
    taken = dot(keep, jnp.concatenate(split3(here), axis=0), NT)
    taken = taken[:, :ROWS] + taken[:, ROWS : 2 * ROWS] + taken[:, 2 * ROWS :]
    mom_ref[...] = taken[:, :comps]

    moments = jnp.concatenate([before, here, after], axis=1)
    row_id = lax.broadcasted_iota(jnp.int32, (3 * atoms, LANES), 0)
    pick = (row_id == atom_ref[...]).astype(jnp.float32).astype(jnp.bfloat16)
    got = dot(jnp.concatenate(split3(moments), axis=0), pick)
    chosen = got[:ROWS] + got[ROWS : 2 * ROWS] + got[2 * ROWS :]
    chosen = chosen[:comps]
    lane = lax.broadcasted_iota(jnp.int32, (1, points), 1)
    for b in range(batches):
        total = jnp.zeros((comps, points), jnp.float32)
        for i in range(near):
            column = chosen[:, b * SLOT + i : b * SLOT + i + 1]
            total = total + column * g_ref[b * near + i]
        row = jnp.sum(total, axis=0, keepdims=True)
        pot_ref[b : b + 1, :] = jnp.where(lane < size_ref[0, b], row, 0.0)


def crossed(value, axis, m):
    return lax.ppermute(value, axis, [(i, i ^ m) for i in range(lax.axis_size(axis))])


def shifted(value, axis, step):
    count = lax.axis_size(axis)
    return lax.ppermute(value, axis, [(i, (i + step) % count) for i in range(count)])


def per_device(
    basis_values,
    density_rows,
    block_mask,
    window_start,
    batch_offsets,
    batch_sizes,
    atom_near,
    harmonics,
    partition,
    radius,
    radial_table,
):
    dev_count = lax.axis_size("dev")
    region_count = lax.axis_size("region")
    blocks_dev, band, width = density_rows.shape[:3]
    batches, near, comps, points = harmonics.shape
    near_blocks = basis_values.shape[1]
    mine = 16
    atoms = mine * dev_count
    f32, bf16 = jnp.float32, jnp.bfloat16

    pair = jnp.concatenate([window_start, crossed(window_start, "dev", 1)])
    starts = jnp.concatenate([pair] + [crossed(pair, "dev", m) for m in range(2, dev_count, 2)])
    served = pl.pallas_call(
        functools.partial(select_kernel, dev_count),
        out_shape=tuple(
            jax.ShapeDtypeStruct((band, width, width), bf16) for _ in range(dev_count)
        ),
        in_specs=[SMEM, SMEM, VMEM],
        out_specs=(VMEM,) * dev_count,
        compiler_params=PARAMS,
        name="select",
    )(starts, block_mask, density_rows)
    order = sorted(range(1, dev_count), key=lambda m: -bin(m).count("1"))
    pieces = {m: crossed(served[m], "dev", m) for m in order}
    pieces[0] = served[0]

    g, hpad, phit = pl.pallas_call(
        pre_kernel,
        out_shape=(
            jax.ShapeDtypeStruct((batches * near, comps, points), f32),
            jax.ShapeDtypeStruct((batches * near, ROWS, points), bf16),
            jax.ShapeDtypeStruct((batches, near_blocks, width, points), bf16),
        ),
        in_specs=[ANY] + [VMEM] * 3,
        out_specs=(VMEM,) * 3,
        scratch_shapes=[pltpu.VMEM(basis_values.shape, bf16), pltpu.SemaphoreType.DMA],
        compiler_params=PARAMS,
        cost_estimate=pl.CostEstimate(flops=2_000_000_000, bytes_accessed=8_000_000, transcendentals=0),
        name="pre",
    )(basis_values, harmonics, radius, radial_table)

    atom_rows = jnp.pad(atom_near, ((0, LANES // SLOT - batches), (0, SLOT - near)), constant_values=-1)
    atom_rows = atom_rows.reshape(1, LANES)

    density, terms = pl.pallas_call(
        density_kernel,
        out_shape=(
            jax.ShapeDtypeStruct((batches, points), f32),
            jax.ShapeDtypeStruct((ROWS, LANES), f32),
        ),
        in_specs=[SMEM] * 3 + [VMEM] * (4 + dev_count),
        out_specs=(VMEM, VMEM),
        scratch_shapes=[
            pltpu.VMEM((dev_count, band, width, width), bf16),
            pltpu.VMEM((LANES // SLOT, SLOT, points), f32),
        ],
        compiler_params=PARAMS,
        cost_estimate=pl.CostEstimate(flops=2_000_000_000, bytes_accessed=6_000_000, transcendentals=0),
        name="density",
    )(
        window_start, batch_offsets, batch_sizes, atom_rows, phit, partition, hpad,
        *[pieces[m] for m in range(dev_count)],
    )

    both = jnp.stack([terms, crossed(terms, "dev", 1)])
    groups = [both] + [crossed(both, "dev", m) for m in range(2, dev_count, 2)]
    flip = region_count == 4
    own, near_a, near_b, far = pl.pallas_call(
        functools.partial(scatter_kernel, comps, atoms, flip),
        out_shape=tuple(jax.ShapeDtypeStruct((ROWS, n * atoms), f32) for n in (3, 2, 2, 2)),
        in_specs=[VMEM] * len(groups),
        out_specs=(VMEM,) * 4,
        compiler_params=PARAMS,
        name="scatter",
    )(*groups)
    if flip:
        far_a = far_b = crossed(far, "region", 2)
        near_a = crossed(near_a, "region", 1)
        near_b = crossed(near_b, "region", 3)
    else:
        far_a = shifted(far, "region", 2)
        far_b = shifted(far, "region", -2)
        near_a = shifted(near_a, "region", 1)
        near_b = shifted(near_b, "region", -1)

    moments, potential = pl.pallas_call(
        functools.partial(potential_kernel, comps, atoms, flip),
        out_shape=(
            jax.ShapeDtypeStruct((mine, comps), f32),
            jax.ShapeDtypeStruct((batches, points), f32),
        ),
        in_specs=[SMEM] + [VMEM] * 7,
        out_specs=(VMEM, VMEM),
        compiler_params=PARAMS,
        name="potential",
    )(batch_sizes, own, near_a, near_b, far_a, far_b, atom_rows, g)
    return (density, moments.T, potential)


def solution(mesh):
    both = ("region", "dev")
    placed = (
        P(both, None, None, None),
        P(both, None, None, None),
        P(both, None),
        P(both),
        P(both, None),
        P(both, None),
        P(both, None),
        P(both, None, None, None),
        P(both, None, None),
        P(both, None, None),
        P(),
    )
    return jax.shard_map(
        per_device,
        mesh=mesh,
        in_specs=placed,
        out_specs=(P(both, None), P(None, both), P(both, None)),
        check_vma=False,
    )
```

```python
import functools
import jax
import jax.numpy as jnp
from jax import lax
from jax.experimental import pallas as pl
from jax.experimental.pallas import tpu as pltpu
from jax.sharding import PartitionSpec as P

EVEN_OWNERS = (0, 1, 4, 3, 2, 5, 6, 7)
ODD_OWNERS = (0, 1, 2, 5, 4, 3, 6, 7)
LANES = 128
ROWS = 32
SLOT = 8
NT = (((1,), (1,)), ((), ()))
NN = (((1,), (0,)), ((), ()))
VMEM = pl.BlockSpec(memory_space=pltpu.VMEM)
SMEM = pl.BlockSpec(memory_space=pltpu.SMEM)
HBM = pl.BlockSpec(memory_space=pltpu.HBM)
WIDE = pltpu.CompilerParams(vmem_limit_bytes=50 * 1024 * 1024)
PARAMS = pltpu.CompilerParams(vmem_limit_bytes=16 * 1024 * 1024)


def dot(a, b, dims=NN):
    return lax.dot_general(a, b, dims, preferred_element_type=jnp.float32)


def split2(x):
    hi = x.astype(jnp.bfloat16)
    lo = (x - hi.astype(jnp.float32)).astype(jnp.bfloat16)
    return hi, lo


def split3(x):
    hi, mid = split2(x)
    rest = x - hi.astype(jnp.float32) - mid.astype(jnp.float32)
    return hi, mid, rest.astype(jnp.bfloat16)


def cubic(distance):
    inner = 2.0 / 3.0 - distance * distance + 0.5 * distance * distance * distance
    remote = 2.0 - distance
    outer = remote * remote * remote * (1.0 / 6.0)
    return jnp.where(distance < 1.0, inner, jnp.where(distance < 2.0, outer, 0.0))


def mask_kernel(mask_ref, rows_ref, out_ref, mask, rows, sems):
    stored, band = rows_ref.shape[:2]
    fetch = pltpu.make_async_copy(mask_ref, mask, sems.at[stored])
    copies = [
        pltpu.make_async_copy(rows_ref.at[t], rows.at[t], sems.at[t]) for t in range(stored)
    ]
    fetch.start()
    for copy in copies:
        copy.start()
    fetch.wait()
    factors = mask[...].astype(jnp.float32)
    for t, copy in enumerate(copies):
        copy.wait()
        for k in range(band):
            factor = factors[t : t + 1, k : k + 1]
            out_ref[t, k] = (rows[t, k].astype(jnp.float32) * factor).astype(jnp.bfloat16)


def field_kernel(
    after_hbm, near_ref, table_hbm, radius_hbm, harm_hbm,
    g_ref, hpad_ref, atom_ref, table_ref, radius_ref, harm_ref, sems,
):
    batches, near, comps, points = harm_ref.shape
    knots = table_ref.shape[0]
    moves = ((table_hbm, table_ref), (radius_hbm, radius_ref), (harm_hbm, harm_ref))
    copies = [pltpu.make_async_copy(a, b, sems.at[n]) for n, (a, b) in enumerate(moves)]
    for copy in copies:
        copy.start()
    lane = lax.broadcasted_iota(jnp.int32, atom_ref.shape, 1)
    atom = jnp.full(atom_ref.shape, -1, jnp.int32)
    for b in range(batches):
        for i in range(near):
            atom = jnp.where(lane == b * SLOT + i, near_ref[i, b], atom)
    atom_ref[...] = atom
    hpad_ref[...] = jnp.zeros(hpad_ref.shape, hpad_ref.dtype)
    knot = lax.broadcasted_iota(jnp.int32, (knots, points), 0).astype(jnp.float32)
    for copy in copies:
        copy.wait()
    r_hi, r_lo = split2(table_ref[...].T)
    coeffs = jnp.concatenate([r_hi, r_hi, r_lo], axis=1)

    def body(b, carry):
        rows = radius_ref[b]
        for i in range(near):
            spline = cubic(jnp.abs(rows[i : i + 1, :] - knot))
            s_hi, s_lo = split2(spline)
            radial = dot(coeffs, jnp.concatenate([s_hi, s_lo, s_hi], axis=0))
            h = harm_ref[b, i]
            g_ref[b * near + i] = radial * h.astype(jnp.float32)
            hpad_ref[b * near + i, 0:comps, :] = h
        return carry

    lax.fori_loop(0, batches, body, 0)


def turn_kernel(after_hbm, basis_hbm, part_hbm, phit_ref, part_ref, basis, sems):
    batches, near_blocks = basis.shape[:2]
    halves = [pl.ds(0, batches // 2), pl.ds(batches // 2, batches - batches // 2)]
    copies = [
        pltpu.make_async_copy(basis_hbm.at[half], basis.at[half], sems.at[n])
        for n, half in enumerate(halves)
    ]
    copies.append(pltpu.make_async_copy(part_hbm, part_ref, sems.at[2]))
    for copy in copies:
        copy.start()

    def turn(b, carry):
        for j in range(near_blocks):
            phit_ref[b, j] = basis[b, j].T
        return carry

    copies[0].wait()
    lax.fori_loop(0, batches // 2, turn, 0)
    copies[1].wait()
    lax.fori_loop(batches // 2, batches, turn, 0)
    copies[2].wait()


def density_kernel(start_ref, offset_ref, size_ref, atom_ref, phit_ref, part_ref, hpad_ref, *refs):
    dens_ref, terms_ref, window_ref, w_ref = refs[-4:]
    pieces = refs[:-4]
    owners = window_ref.shape[0]
    batches, near_blocks, width, points = phit_ref.shape
    near = part_ref.shape[1]
    if len(pieces) == owners:
        me = lax.axis_index("dev")
        odd = lax.rem(me, 2)
        held = [
            (piece, lax.bitwise_xor(me, jnp.where(odd == 1, b, a)))
            for piece, a, b in zip(pieces, EVEN_OWNERS, ODD_OWNERS)
        ]
    else:
        held = [(pieces[0].at[owner], owner) for owner in range(owners)]
    stored = held[0][0].shape[0]
    start = start_ref[0]
    for piece, owner in held:
        ahead = lax.rem(owner - start + stored * owners, owners)
        row = lax.rem(start + ahead, stored * owners) // owners
        window_ref[ahead] = piece[row]
    w_ref[...] = jnp.zeros(w_ref.shape, w_ref.dtype)
    lane = lax.broadcasted_iota(jnp.int32, (1, points), 1)
    zero = jnp.zeros((width, width), jnp.bfloat16)

    def body(b, carry):
        first = offset_ref[0, b]
        total = jnp.zeros((width, points), jnp.float32)
        for q, js in ((0, (0, 1, 2)), (2, (0, 1, 2, 3))):
            left = []
            for j in js:
                pair = [
                    window_ref[first + j, f - j + 1] if 0 <= f - j + 1 < 4 else zero
                    for f in (q, q + 1)
                ]
                left.append(jnp.concatenate(pair, axis=1))
            right = jnp.concatenate([phit_ref[b, q], phit_ref[b, q + 1]], axis=0)
            mixed = dot(jnp.concatenate(left, axis=0), right)
            for at, j in enumerate(js):
                part = mixed[at * width : (at + 1) * width]
                total = total + part * phit_ref[b, j].astype(jnp.float32)
        summed = jnp.sum(total, axis=0, keepdims=True)
        alive = lane < size_ref[0, b]
        row = jnp.where(alive, summed, 0.0)
        dens_ref[pl.ds(b, 1), :] = row
        w_ref[b, 0:near, :] = part_ref[b] * row
        return carry

    lax.fori_loop(0, batches, body, 0, unroll=2)
    weights = w_ref[...].reshape(LANES, points)
    columns = jnp.concatenate(split2(weights), axis=0)
    slot = lax.broadcasted_iota(jnp.int32, (1, 2 * LANES), 1) % LANES
    cross = dot(hpad_ref[...].reshape(batches * near * ROWS, points), columns, NT)
    terms = jnp.zeros((ROWS, 2 * LANES), jnp.float32)
    for b in range(batches):
        for i in range(near):
            at = (b * near + i) * ROWS
            terms = terms + jnp.where(slot == b * SLOT + i, cross[at : at + ROWS], 0.0)
    result = terms[:, :LANES] + terms[:, LANES:]
    row_id = lax.broadcasted_iota(jnp.int32, (ROWS, LANES), 0)
    comps = ROWS - 7
    terms_ref[...] = jnp.where(row_id == comps, atom_ref[...].astype(jnp.float32), result)


def scatter_kernel(comps, atoms, flip, *refs):
    outs = refs[-4:]
    pieces = refs[:-4]
    row_id = lax.broadcasted_iota(jnp.int32, (3 * atoms, LANES), 0)
    total = jnp.zeros((3 * ROWS, 3 * atoms), jnp.float32)
    for piece in pieces:
        left, right = [], []
        for part in range(piece.shape[0]):
            values = piece[part]
            chosen = values[comps : comps + 1, :].astype(jnp.int32)
            right.append((row_id == chosen).astype(jnp.float32).astype(jnp.bfloat16))
            left.append(jnp.concatenate(split3(values), axis=0))
        total = total + dot(jnp.concatenate(left, axis=1), jnp.concatenate(right, axis=1), NT)
    sums = total[:ROWS] + total[ROWS : 2 * ROWS] + total[2 * ROWS :]
    own, near_a, near_b, far = outs
    own[...] = sums
    ahead, back = sums[:, atoms:], sums[:, : 2 * atoms]
    if flip:
        odd = lax.rem(lax.axis_index("region"), 2) == 1
        near_a[...] = jnp.where(odd, back, ahead)
        near_b[...] = jnp.where(odd, ahead, back)
    else:
        near_a[...] = ahead
        near_b[...] = back
    far[:, :atoms] = sums[:, :atoms]
    far[:, atoms:] = sums[:, 2 * atoms :]


def potential_kernel(
    comps, atoms, flip, size_ref, own_ref, near_a_ref, near_b_ref, fa_ref, fb_ref, atom_ref, g_ref,
    mom_ref, pot_ref,
):
    batches, points = pot_ref.shape
    near = g_ref.shape[0] // batches
    own = own_ref[...]
    near_a, near_b = near_a_ref[...], near_b_ref[...]
    if flip:
        odd = lax.rem(lax.axis_index("region"), 2) == 1
        low = jnp.where(odd, near_a, near_b)
        high = jnp.where(odd, near_b, near_a)
    else:
        low, high = near_a, near_b
    before = fa_ref[:, atoms:] + low[:, :atoms] + own[:, :atoms]
    here = low[:, atoms:] + own[:, atoms : 2 * atoms] + high[:, :atoms]
    after = own[:, 2 * atoms :] + high[:, atoms:] + fb_ref[:, :atoms]

    mine = mom_ref.shape[0]
    want = lax.broadcasted_iota(jnp.int32, (mine, atoms), 0) + lax.axis_index("dev") * mine
    keep = want == lax.broadcasted_iota(jnp.int32, (mine, atoms), 1)
    keep = keep.astype(jnp.float32).astype(jnp.bfloat16)
    taken = dot(keep, jnp.concatenate(split3(here), axis=0), NT)
    taken = taken[:, :ROWS] + taken[:, ROWS : 2 * ROWS] + taken[:, 2 * ROWS :]
    mom_ref[...] = taken[:, :comps]

    moments = jnp.concatenate([before, here, after], axis=1)
    row_id = lax.broadcasted_iota(jnp.int32, (3 * atoms, LANES), 0)
    pick = (row_id == atom_ref[...]).astype(jnp.float32).astype(jnp.bfloat16)
    got = dot(jnp.concatenate(split3(moments), axis=0), pick)
    chosen = got[:ROWS] + got[ROWS : 2 * ROWS] + got[2 * ROWS :]
    chosen = chosen[:comps]
    lane = lax.broadcasted_iota(jnp.int32, (1, points), 1)
    for b in range(batches):
        total = jnp.zeros((comps, points), jnp.float32)
        for i in range(near):
            column = chosen[:, b * SLOT + i : b * SLOT + i + 1]
            total = total + column * g_ref[b * near + i]
        row = jnp.sum(total, axis=0, keepdims=True)
        pot_ref[b : b + 1, :] = jnp.where(lane < size_ref[0, b], row, 0.0)


def crossed(value, axis, m):
    return lax.ppermute(value, axis, [(i, i ^ m) for i in range(lax.axis_size(axis))])


def turned(value, even, odd):
    count = lax.axis_size("dev")
    return lax.ppermute(value, "dev", [(i, i ^ (odd if i % 2 else even)) for i in range(count)])


def shifted(value, axis, step):
    count = lax.axis_size(axis)
    return lax.ppermute(value, axis, [(i, (i + step) % count) for i in range(count)])


def per_device(
    basis_values,
    density_rows,
    block_mask,
    window_start,
    batch_offsets,
    batch_sizes,
    atom_near,
    harmonics,
    partition,
    radius,
    radial_table,
):
    dev_count = lax.axis_size("dev")
    region_count = lax.axis_size("region")
    blocks_dev, band, width = density_rows.shape[:3]
    batches, near, comps, points = harmonics.shape
    near_blocks = basis_values.shape[1]
    mine = 16
    atoms = mine * dev_count
    f32, bf16 = jnp.float32, jnp.bfloat16

    masked = pl.pallas_call(
        mask_kernel,
        out_shape=jax.ShapeDtypeStruct(density_rows.shape, bf16),
        in_specs=[HBM, HBM],
        out_specs=VMEM,
        scratch_shapes=[
            pltpu.VMEM(block_mask.shape, jnp.int32),
            pltpu.VMEM(density_rows.shape, bf16),
            pltpu.SemaphoreType.DMA((blocks_dev + 1,)),
        ],
        compiler_params=pltpu.CompilerParams(vmem_limit_bytes=63 * 1024 * 1024),
        name="mask",
    )(block_mask, density_rows)
    g, hpad, atom_rows = pl.pallas_call(
        field_kernel,
        out_shape=(
            jax.ShapeDtypeStruct((batches * near, comps, points), f32),
            jax.ShapeDtypeStruct((batches * near, ROWS, points), bf16),
            jax.ShapeDtypeStruct((1, LANES), jnp.int32),
        ),
        in_specs=[HBM, SMEM] + [HBM] * 3,
        out_specs=(VMEM,) * 3,
        scratch_shapes=[
            pltpu.VMEM(radial_table.shape[::-1], f32),
            pltpu.VMEM(radius.shape, f32),
            pltpu.VMEM(harmonics.shape, bf16),
            pltpu.SemaphoreType.DMA((3,)),
        ],
        compiler_params=WIDE,
        cost_estimate=pl.CostEstimate(flops=2_000_000_000, bytes_accessed=8_000_000, transcendentals=0),
        name="field",
    )(masked, atom_near.T, radial_table.T, radius, harmonics)

    def turned_basis(after):
        return pl.pallas_call(
            turn_kernel,
            out_shape=(
                jax.ShapeDtypeStruct((batches, near_blocks, width, points), bf16),
                jax.ShapeDtypeStruct(partition.shape, f32),
            ),
            in_specs=[HBM] * 3,
            out_specs=(VMEM,) * 2,
            scratch_shapes=[pltpu.VMEM(basis_values.shape, bf16), pltpu.SemaphoreType.DMA((3,))],
            compiler_params=WIDE,
            cost_estimate=pl.CostEstimate(
                flops=2_000_000_000, bytes_accessed=8_000_000, transcendentals=0
            ),
            name="turn",
        )(after, basis_values, partition)

    if dev_count == 8:
        first = turned(masked, 4, 2)
        second = turned(masked, 2, 4)
        first, g = lax.optimization_barrier((first, g))
        third = turned(first, 2, 4)
        phit, weights = turned_basis(first)
        second, phit = lax.optimization_barrier((second, phit))
        sent = (masked, first, second, third)
        pieces = [piece for value in sent for piece in (value, crossed(value, "dev", 1))]
    else:
        phit, weights = turned_basis(masked)
        pieces = [lax.all_gather(masked, "dev", axis=0)]

    density, terms = pl.pallas_call(
        density_kernel,
        out_shape=(
            jax.ShapeDtypeStruct((batches, points), f32),
            jax.ShapeDtypeStruct((ROWS, LANES), f32),
        ),
        in_specs=[SMEM] * 3 + [VMEM] * (4 + len(pieces)),
        out_specs=(VMEM, VMEM),
        scratch_shapes=[
            pltpu.VMEM((dev_count, band, width, width), bf16),
            pltpu.VMEM((LANES // SLOT, SLOT, points), f32),
        ],
        compiler_params=PARAMS,
        cost_estimate=pl.CostEstimate(flops=2_000_000_000, bytes_accessed=6_000_000, transcendentals=0),
        name="density",
    )(
        window_start, batch_offsets, batch_sizes, atom_rows, phit, weights, hpad,
        *pieces,
    )

    both = jnp.stack([terms, crossed(terms, "dev", 1)])
    groups = [both] + [crossed(both, "dev", m) for m in range(2, dev_count, 2)]
    flip = region_count == 4
    own, near_a, near_b, far = pl.pallas_call(
        functools.partial(scatter_kernel, comps, atoms, flip),
        out_shape=tuple(jax.ShapeDtypeStruct((ROWS, n * atoms), f32) for n in (3, 2, 2, 2)),
        in_specs=[VMEM] * len(groups),
        out_specs=(VMEM,) * 4,
        compiler_params=PARAMS,
        name="scatter",
    )(*groups)
    if flip:
        far_a = far_b = crossed(far, "region", 2)
        near_a = crossed(near_a, "region", 1)
        near_b = crossed(near_b, "region", 3)
    else:
        far_a = shifted(far, "region", 2)
        far_b = shifted(far, "region", -2)
        near_a = shifted(near_a, "region", 1)
        near_b = shifted(near_b, "region", -1)

    moments, potential = pl.pallas_call(
        functools.partial(potential_kernel, comps, atoms, flip),
        out_shape=(
            jax.ShapeDtypeStruct((mine, comps), f32),
            jax.ShapeDtypeStruct((batches, points), f32),
        ),
        in_specs=[SMEM] + [VMEM] * 7,
        out_specs=(VMEM, VMEM),
        compiler_params=PARAMS,
        name="potential",
    )(batch_sizes, own, near_a, near_b, far_a, far_b, atom_rows, g)
    return (density, moments.T, potential)


def solution(mesh):
    both = ("region", "dev")
    placed = (
        P(both, None, None, None),
        P(both, None, None, None),
        P(both, None),
        P(both),
        P(both, None),
        P(both, None),
        P(both, None),
        P(both, None, None, None),
        P(both, None, None),
        P(both, None, None),
        P(),
    )
    return jax.shard_map(
        per_device,
        mesh=mesh,
        in_specs=placed,
        out_specs=(P(both, None), P(None, both), P(both, None)),
        check_vma=False,
    )
```

```python
import functools
import jax
import jax.numpy as jnp
from jax import lax
from jax.experimental import pallas as pl
from jax.experimental.pallas import tpu as pltpu
from jax.sharding import PartitionSpec as P

EVEN_OWNERS = (0, 1, 4, 3, 2, 5, 6, 7)
ODD_OWNERS = (0, 1, 2, 5, 4, 3, 6, 7)
DOUBLED = (0, 4, 2, 6, 1, 5, 3, 7)
LANES = 128
ROWS = 32
SLOT = 8
NT = (((1,), (1,)), ((), ()))
NN = (((1,), (0,)), ((), ()))
VMEM = pl.BlockSpec(memory_space=pltpu.VMEM)
SMEM = pl.BlockSpec(memory_space=pltpu.SMEM)
HBM = pl.BlockSpec(memory_space=pltpu.HBM)
WIDE = pltpu.CompilerParams(vmem_limit_bytes=16 * 1024 * 1024)
PARAMS = pltpu.CompilerParams(vmem_limit_bytes=16 * 1024 * 1024)


def dot(a, b, dims=NN):
    return lax.dot_general(a, b, dims, preferred_element_type=jnp.float32)


def split2(x):
    hi = x.astype(jnp.bfloat16)
    lo = (x - hi.astype(jnp.float32)).astype(jnp.bfloat16)
    return hi, lo


def split3(x):
    hi, mid = split2(x)
    rest = x - hi.astype(jnp.float32) - mid.astype(jnp.float32)
    return hi, mid, rest.astype(jnp.bfloat16)


def cubic(distance):
    inner = 2.0 / 3.0 - distance * distance + 0.5 * distance * distance * distance
    remote = 2.0 - distance
    outer = remote * remote * remote * (1.0 / 6.0)
    return jnp.where(distance < 1.0, inner, jnp.where(distance < 2.0, outer, 0.0))


def field_kernel(
    near_ref, table_hbm, radius_hbm, harm_hbm,
    g_ref, hpad_ref, atom_ref, table_ref, radius_ref, harm_ref, sems,
):
    batches, near, comps, points = harm_ref.shape
    knots = table_ref.shape[0]
    moves = ((table_hbm, table_ref), (radius_hbm, radius_ref), (harm_hbm, harm_ref))
    copies = [pltpu.make_async_copy(a, b, sems.at[n]) for n, (a, b) in enumerate(moves)]
    for copy in copies:
        copy.start()
    lane = lax.broadcasted_iota(jnp.int32, atom_ref.shape, 1)
    atom = jnp.full(atom_ref.shape, -1, jnp.int32)
    for b in range(batches):
        for i in range(near):
            atom = jnp.where(lane == b * SLOT + i, near_ref[i, b], atom)
    atom_ref[...] = atom
    hpad_ref[...] = jnp.zeros(hpad_ref.shape, hpad_ref.dtype)
    knot = lax.broadcasted_iota(jnp.int32, (knots, points), 0).astype(jnp.float32)
    for copy in copies:
        copy.wait()
    r_hi, r_lo = split2(table_ref[...].T)
    coeffs = jnp.concatenate([r_hi, r_hi, r_lo], axis=1)

    def body(b, carry):
        rows = radius_ref[b]
        for i in range(near):
            spline = cubic(jnp.abs(rows[i : i + 1, :] - knot))
            s_hi, s_lo = split2(spline)
            radial = dot(coeffs, jnp.concatenate([s_hi, s_lo, s_hi], axis=0))
            h = harm_ref[b, i]
            g_ref[b * near + i] = radial * h.astype(jnp.float32)
            hpad_ref[b * near + i, 0:comps, :] = h
        return carry

    lax.fori_loop(0, batches, body, 0)


def turn_kernel(after_hbm, basis_hbm, part_hbm, phit_ref, part_ref, basis, sems):
    batches, near_blocks = basis.shape[:2]
    halves = [pl.ds(0, batches // 2), pl.ds(batches // 2, batches - batches // 2)]
    copies = [
        pltpu.make_async_copy(basis_hbm.at[half], basis.at[half], sems.at[n])
        for n, half in enumerate(halves)
    ]
    copies.append(pltpu.make_async_copy(part_hbm, part_ref, sems.at[2]))
    for copy in copies:
        copy.start()

    def turn(b, carry):
        for j in range(near_blocks):
            phit_ref[b, j] = basis[b, j].T
        return carry

    copies[0].wait()
    lax.fori_loop(0, batches // 2, turn, 0)
    copies[1].wait()
    lax.fori_loop(batches // 2, batches, turn, 0)
    copies[2].wait()


def density_kernel(start_ref, offset_ref, size_ref, mask_ref, atom_ref, phit_ref, part_ref, hpad_ref, *refs):
    dens_ref, terms_ref, window_ref, w_ref = refs[-4:]
    pieces = refs[:-4]
    owners = window_ref.shape[0]
    batches, near_blocks, width, points = phit_ref.shape
    near = part_ref.shape[1]
    if len(pieces) == owners:
        me = lax.axis_index("dev")
        odd = lax.rem(me, 2) == 1
        held = [
            (
                piece,
                lax.bitwise_xor(me, jnp.where(odd, b, a)),
                jnp.where(odd, DOUBLED.index(b), DOUBLED.index(a)),
            )
            for piece, a, b in zip(pieces, EVEN_OWNERS, ODD_OWNERS)
        ]
    else:
        held = [(pieces[0].at[owner], owner, owner) for owner in range(owners)]
    stored, band = held[0][0].shape[:2]
    start = start_ref[0]
    for piece, owner, at in held:
        ahead = lax.rem(owner - start + stored * owners, owners)
        row = lax.rem(start + ahead, stored * owners) // owners
        for k in range(band):
            factor = jnp.full((width, width), mask_ref[at * stored + row, k].astype(jnp.float32))
            window_ref[ahead, k] = piece[row, k] * factor.astype(jnp.bfloat16)
    w_ref[...] = jnp.zeros(w_ref.shape, w_ref.dtype)
    lane = lax.broadcasted_iota(jnp.int32, (1, points), 1)
    zero = jnp.zeros((width, width), jnp.bfloat16)

    def body(b, carry):
        first = offset_ref[0, b]
        total = jnp.zeros((width, points), jnp.float32)
        for q, js in ((0, (0, 1, 2)), (2, (0, 1, 2, 3))):
            left = []
            for j in js:
                pair = [
                    window_ref[first + j, f - j + 1] if 0 <= f - j + 1 < 4 else zero
                    for f in (q, q + 1)
                ]
                left.append(jnp.concatenate(pair, axis=1))
            right = jnp.concatenate([phit_ref[b, q], phit_ref[b, q + 1]], axis=0)
            mixed = dot(jnp.concatenate(left, axis=0), right)
            for at, j in enumerate(js):
                part = mixed[at * width : (at + 1) * width]
                total = total + part * phit_ref[b, j].astype(jnp.float32)
        summed = jnp.sum(total, axis=0, keepdims=True)
        alive = lane < size_ref[0, b]
        row = jnp.where(alive, summed, 0.0)
        dens_ref[pl.ds(b, 1), :] = row
        w_ref[b, 0:near, :] = part_ref[b] * row
        return carry

    lax.fori_loop(0, batches, body, 0, unroll=4)
    weights = w_ref[...].reshape(LANES, points)
    columns = jnp.concatenate(split2(weights), axis=0)
    slot = lax.broadcasted_iota(jnp.int32, (1, 2 * LANES), 1) % LANES
    cross = dot(hpad_ref[...].reshape(batches * near * ROWS, points), columns, NT)
    terms = jnp.zeros((ROWS, 2 * LANES), jnp.float32)
    for b in range(batches):
        for i in range(near):
            at = (b * near + i) * ROWS
            terms = terms + jnp.where(slot == b * SLOT + i, cross[at : at + ROWS], 0.0)
    result = terms[:, :LANES] + terms[:, LANES:]
    row_id = lax.broadcasted_iota(jnp.int32, (ROWS, LANES), 0)
    comps = ROWS - 7
    terms_ref[...] = jnp.where(row_id == comps, atom_ref[...].astype(jnp.float32), result)


def scatter_kernel(comps, atoms, flip, pieces, own, near_a, near_b, far):
    row_id = lax.broadcasted_iota(jnp.int32, (3 * atoms, LANES), 0)
    total = jnp.zeros((3 * ROWS, 3 * atoms), jnp.float32)
    for m in range(0, pieces.shape[0], 2):
        left, right = [], []
        for values in (pieces[m], pieces[m + 1]):
            chosen = values[comps : comps + 1, :].astype(jnp.int32)
            right.append((row_id == chosen).astype(jnp.float32).astype(jnp.bfloat16))
            left.append(jnp.concatenate(split3(values), axis=0))
        total = total + dot(jnp.concatenate(left, axis=1), jnp.concatenate(right, axis=1), NT)
    sums = total[:ROWS] + total[ROWS : 2 * ROWS] + total[2 * ROWS :]
    own[...] = sums
    ahead, back = sums[:, atoms:], sums[:, : 2 * atoms]
    if flip:
        odd = lax.rem(lax.axis_index("region"), 2) == 1
        near_a[...] = jnp.where(odd, back, ahead)
        near_b[...] = jnp.where(odd, ahead, back)
    else:
        near_a[...] = ahead
        near_b[...] = back
    far[:, :atoms] = sums[:, :atoms]
    far[:, atoms:] = sums[:, 2 * atoms :]


def potential_kernel(
    comps, atoms, flip, size_ref, own_ref, near_a_ref, near_b_ref, fa_ref, fb_ref, atom_ref, g_ref,
    mom_ref, pot_ref,
):
    batches, points = pot_ref.shape
    near = g_ref.shape[0] // batches
    own = own_ref[...]
    near_a, near_b = near_a_ref[...], near_b_ref[...]
    if flip:
        odd = lax.rem(lax.axis_index("region"), 2) == 1
        low = jnp.where(odd, near_a, near_b)
        high = jnp.where(odd, near_b, near_a)
    else:
        low, high = near_a, near_b
    before = fa_ref[:, atoms:] + low[:, :atoms] + own[:, :atoms]
    here = low[:, atoms:] + own[:, atoms : 2 * atoms] + high[:, :atoms]
    after = own[:, 2 * atoms :] + high[:, atoms:] + fb_ref[:, :atoms]

    mine = mom_ref.shape[0]
    want = lax.broadcasted_iota(jnp.int32, (mine, atoms), 0) + lax.axis_index("dev") * mine
    keep = want == lax.broadcasted_iota(jnp.int32, (mine, atoms), 1)
    keep = keep.astype(jnp.float32).astype(jnp.bfloat16)
    taken = dot(keep, jnp.concatenate(split3(here), axis=0), NT)
    taken = taken[:, :ROWS] + taken[:, ROWS : 2 * ROWS] + taken[:, 2 * ROWS :]
    mom_ref[...] = taken[:, :comps]

    moments = jnp.concatenate([before, here, after], axis=1)
    row_id = lax.broadcasted_iota(jnp.int32, (3 * atoms, LANES), 0)
    pick = (row_id == atom_ref[...]).astype(jnp.float32).astype(jnp.bfloat16)
    got = dot(jnp.concatenate(split3(moments), axis=0), pick)
    chosen = got[:ROWS] + got[ROWS : 2 * ROWS] + got[2 * ROWS :]
    chosen = chosen[:comps]
    lane = lax.broadcasted_iota(jnp.int32, (1, points), 1)
    for b in range(batches):
        total = jnp.zeros((comps, points), jnp.float32)
        for i in range(near):
            column = chosen[:, b * SLOT + i : b * SLOT + i + 1]
            total = total + column * g_ref[b * near + i]
        row = jnp.sum(total, axis=0, keepdims=True)
        pot_ref[b : b + 1, :] = jnp.where(lane < size_ref[0, b], row, 0.0)


def held_in_hbm(*values):
    return [pltpu.with_memory_space_constraint(value, pltpu.HBM) for value in values]


def crossed(value, axis, m):
    return lax.ppermute(value, axis, [(i, i ^ m) for i in range(lax.axis_size(axis))])


def turned(value, even, odd):
    count = lax.axis_size("dev")
    return lax.ppermute(value, "dev", [(i, i ^ (odd if i % 2 else even)) for i in range(count)])


def shifted(value, axis, step):
    count = lax.axis_size(axis)
    return lax.ppermute(value, axis, [(i, (i + step) % count) for i in range(count)])


def per_device(
    basis_values,
    density_rows,
    block_mask,
    window_start,
    batch_offsets,
    batch_sizes,
    atom_near,
    harmonics,
    partition,
    radius,
    radial_table,
):
    dev_count = lax.axis_size("dev")
    region_count = lax.axis_size("region")
    blocks_dev, band, width = density_rows.shape[:3]
    batches, near, comps, points = harmonics.shape
    near_blocks = basis_values.shape[1]
    mine = 16
    atoms = mine * dev_count
    f32, bf16 = jnp.float32, jnp.bfloat16

    g, hpad, atom_rows = pl.pallas_call(
        field_kernel,
        out_shape=(
            pltpu.VMEM((batches * near, comps, points), f32),
            pltpu.VMEM((batches * near, ROWS, points), bf16),
            pltpu.VMEM((1, LANES), jnp.int32),
        ),
        in_specs=[SMEM] + [HBM] * 3,
        out_specs=(VMEM,) * 3,
        scratch_shapes=[
            pltpu.VMEM(radial_table.shape[::-1], f32),
            pltpu.VMEM(radius.shape, f32),
            pltpu.VMEM(harmonics.shape, bf16),
            pltpu.SemaphoreType.DMA((3,)),
        ],
        compiler_params=WIDE,
        cost_estimate=pl.CostEstimate(flops=2_000_000_000, bytes_accessed=8_000_000, transcendentals=0),
        name="field",
    )(atom_near.T, *held_in_hbm(radial_table.T, radius, harmonics))

    def turned_basis(after):
        return pl.pallas_call(
            turn_kernel,
            out_shape=(
                pltpu.VMEM((batches, near_blocks, width, points), bf16),
                pltpu.VMEM(partition.shape, f32),
            ),
            in_specs=[HBM] * 3,
            out_specs=(VMEM,) * 2,
            scratch_shapes=[pltpu.VMEM(basis_values.shape, bf16), pltpu.SemaphoreType.DMA((3,))],
            compiler_params=WIDE,
            cost_estimate=pl.CostEstimate(
                flops=2_000_000_000, bytes_accessed=8_000_000, transcendentals=0
            ),
            name="turn",
        )(after, *held_in_hbm(basis_values, partition))

    if dev_count == 8:
        masks = block_mask
        other = crossed(masks, "dev", 4)
        first = turned(density_rows, 4, 2)
        rows, g = lax.optimization_barrier((density_rows, g))
        first, other, g = lax.optimization_barrier((first, other, g))
        second = turned(rows, 2, 4)
        third = turned(first, 2, 4)
        masks = jnp.concatenate([masks, other])
        other = crossed(masks, "dev", 2)
        phit, weights = turned_basis(first)
        other, phit = lax.optimization_barrier((other, phit))
        second, phit = lax.optimization_barrier((second, phit))
        masks = jnp.concatenate([masks, other])
        masks = jnp.concatenate([masks, crossed(masks, "dev", 1)])
        sent = (density_rows, first, second, third)
        pieces = [piece for value in sent for piece in (value, crossed(value, "dev", 1))]
    else:
        phit, weights = turned_basis(density_rows)
        pieces = [lax.all_gather(density_rows, "dev", axis=0)]
        masks = lax.all_gather(block_mask, "dev", axis=0, tiled=True)

    density, terms = pl.pallas_call(
        density_kernel,
        out_shape=(
            jax.ShapeDtypeStruct((batches, points), f32),
            jax.ShapeDtypeStruct((ROWS, LANES), f32),
        ),
        in_specs=[SMEM] * 4 + [VMEM] * (4 + len(pieces)),
        out_specs=(VMEM, VMEM),
        scratch_shapes=[
            pltpu.VMEM((dev_count, band, width, width), bf16),
            pltpu.VMEM((LANES // SLOT, SLOT, points), f32),
        ],
        compiler_params=PARAMS,
        cost_estimate=pl.CostEstimate(flops=2_000_000_000, bytes_accessed=6_000_000, transcendentals=0),
        name="density",
    )(
        window_start, batch_offsets, batch_sizes, masks, atom_rows, phit, weights, hpad,
        *pieces,
    )

    if dev_count == 8:
        groups = terms[None]
        for m in (4, 2, 1):
            groups = jnp.concatenate([groups, crossed(groups, "dev", m)])
    else:
        groups = lax.all_gather(terms, "dev", axis=0)
    flip = region_count == 4
    own, near_a, near_b, far = pl.pallas_call(
        functools.partial(scatter_kernel, comps, atoms, flip),
        out_shape=tuple(jax.ShapeDtypeStruct((ROWS, n * atoms), f32) for n in (3, 2, 2, 2)),
        in_specs=[VMEM],
        out_specs=(VMEM,) * 4,
        compiler_params=PARAMS,
        name="scatter",
    )(groups)
    if flip:
        far_a = far_b = crossed(far, "region", 2)
        near_a = crossed(near_a, "region", 1)
        near_b = crossed(near_b, "region", 3)
    else:
        far_a = shifted(far, "region", 2)
        far_b = shifted(far, "region", -2)
        near_a = shifted(near_a, "region", 1)
        near_b = shifted(near_b, "region", -1)

    moments, potential = pl.pallas_call(
        functools.partial(potential_kernel, comps, atoms, flip),
        out_shape=(
            jax.ShapeDtypeStruct((mine, comps), f32),
            jax.ShapeDtypeStruct((batches, points), f32),
        ),
        in_specs=[SMEM] + [VMEM] * 7,
        out_specs=(VMEM, VMEM),
        compiler_params=PARAMS,
        name="potential",
    )(batch_sizes, own, near_a, near_b, far_a, far_b, atom_rows, g)
    return (density, moments.T, potential)


def solution(mesh):
    both = ("region", "dev")
    placed = (
        P(both, None, None, None),
        P(both, None, None, None),
        P(both, None),
        P(both),
        P(both, None),
        P(both, None),
        P(both, None),
        P(both, None, None, None),
        P(both, None, None),
        P(both, None, None),
        P(),
    )
    return jax.shard_map(
        per_device,
        mesh=mesh,
        in_specs=placed,
        out_specs=(P(both, None), P(None, both), P(both, None)),
        check_vma=False,
    )
```

```python
import functools
import jax
import jax.numpy as jnp
from jax import lax
from jax.experimental import pallas as pl
from jax.experimental.pallas import tpu as pltpu
from jax.sharding import PartitionSpec as P

EVEN_OWNERS = (0, 1, 4, 3, 2, 5, 6, 7)
ODD_OWNERS = (0, 1, 2, 5, 4, 3, 6, 7)
DOUBLED = (0, 4, 2, 6, 1, 5, 3, 7)
LANES = 128
ROWS = 32
SLOT = 8
NT = (((1,), (1,)), ((), ()))
NN = (((1,), (0,)), ((), ()))
VMEM = pl.BlockSpec(memory_space=pltpu.VMEM)
SMEM = pl.BlockSpec(memory_space=pltpu.SMEM)
HBM = pl.BlockSpec(memory_space=pltpu.HBM)
WIDE = pltpu.CompilerParams(vmem_limit_bytes=16 * 1024 * 1024)
PARAMS = pltpu.CompilerParams(vmem_limit_bytes=16 * 1024 * 1024)


def dot(a, b, dims=NN):
    return lax.dot_general(a, b, dims, preferred_element_type=jnp.float32)


def split2(x):
    hi = x.astype(jnp.bfloat16)
    lo = (x - hi.astype(jnp.float32)).astype(jnp.bfloat16)
    return hi, lo


def split3(x):
    hi, mid = split2(x)
    rest = x - hi.astype(jnp.float32) - mid.astype(jnp.float32)
    return hi, mid, rest.astype(jnp.bfloat16)


def cubic(distance):
    inner = 2.0 / 3.0 - distance * distance + 0.5 * distance * distance * distance
    remote = 2.0 - distance
    outer = remote * remote * remote * (1.0 / 6.0)
    return jnp.where(distance < 1.0, inner, jnp.where(distance < 2.0, outer, 0.0))


def field_kernel(
    near_ref, table_hbm, radius_hbm, harm_hbm,
    g_ref, hpad_ref, atom_ref, table_ref, radius_ref, harm_ref, sems,
):
    batches, near, comps, points = harm_ref.shape
    knots = table_ref.shape[0]
    moves = ((table_hbm, table_ref), (radius_hbm, radius_ref), (harm_hbm, harm_ref))
    copies = [pltpu.make_async_copy(a, b, sems.at[n]) for n, (a, b) in enumerate(moves)]
    for copy in copies:
        copy.start()
    lane = lax.broadcasted_iota(jnp.int32, atom_ref.shape, 1)
    atom = jnp.full(atom_ref.shape, -1, jnp.int32)
    for b in range(batches):
        for i in range(near):
            atom = jnp.where(lane == b * SLOT + i, near_ref[i, b], atom)
    atom_ref[...] = atom
    hpad_ref[...] = jnp.zeros(hpad_ref.shape, hpad_ref.dtype)
    knot = lax.broadcasted_iota(jnp.int32, (knots, points), 0).astype(jnp.float32)
    for copy in copies:
        copy.wait()
    r_hi, r_lo = split2(table_ref[...].T)
    coeffs = jnp.concatenate([r_hi, r_hi, r_lo], axis=1)

    def body(b, carry):
        rows = radius_ref[b]
        for i in range(near):
            spline = cubic(jnp.abs(rows[i : i + 1, :] - knot))
            s_hi, s_lo = split2(spline)
            radial = dot(coeffs, jnp.concatenate([s_hi, s_lo, s_hi], axis=0))
            h = harm_ref[b, i]
            g_ref[b * near + i] = radial * h.astype(jnp.float32)
            hpad_ref[b * near + i, 0:comps, :] = h
        return carry

    lax.fori_loop(0, batches, body, 0)


def turn_kernel(after_hbm, basis_hbm, part_hbm, phit_ref, part_ref, basis, sems):
    batches, near_blocks = basis.shape[:2]
    halves = [pl.ds(0, batches // 2), pl.ds(batches // 2, batches - batches // 2)]
    copies = [
        pltpu.make_async_copy(basis_hbm.at[half], basis.at[half], sems.at[n])
        for n, half in enumerate(halves)
    ]
    copies.append(pltpu.make_async_copy(part_hbm, part_ref, sems.at[2]))
    for copy in copies:
        copy.start()

    def turn(b, carry):
        for j in range(near_blocks):
            phit_ref[b, j] = basis[b, j].T
        return carry

    copies[0].wait()
    lax.fori_loop(0, batches // 2, turn, 0)
    copies[1].wait()
    lax.fori_loop(batches // 2, batches, turn, 0)
    copies[2].wait()


def density_kernel(start_ref, offset_ref, size_ref, mask_ref, atom_ref, phit_ref, part_ref, hpad_ref, *refs):
    dens_ref, terms_ref, window_ref, w_ref = refs[-4:]
    pieces = refs[:-4]
    owners = window_ref.shape[0]
    batches, near_blocks, width, points = phit_ref.shape
    near = part_ref.shape[1]
    if len(pieces) == owners:
        me = lax.axis_index("dev")
        odd = lax.rem(me, 2) == 1
        held = [
            (
                piece,
                lax.bitwise_xor(me, jnp.where(odd, b, a)),
                jnp.where(odd, DOUBLED.index(b), DOUBLED.index(a)),
            )
            for piece, a, b in zip(pieces, EVEN_OWNERS, ODD_OWNERS)
        ]
    else:
        held = [(pieces[0].at[owner], owner, owner) for owner in range(owners)]
    stored, band = held[0][0].shape[:2]
    start = start_ref[0]
    for piece, owner, at in held:
        ahead = lax.rem(owner - start + stored * owners, owners)
        row = lax.rem(start + ahead, stored * owners) // owners
        for k in range(band):
            factor = jnp.full((width, width), mask_ref[at * stored + row, k].astype(jnp.float32))
            window_ref[ahead, k] = piece[row, k] * factor.astype(jnp.bfloat16)
    w_ref[...] = jnp.zeros(w_ref.shape, w_ref.dtype)
    lane = lax.broadcasted_iota(jnp.int32, (1, points), 1)
    zero = jnp.zeros((width, width), jnp.bfloat16)

    def body(b, carry):
        first = offset_ref[0, b]
        total = jnp.zeros((width, points), jnp.float32)
        for q, js in ((0, (0, 1, 2)), (2, (0, 1, 2, 3))):
            left = []
            for j in js:
                pair = [
                    window_ref[first + j, f - j + 1] if 0 <= f - j + 1 < 4 else zero
                    for f in (q, q + 1)
                ]
                left.append(jnp.concatenate(pair, axis=1))
            right = jnp.concatenate([phit_ref[b, q], phit_ref[b, q + 1]], axis=0)
            mixed = dot(jnp.concatenate(left, axis=0), right)
            for at, j in enumerate(js):
                part = mixed[at * width : (at + 1) * width]
                total = total + part * phit_ref[b, j].astype(jnp.float32)
        summed = jnp.sum(total, axis=0, keepdims=True)
        alive = lane < size_ref[0, b]
        row = jnp.where(alive, summed, 0.0)
        dens_ref[pl.ds(b, 1), :] = row
        w_ref[b, 0:near, :] = part_ref[b] * row
        return carry

    lax.fori_loop(0, batches, body, 0, unroll=4)
    weights = w_ref[...].reshape(LANES, points)
    columns = jnp.concatenate(split2(weights), axis=0)
    slot = lax.broadcasted_iota(jnp.int32, (1, 2 * LANES), 1) % LANES
    cross = dot(hpad_ref[...].reshape(batches * near * ROWS, points), columns, NT)
    terms = jnp.zeros((ROWS, 2 * LANES), jnp.float32)
    for b in range(batches):
        for i in range(near):
            at = (b * near + i) * ROWS
            terms = terms + jnp.where(slot == b * SLOT + i, cross[at : at + ROWS], 0.0)
    result = terms[:, :LANES] + terms[:, LANES:]
    row_id = lax.broadcasted_iota(jnp.int32, (ROWS, LANES), 0)
    comps = ROWS - 7
    terms_ref[...] = jnp.where(row_id == comps, atom_ref[...].astype(jnp.float32), result)


def scatter_kernel(comps, atoms, flip, *refs):
    own, near_a, near_b, far = refs[-4:]
    pieces = [group.at[m] for group in refs[:-4] for m in range(group.shape[0])]
    row_id = lax.broadcasted_iota(jnp.int32, (3 * atoms, LANES), 0)
    total = jnp.zeros((3 * ROWS, 3 * atoms), jnp.float32)
    for m in range(0, len(pieces), 2):
        left, right = [], []
        for values in (pieces[m][...], pieces[m + 1][...]):
            chosen = values[comps : comps + 1, :].astype(jnp.int32)
            right.append((row_id == chosen).astype(jnp.float32).astype(jnp.bfloat16))
            left.append(jnp.concatenate(split3(values), axis=0))
        total = total + dot(jnp.concatenate(left, axis=1), jnp.concatenate(right, axis=1), NT)
    sums = total[:ROWS] + total[ROWS : 2 * ROWS] + total[2 * ROWS :]
    own[...] = sums
    ahead, back = sums[:, atoms:], sums[:, : 2 * atoms]
    if flip:
        odd = lax.rem(lax.axis_index("region"), 2) == 1
        near_a[...] = jnp.where(odd, back, ahead)
        near_b[...] = jnp.where(odd, ahead, back)
    else:
        near_a[...] = ahead
        near_b[...] = back
    far[:, :atoms] = sums[:, :atoms]
    far[:, atoms:] = sums[:, 2 * atoms :]


def moments_kernel(atoms, flip, own_ref, near_a_ref, near_b_ref, fa_ref, fb_ref, out_ref):
    own = own_ref[...]
    near_a, near_b = near_a_ref[...], near_b_ref[...]
    if flip:
        odd = lax.rem(lax.axis_index("region"), 2) == 1
        low = jnp.where(odd, near_a, near_b)
        high = jnp.where(odd, near_b, near_a)
    else:
        low, high = near_a, near_b
    out_ref[:, :atoms] = fa_ref[:, atoms:] + low[:, :atoms] + own[:, :atoms]
    out_ref[:, atoms : 2 * atoms] = low[:, atoms:] + own[:, atoms : 2 * atoms] + high[:, :atoms]
    out_ref[:, 2 * atoms :] = own[:, 2 * atoms :] + high[:, atoms:] + fb_ref[:, :atoms]


def potential_kernel(
    comps, atoms, size_ref, moments_ref, other_ref, atom_ref, g_ref, mom_ref, pot_ref
):
    batches, points = pot_ref.shape
    near = g_ref.shape[0] // batches
    odd = lax.rem(lax.axis_index("dev"), 2) == 1
    moments = jnp.where(odd, moments_ref[...], other_ref[...])
    parts = jnp.concatenate(split3(moments), axis=0)

    mine = mom_ref.shape[0]
    want = lax.broadcasted_iota(jnp.int32, (mine, atoms), 0) + lax.axis_index("dev") * mine
    keep = want == lax.broadcasted_iota(jnp.int32, (mine, atoms), 1)
    keep = keep.astype(jnp.float32).astype(jnp.bfloat16)
    taken = dot(keep, parts[:, atoms : 2 * atoms], NT)
    taken = taken[:, :ROWS] + taken[:, ROWS : 2 * ROWS] + taken[:, 2 * ROWS :]
    mom_ref[...] = taken[:, :comps]

    row_id = lax.broadcasted_iota(jnp.int32, (3 * atoms, LANES), 0)
    pick = (row_id == atom_ref[...]).astype(jnp.float32).astype(jnp.bfloat16)
    got = dot(parts, pick)
    chosen = got[:ROWS] + got[ROWS : 2 * ROWS] + got[2 * ROWS :]
    chosen = chosen[:comps]
    lane = lax.broadcasted_iota(jnp.int32, (1, points), 1)
    for b in range(batches):
        total = jnp.zeros((comps, points), jnp.float32)
        for i in range(near):
            column = chosen[:, b * SLOT + i : b * SLOT + i + 1]
            total = total + column * g_ref[b * near + i]
        row = jnp.sum(total, axis=0, keepdims=True)
        pot_ref[b : b + 1, :] = jnp.where(lane < size_ref[0, b], row, 0.0)


def held_in_hbm(*values):
    return [pltpu.with_memory_space_constraint(value, pltpu.HBM) for value in values]


def crossed(value, axis, m):
    return lax.ppermute(value, axis, [(i, i ^ m) for i in range(lax.axis_size(axis))])


def turned(value, even, odd):
    count = lax.axis_size("dev")
    return lax.ppermute(value, "dev", [(i, i ^ (odd if i % 2 else even)) for i in range(count)])


def among_odd(value, m):
    count = lax.axis_size("dev")
    return lax.ppermute(value, "dev", [(i, i ^ m) for i in range(1, count, 2)])


def regions_of_odd(value, m):
    count, regions = lax.axis_size("dev"), lax.axis_size("region")
    pairs = [(r * count + i, (r ^ m) * count + i) for r in range(regions) for i in range(1, count, 2)]
    return lax.ppermute(value, ("region", "dev"), pairs)


def from_core(value, parity):
    count = lax.axis_size("dev")
    return lax.ppermute(value, "dev", [(i, i ^ 1) for i in range(parity, count, 2)])


def shifted(value, axis, step):
    count = lax.axis_size(axis)
    return lax.ppermute(value, axis, [(i, (i + step) % count) for i in range(count)])


def per_device(
    basis_values,
    density_rows,
    block_mask,
    window_start,
    batch_offsets,
    batch_sizes,
    atom_near,
    harmonics,
    partition,
    radius,
    radial_table,
):
    dev_count = lax.axis_size("dev")
    region_count = lax.axis_size("region")
    blocks_dev, band, width = density_rows.shape[:3]
    batches, near, comps, points = harmonics.shape
    near_blocks = basis_values.shape[1]
    mine = 16
    atoms = mine * dev_count
    f32, bf16 = jnp.float32, jnp.bfloat16

    g, hpad, atom_rows = pl.pallas_call(
        field_kernel,
        out_shape=(
            pltpu.VMEM((batches * near, comps, points), f32),
            pltpu.VMEM((batches * near, ROWS, points), bf16),
            pltpu.VMEM((1, LANES), jnp.int32),
        ),
        in_specs=[SMEM] + [HBM] * 3,
        out_specs=(VMEM,) * 3,
        scratch_shapes=[
            pltpu.VMEM(radial_table.shape[::-1], f32),
            pltpu.VMEM(radius.shape, f32),
            pltpu.VMEM(harmonics.shape, bf16),
            pltpu.SemaphoreType.DMA((3,)),
        ],
        compiler_params=WIDE,
        cost_estimate=pl.CostEstimate(flops=2_000_000_000, bytes_accessed=8_000_000, transcendentals=0),
        name="field",
    )(atom_near.T, *held_in_hbm(radial_table.T, radius, harmonics))

    def turned_basis(after):
        return pl.pallas_call(
            turn_kernel,
            out_shape=(
                pltpu.VMEM((batches, near_blocks, width, points), bf16),
                pltpu.VMEM(partition.shape, f32),
            ),
            in_specs=[HBM] * 3,
            out_specs=(VMEM,) * 2,
            scratch_shapes=[pltpu.VMEM(basis_values.shape, bf16), pltpu.SemaphoreType.DMA((3,))],
            compiler_params=WIDE,
            cost_estimate=pl.CostEstimate(
                flops=2_000_000_000, bytes_accessed=8_000_000, transcendentals=0
            ),
            name="turn",
        )(after, *held_in_hbm(basis_values, partition))

    if dev_count == 8:
        masks = block_mask
        other = crossed(masks, "dev", 4)
        first = turned(density_rows, 4, 2)
        first, other, g = lax.optimization_barrier((first, other, g))
        second = turned(density_rows, 2, 4)
        third = turned(first, 2, 4)
        masks = jnp.concatenate([masks, other])
        other = crossed(masks, "dev", 2)
        phit, weights = turned_basis(first)
        other, phit = lax.optimization_barrier((other, phit))
        second, phit = lax.optimization_barrier((second, phit))
        masks = jnp.concatenate([masks, other])
        masks = jnp.concatenate([masks, crossed(masks, "dev", 1)])
        sent = (density_rows, first, second, third)
        pieces = [piece for value in sent for piece in (value, crossed(value, "dev", 1))]
    else:
        phit, weights = turned_basis(density_rows)
        pieces = [lax.all_gather(density_rows, "dev", axis=0)]
        masks = lax.all_gather(block_mask, "dev", axis=0, tiled=True)

    density, terms = pl.pallas_call(
        density_kernel,
        out_shape=(
            jax.ShapeDtypeStruct((batches, points), f32),
            jax.ShapeDtypeStruct((ROWS, LANES), f32),
        ),
        in_specs=[SMEM] * 4 + [VMEM] * (4 + len(pieces)),
        out_specs=(VMEM, VMEM),
        scratch_shapes=[
            pltpu.VMEM((dev_count, band, width, width), bf16),
            pltpu.VMEM((LANES // SLOT, SLOT, points), f32),
        ],
        compiler_params=PARAMS,
        cost_estimate=pl.CostEstimate(flops=2_000_000_000, bytes_accessed=6_000_000, transcendentals=0),
        name="density",
    )(
        window_start, batch_offsets, batch_sizes, masks, atom_rows, phit, weights, hpad,
        *pieces,
    )

    small = dev_count == 8 and region_count == 4
    if small:
        both = jnp.stack([terms, from_core(terms, 0)])
        groups = [both] + [among_odd(both, m) for m in (6, 2, 4)]
    else:
        groups = [lax.all_gather(terms, "dev", axis=0)]
    own, near_a, near_b, far = pl.pallas_call(
        functools.partial(scatter_kernel, comps, atoms, small),
        out_shape=tuple(jax.ShapeDtypeStruct((ROWS, n * atoms), f32) for n in (3, 2, 2, 2)),
        in_specs=[VMEM] * len(groups),
        out_specs=(VMEM,) * 4,
        compiler_params=PARAMS,
        name="scatter",
    )(*groups)
    if small:
        far_a = far_b = regions_of_odd(far, 2)
        near_a = regions_of_odd(near_a, 1)
        near_b = regions_of_odd(near_b, 3)
    else:
        far_a = shifted(far, "region", 2)
        far_b = shifted(far, "region", -2)
        near_a = shifted(near_a, "region", 1)
        near_b = shifted(near_b, "region", -1)
    moments = pl.pallas_call(
        functools.partial(moments_kernel, atoms, small),
        out_shape=jax.ShapeDtypeStruct((ROWS, 3 * atoms), f32),
        in_specs=[VMEM] * 5,
        out_specs=VMEM,
        compiler_params=PARAMS,
        name="moments",
    )(own, near_a, near_b, far_a, far_b)
    other = from_core(moments, 1) if small else moments

    moments, potential = pl.pallas_call(
        functools.partial(potential_kernel, comps, atoms),
        out_shape=(
            jax.ShapeDtypeStruct((mine, comps), f32),
            jax.ShapeDtypeStruct((batches, points), f32),
        ),
        in_specs=[SMEM] + [VMEM] * 4,
        out_specs=(VMEM, VMEM),
        compiler_params=PARAMS,
        name="potential",
    )(batch_sizes, moments, other, atom_rows, g)
    return (density, moments.T, potential)


def solution(mesh):
    both = ("region", "dev")
    placed = (
        P(both, None, None, None),
        P(both, None, None, None),
        P(both, None),
        P(both),
        P(both, None),
        P(both, None),
        P(both, None),
        P(both, None, None, None),
        P(both, None, None),
        P(both, None, None),
        P(),
    )
    return jax.shard_map(
        per_device,
        mesh=mesh,
        in_specs=placed,
        out_specs=(P(both, None), P(None, both), P(both, None)),
        check_vma=False,
    )
```

```python
import functools
import jax
import jax.numpy as jnp
from jax import lax
from jax.experimental import pallas as pl
from jax.experimental.pallas import tpu as pltpu
from jax.sharding import PartitionSpec as P

EVEN_OWNERS = (0, 1, 4, 3, 2, 5, 6, 7)
ODD_OWNERS = (0, 1, 2, 5, 4, 3, 6, 7)
LANES = 128
ROWS = 32
SLOT = 8
NT = (((1,), (1,)), ((), ()))
NN = (((1,), (0,)), ((), ()))
VMEM = pl.BlockSpec(memory_space=pltpu.VMEM)
SMEM = pl.BlockSpec(memory_space=pltpu.SMEM)
HBM = pl.BlockSpec(memory_space=pltpu.HBM)
WIDE = pltpu.CompilerParams(vmem_limit_bytes=16 * 1024 * 1024)
PARAMS = pltpu.CompilerParams(vmem_limit_bytes=16 * 1024 * 1024)


def dot(a, b, dims=NN):
    return lax.dot_general(a, b, dims, preferred_element_type=jnp.float32)


def split2(x):
    hi = x.astype(jnp.bfloat16)
    lo = (x - hi.astype(jnp.float32)).astype(jnp.bfloat16)
    return hi, lo


def split3(x):
    hi, mid = split2(x)
    rest = x - hi.astype(jnp.float32) - mid.astype(jnp.float32)
    return hi, mid, rest.astype(jnp.bfloat16)


def cubic(distance):
    inner = 2.0 / 3.0 - distance * distance + 0.5 * distance * distance * distance
    remote = 2.0 - distance
    outer = remote * remote * remote * (1.0 / 6.0)
    return jnp.where(distance < 1.0, inner, jnp.where(distance < 2.0, outer, 0.0))


def mask_kernel(mask_hbm, rows_hbm, out_ref, mask, rows, sems):
    stored, band = rows.shape[:2]
    fetch = pltpu.make_async_copy(mask_hbm, mask, sems.at[stored])
    copies = [
        pltpu.make_async_copy(rows_hbm.at[t], rows.at[t], sems.at[t]) for t in range(stored)
    ]
    fetch.start()
    for copy in copies:
        copy.start()
    fetch.wait()
    factors = mask[...].astype(jnp.float32)
    for t, copy in enumerate(copies):
        copy.wait()
        for k in range(band):
            factor = jnp.broadcast_to(factors[t : t + 1, k : k + 1], rows.shape[2:])
            out_ref[t, k] = rows[t, k] * factor.astype(jnp.bfloat16)


def field_kernel(
    after_hbm, near_ref, table_hbm, radius_hbm, harm_hbm,
    g_ref, hpad_ref, atom_ref, table_ref, radius_ref, harm_ref, sems,
):
    batches, near, comps, points = harm_ref.shape
    knots = table_ref.shape[0]
    moves = ((table_hbm, table_ref), (radius_hbm, radius_ref), (harm_hbm, harm_ref))
    copies = [pltpu.make_async_copy(a, b, sems.at[n]) for n, (a, b) in enumerate(moves)]
    for copy in copies:
        copy.start()
    lane = lax.broadcasted_iota(jnp.int32, atom_ref.shape, 1)
    atom = jnp.full(atom_ref.shape, -1, jnp.int32)
    for b in range(batches):
        for i in range(near):
            atom = jnp.where(lane == b * SLOT + i, near_ref[i, b], atom)
    atom_ref[...] = atom
    hpad_ref[...] = jnp.zeros(hpad_ref.shape, hpad_ref.dtype)
    knot = lax.broadcasted_iota(jnp.int32, (knots, points), 0).astype(jnp.float32)
    for copy in copies:
        copy.wait()
    r_hi, r_lo = split2(table_ref[...].T)
    coeffs = jnp.concatenate([r_hi, r_hi, r_lo], axis=1)

    def body(b, carry):
        rows = radius_ref[b]
        for i in range(near):
            spline = cubic(jnp.abs(rows[i : i + 1, :] - knot))
            s_hi, s_lo = split2(spline)
            radial = dot(coeffs, jnp.concatenate([s_hi, s_lo, s_hi], axis=0))
            h = harm_ref[b, i]
            g_ref[b * near + i] = radial * h.astype(jnp.float32)
            hpad_ref[b * near + i, 0:comps, :] = h
        return carry

    lax.fori_loop(0, batches, body, 0)


def turn_kernel(after_hbm, basis_hbm, part_hbm, phit_ref, part_ref, basis, sems):
    batches, near_blocks = basis.shape[:2]
    halves = [pl.ds(0, batches // 2), pl.ds(batches // 2, batches - batches // 2)]
    copies = [
        pltpu.make_async_copy(basis_hbm.at[half], basis.at[half], sems.at[n])
        for n, half in enumerate(halves)
    ]
    copies.append(pltpu.make_async_copy(part_hbm, part_ref, sems.at[2]))
    for copy in copies:
        copy.start()

    def turn(b, carry):
        for j in range(near_blocks):
            phit_ref[b, j] = basis[b, j].T
        return carry

    copies[0].wait()
    lax.fori_loop(0, batches // 2, turn, 0)
    copies[1].wait()
    lax.fori_loop(batches // 2, batches, turn, 0)
    copies[2].wait()


def density_kernel(start_ref, offset_ref, size_ref, atom_ref, phit_ref, part_ref, hpad_ref, *refs):
    dens_ref, terms_ref, window_ref, w_ref = refs[-4:]
    pieces = refs[:-4]
    owners = window_ref.shape[0]
    batches, near_blocks, width, points = phit_ref.shape
    near = part_ref.shape[1]
    if len(pieces) == owners:
        me = lax.axis_index("dev")
        odd = lax.rem(me, 2) == 1
        held = [
            (piece, lax.bitwise_xor(me, jnp.where(odd, b, a)))
            for piece, a, b in zip(pieces, EVEN_OWNERS, ODD_OWNERS)
        ]
    else:
        held = [(pieces[0].at[owner], owner) for owner in range(owners)]
    stored = held[0][0].shape[0]
    start = start_ref[0]
    for piece, owner in held:
        ahead = lax.rem(owner - start + stored * owners, owners)
        row = lax.rem(start + ahead, stored * owners) // owners
        window_ref[ahead] = piece[row]
    w_ref[...] = jnp.zeros(w_ref.shape, w_ref.dtype)
    lane = lax.broadcasted_iota(jnp.int32, (1, points), 1)
    zero = jnp.zeros((width, width), jnp.bfloat16)

    def body(b, carry):
        first = offset_ref[0, b]
        total = jnp.zeros((width, points), jnp.float32)
        for q, js in ((0, (0, 1, 2)), (2, (0, 1, 2, 3))):
            left = []
            for j in js:
                pair = [
                    window_ref[first + j, f - j + 1] if 0 <= f - j + 1 < 4 else zero
                    for f in (q, q + 1)
                ]
                left.append(jnp.concatenate(pair, axis=1))
            right = jnp.concatenate([phit_ref[b, q], phit_ref[b, q + 1]], axis=0)
            mixed = dot(jnp.concatenate(left, axis=0), right)
            for at, j in enumerate(js):
                part = mixed[at * width : (at + 1) * width]
                total = total + part * phit_ref[b, j].astype(jnp.float32)
        summed = jnp.sum(total, axis=0, keepdims=True)
        alive = lane < size_ref[0, b]
        row = jnp.where(alive, summed, 0.0)
        dens_ref[pl.ds(b, 1), :] = row
        w_ref[b, 0:near, :] = part_ref[b] * row
        return carry

    lax.fori_loop(0, batches, body, 0, unroll=4)
    weights = w_ref[...].reshape(LANES, points)
    columns = jnp.concatenate(split2(weights), axis=0)
    slot = lax.broadcasted_iota(jnp.int32, (1, 2 * LANES), 1) % LANES
    cross = dot(hpad_ref[...].reshape(batches * near * ROWS, points), columns, NT)
    terms = jnp.zeros((ROWS, 2 * LANES), jnp.float32)
    for b in range(batches):
        for i in range(near):
            at = (b * near + i) * ROWS
            terms = terms + jnp.where(slot == b * SLOT + i, cross[at : at + ROWS], 0.0)
    result = terms[:, :LANES] + terms[:, LANES:]
    row_id = lax.broadcasted_iota(jnp.int32, (ROWS, LANES), 0)
    comps = ROWS - 7
    terms_ref[...] = jnp.where(row_id == comps, atom_ref[...].astype(jnp.float32), result)


def scatter_kernel(comps, atoms, flip, *refs):
    own, near_a, near_b, far = refs[-4:]
    pieces = [group.at[m] for group in refs[:-4] for m in range(group.shape[0])]
    row_id = lax.broadcasted_iota(jnp.int32, (3 * atoms, LANES), 0)
    total = jnp.zeros((3 * ROWS, 3 * atoms), jnp.float32)
    for m in range(0, len(pieces), 2):
        left, right = [], []
        for values in (pieces[m][...], pieces[m + 1][...]):
            chosen = values[comps : comps + 1, :].astype(jnp.int32)
            right.append((row_id == chosen).astype(jnp.float32).astype(jnp.bfloat16))
            left.append(jnp.concatenate(split3(values), axis=0))
        total = total + dot(jnp.concatenate(left, axis=1), jnp.concatenate(right, axis=1), NT)
    sums = total[:ROWS] + total[ROWS : 2 * ROWS] + total[2 * ROWS :]
    own[...] = sums
    ahead, back = sums[:, atoms:], sums[:, : 2 * atoms]
    if flip:
        odd = lax.rem(lax.axis_index("region"), 2) == 1
        near_a[...] = jnp.where(odd, back, ahead)
        near_b[...] = jnp.where(odd, ahead, back)
    else:
        near_a[...] = ahead
        near_b[...] = back
    far[:, :atoms] = sums[:, :atoms]
    far[:, atoms:] = sums[:, 2 * atoms :]


def moments_kernel(atoms, flip, own_ref, near_a_ref, near_b_ref, fa_ref, fb_ref, out_ref):
    own = own_ref[...]
    near_a, near_b = near_a_ref[...], near_b_ref[...]
    if flip:
        odd = lax.rem(lax.axis_index("region"), 2) == 1
        low = jnp.where(odd, near_a, near_b)
        high = jnp.where(odd, near_b, near_a)
    else:
        low, high = near_a, near_b
    out_ref[:, :atoms] = fa_ref[:, atoms:] + low[:, :atoms] + own[:, :atoms]
    out_ref[:, atoms : 2 * atoms] = low[:, atoms:] + own[:, atoms : 2 * atoms] + high[:, :atoms]
    out_ref[:, 2 * atoms :] = own[:, 2 * atoms :] + high[:, atoms:] + fb_ref[:, :atoms]


def potential_kernel(
    comps, atoms, size_ref, moments_ref, other_ref, atom_ref, g_ref, mom_ref, pot_ref
):
    batches, points = pot_ref.shape
    near = g_ref.shape[0] // batches
    odd = lax.rem(lax.axis_index("dev"), 2) == 1
    moments = jnp.where(odd, moments_ref[...], other_ref[...])
    parts = jnp.concatenate(split3(moments), axis=0)

    mine = mom_ref.shape[0]
    want = lax.broadcasted_iota(jnp.int32, (mine, atoms), 0) + lax.axis_index("dev") * mine
    keep = want == lax.broadcasted_iota(jnp.int32, (mine, atoms), 1)
    keep = keep.astype(jnp.float32).astype(jnp.bfloat16)
    taken = dot(keep, parts[:, atoms : 2 * atoms], NT)
    taken = taken[:, :ROWS] + taken[:, ROWS : 2 * ROWS] + taken[:, 2 * ROWS :]
    mom_ref[...] = taken[:, :comps]

    row_id = lax.broadcasted_iota(jnp.int32, (3 * atoms, LANES), 0)
    pick = (row_id == atom_ref[...]).astype(jnp.float32).astype(jnp.bfloat16)
    got = dot(parts, pick)
    chosen = got[:ROWS] + got[ROWS : 2 * ROWS] + got[2 * ROWS :]
    chosen = chosen[:comps]
    lane = lax.broadcasted_iota(jnp.int32, (1, points), 1)
    for b in range(batches):
        total = jnp.zeros((comps, points), jnp.float32)
        for i in range(near):
            column = chosen[:, b * SLOT + i : b * SLOT + i + 1]
            total = total + column * g_ref[b * near + i]
        row = jnp.sum(total, axis=0, keepdims=True)
        pot_ref[b : b + 1, :] = jnp.where(lane < size_ref[0, b], row, 0.0)


def held_in_hbm(*values):
    return [pltpu.with_memory_space_constraint(value, pltpu.HBM) for value in values]


def crossed(value, axis, m):
    return lax.ppermute(value, axis, [(i, i ^ m) for i in range(lax.axis_size(axis))])


def turned(value, even, odd):
    count = lax.axis_size("dev")
    return lax.ppermute(value, "dev", [(i, i ^ (odd if i % 2 else even)) for i in range(count)])


def among_odd(value, m):
    count = lax.axis_size("dev")
    return lax.ppermute(value, "dev", [(i, i ^ m if i % 2 else i) for i in range(count)])


def regions_of_odd(value, m):
    count, regions = lax.axis_size("dev"), lax.axis_size("region")
    pairs = [
        (r * count + i, (r ^ m if i % 2 else r) * count + i)
        for r in range(regions)
        for i in range(count)
    ]
    return lax.ppermute(value, ("region", "dev"), pairs)


def shifted(value, axis, step):
    count = lax.axis_size(axis)
    return lax.ppermute(value, axis, [(i, (i + step) % count) for i in range(count)])


def per_device(
    basis_values,
    density_rows,
    block_mask,
    window_start,
    batch_offsets,
    batch_sizes,
    atom_near,
    harmonics,
    partition,
    radius,
    radial_table,
):
    dev_count = lax.axis_size("dev")
    region_count = lax.axis_size("region")
    blocks_dev, band, width = density_rows.shape[:3]
    batches, near, comps, points = harmonics.shape
    near_blocks = basis_values.shape[1]
    mine = 16
    atoms = mine * dev_count
    f32, bf16 = jnp.float32, jnp.bfloat16

    masked = pl.pallas_call(
        mask_kernel,
        out_shape=pltpu.VMEM(density_rows.shape, bf16),
        in_specs=[HBM, HBM],
        out_specs=VMEM,
        scratch_shapes=[
            pltpu.VMEM(block_mask.shape, jnp.int32),
            pltpu.VMEM(density_rows.shape, bf16),
            pltpu.SemaphoreType.DMA((blocks_dev + 1,)),
        ],
        compiler_params=PARAMS,
        name="mask",
    )(*held_in_hbm(block_mask, density_rows))

    g, hpad, atom_rows = pl.pallas_call(
        field_kernel,
        out_shape=(
            pltpu.VMEM((batches * near, comps, points), f32),
            pltpu.VMEM((batches * near, ROWS, points), bf16),
            pltpu.VMEM((1, LANES), jnp.int32),
        ),
        in_specs=[HBM, SMEM] + [HBM] * 3,
        out_specs=(VMEM,) * 3,
        scratch_shapes=[
            pltpu.VMEM(radial_table.shape[::-1], f32),
            pltpu.VMEM(radius.shape, f32),
            pltpu.VMEM(harmonics.shape, bf16),
            pltpu.SemaphoreType.DMA((3,)),
        ],
        compiler_params=WIDE,
        cost_estimate=pl.CostEstimate(flops=2_000_000_000, bytes_accessed=8_000_000, transcendentals=0),
        name="field",
    )(masked, atom_near.T, *held_in_hbm(radial_table.T, radius, harmonics))

    def turned_basis(after):
        return pl.pallas_call(
            turn_kernel,
            out_shape=(
                pltpu.VMEM((batches, near_blocks, width, points), bf16),
                pltpu.VMEM(partition.shape, f32),
            ),
            in_specs=[HBM] * 3,
            out_specs=(VMEM,) * 2,
            scratch_shapes=[pltpu.VMEM(basis_values.shape, bf16), pltpu.SemaphoreType.DMA((3,))],
            compiler_params=WIDE,
            cost_estimate=pl.CostEstimate(
                flops=2_000_000_000, bytes_accessed=8_000_000, transcendentals=0
            ),
            name="turn",
        )(after, *held_in_hbm(basis_values, partition))

    phit, weights = turned_basis(g)
    if dev_count == 8:
        first = turned(masked, 4, 2)
        second = turned(masked, 2, 4)
        first, phit = lax.optimization_barrier((first, phit))
        third = turned(first, 2, 4)
        sent = (masked, first, second, third)
        pieces = [piece for value in sent for piece in (value, crossed(value, "dev", 1))]
    else:
        pieces = [lax.all_gather(masked, "dev", axis=0)]

    density, terms = pl.pallas_call(
        density_kernel,
        out_shape=(
            jax.ShapeDtypeStruct((batches, points), f32),
            jax.ShapeDtypeStruct((ROWS, LANES), f32),
        ),
        in_specs=[SMEM] * 3 + [VMEM] * (4 + len(pieces)),
        out_specs=(VMEM, VMEM),
        scratch_shapes=[
            pltpu.VMEM((dev_count, band, width, width), bf16),
            pltpu.VMEM((LANES // SLOT, SLOT, points), f32),
        ],
        compiler_params=PARAMS,
        cost_estimate=pl.CostEstimate(flops=2_000_000_000, bytes_accessed=6_000_000, transcendentals=0),
        name="density",
    )(
        window_start, batch_offsets, batch_sizes, atom_rows, phit, weights, hpad,
        *pieces,
    )

    small = dev_count == 8 and region_count == 4
    if small:
        both = jnp.stack([terms, crossed(terms, "dev", 1)])
        groups = [both] + [among_odd(both, m) for m in (6, 2, 4)]
    else:
        groups = [lax.all_gather(terms, "dev", axis=0)]
    own, near_a, near_b, far = pl.pallas_call(
        functools.partial(scatter_kernel, comps, atoms, small),
        out_shape=tuple(jax.ShapeDtypeStruct((ROWS, n * atoms), f32) for n in (3, 2, 2, 2)),
        in_specs=[VMEM] * len(groups),
        out_specs=(VMEM,) * 4,
        compiler_params=PARAMS,
        name="scatter",
    )(*groups)
    if small:
        far_a = far_b = regions_of_odd(far, 2)
        near_a = regions_of_odd(near_a, 1)
        near_b = regions_of_odd(near_b, 3)
    else:
        far_a = shifted(far, "region", 2)
        far_b = shifted(far, "region", -2)
        near_a = shifted(near_a, "region", 1)
        near_b = shifted(near_b, "region", -1)
    moments = pl.pallas_call(
        functools.partial(moments_kernel, atoms, small),
        out_shape=jax.ShapeDtypeStruct((ROWS, 3 * atoms), f32),
        in_specs=[VMEM] * 5,
        out_specs=VMEM,
        compiler_params=PARAMS,
        name="moments",
    )(own, near_a, near_b, far_a, far_b)
    other = crossed(moments, "dev", 1) if small else moments

    moments, potential = pl.pallas_call(
        functools.partial(potential_kernel, comps, atoms),
        out_shape=(
            jax.ShapeDtypeStruct((mine, comps), f32),
            jax.ShapeDtypeStruct((batches, points), f32),
        ),
        in_specs=[SMEM] + [VMEM] * 4,
        out_specs=(VMEM, VMEM),
        compiler_params=PARAMS,
        name="potential",
    )(batch_sizes, moments, other, atom_rows, g)
    return (density, moments.T, potential)


def solution(mesh):
    both = ("region", "dev")
    placed = (
        P(both, None, None, None),
        P(both, None, None, None),
        P(both, None),
        P(both),
        P(both, None),
        P(both, None),
        P(both, None),
        P(both, None, None, None),
        P(both, None, None),
        P(both, None, None),
        P(),
    )
    return jax.shard_map(
        per_device,
        mesh=mesh,
        in_specs=placed,
        out_specs=(P(both, None), P(None, both), P(both, None)),
        check_vma=False,
    )
```

```python
import functools
import jax
import jax.numpy as jnp
from jax import lax
from jax.experimental import pallas as pl
from jax.experimental.pallas import tpu as pltpu
from jax.sharding import PartitionSpec as P

EVEN_OWNERS = (0, 1, 4, 3, 2, 5, 6, 7)
ODD_OWNERS = (0, 1, 2, 5, 4, 3, 6, 7)
PIECE_ROWS = (None, None, None, None, 0, 1, 0, 1)
LANES = 128
ROWS = 32
SLOT = 8
NT = (((1,), (1,)), ((), ()))
NN = (((1,), (0,)), ((), ()))
VMEM = pl.BlockSpec(memory_space=pltpu.VMEM)
SMEM = pl.BlockSpec(memory_space=pltpu.SMEM)
HBM = pl.BlockSpec(memory_space=pltpu.HBM)
WIDE = pltpu.CompilerParams(vmem_limit_bytes=16 * 1024 * 1024)
PARAMS = pltpu.CompilerParams(vmem_limit_bytes=16 * 1024 * 1024)


def dot(a, b, dims=NN):
    return lax.dot_general(a, b, dims, preferred_element_type=jnp.float32)


def split2(x):
    hi = x.astype(jnp.bfloat16)
    lo = (x - hi.astype(jnp.float32)).astype(jnp.bfloat16)
    return hi, lo


def split3(x):
    hi, mid = split2(x)
    rest = x - hi.astype(jnp.float32) - mid.astype(jnp.float32)
    return hi, mid, rest.astype(jnp.bfloat16)


def cubic(distance):
    inner = 2.0 / 3.0 - distance * distance + 0.5 * distance * distance * distance
    remote = 2.0 - distance
    outer = remote * remote * remote * (1.0 / 6.0)
    return jnp.where(distance < 1.0, inner, jnp.where(distance < 2.0, outer, 0.0))


def chosen_row(owner, start, owners, stored):
    ahead = lax.rem(owner - start + stored * owners, owners)
    return ahead, lax.rem(start + ahead, stored * owners) // owners


def select_kernel(even, odd, owners, starts_ref, rows_ref, out_ref):
    me = lax.axis_index("dev")
    owner = lax.bitwise_xor(me, jnp.where(lax.rem(me, 2) == 1, odd, even))
    for n in range(out_ref.shape[0]):
        row = chosen_row(owner, starts_ref[n], owners, rows_ref.shape[0])[1]
        out_ref[n] = rows_ref[row]


def mask_kernel(mask_hbm, rows_hbm, out_ref, mask, rows, sems):
    stored, band = rows.shape[:2]
    fetch = pltpu.make_async_copy(mask_hbm, mask, sems.at[stored])
    copies = [
        pltpu.make_async_copy(rows_hbm.at[t], rows.at[t], sems.at[t]) for t in range(stored)
    ]
    fetch.start()
    for copy in copies:
        copy.start()
    fetch.wait()
    factors = mask[...].astype(jnp.float32)
    for t, copy in enumerate(copies):
        copy.wait()
        for k in range(band):
            factor = jnp.broadcast_to(factors[t : t + 1, k : k + 1], rows.shape[2:])
            out_ref[t, k] = rows[t, k] * factor.astype(jnp.bfloat16)


def field_kernel(
    begin, after_hbm, near_ref, table_hbm, radius_hbm, harm_hbm,
    g_ref, hpad_ref, atom_ref, table_ref, radius_ref, harm_ref, sems,
):
    batches, near, comps, points = harm_ref.shape
    knots = table_ref.shape[0]
    span = pl.ds(begin, batches)
    moves = (
        (table_hbm, table_ref), (radius_hbm.at[span], radius_ref), (harm_hbm.at[span], harm_ref)
    )
    copies = [pltpu.make_async_copy(a, b, sems.at[n]) for n, (a, b) in enumerate(moves)]
    for copy in copies:
        copy.start()
    lane = lax.broadcasted_iota(jnp.int32, atom_ref.shape, 1)
    atom = jnp.full(atom_ref.shape, -1, jnp.int32)
    for b in range(near_ref.shape[1]):
        for i in range(near):
            atom = jnp.where(lane == b * SLOT + i, near_ref[i, b], atom)
    atom_ref[...] = atom
    for n in range(batches * near):
        hpad_ref[n, ROWS // 2 :, :] = jnp.zeros((ROWS // 2, points), jnp.bfloat16)
    knot = lax.broadcasted_iota(jnp.int32, (knots, points), 0).astype(jnp.float32)
    for copy in copies:
        copy.wait()
    r_hi, r_lo = split2(table_ref[...].T)
    coeffs = jnp.concatenate([r_hi, r_hi, r_lo], axis=1)

    def body(b, carry):
        rows = radius_ref[b]
        for i in range(near):
            spline = cubic(jnp.abs(rows[i : i + 1, :] - knot))
            s_hi, s_lo = split2(spline)
            radial = dot(coeffs, jnp.concatenate([s_hi, s_lo, s_hi], axis=0))
            h = harm_ref[b, i]
            g_ref[b * near + i] = radial * h.astype(jnp.float32)
            hpad_ref[b * near + i, 0:comps, :] = h
        return carry

    lax.fori_loop(0, batches, body, 0, unroll=2)


def turn_kernel(after_hbm, basis_hbm, part_hbm, phit_ref, part_ref, basis, sems):
    batches, near_blocks = basis.shape[:2]
    halves = [pl.ds(0, batches // 2), pl.ds(batches // 2, batches - batches // 2)]
    copies = [
        pltpu.make_async_copy(basis_hbm.at[half], basis.at[half], sems.at[n])
        for n, half in enumerate(halves)
    ]
    copies.append(pltpu.make_async_copy(part_hbm, part_ref, sems.at[2]))
    for copy in copies:
        copy.start()

    def turn(b, carry):
        for j in range(near_blocks):
            phit_ref[b, j] = basis[b, j].T
        return carry

    copies[0].wait()
    lax.fori_loop(0, batches // 2, turn, 0)
    copies[1].wait()
    lax.fori_loop(batches // 2, batches, turn, 0)
    copies[2].wait()


def density_kernel(
    start_ref, offset_ref, size_ref, atom_ref, phit_ref, part_ref, low_ref, high_ref, *refs
):
    dens_ref, terms_ref, window_ref, w_ref = refs[-4:]
    pieces = refs[:-4]
    owners = window_ref.shape[0]
    batches, near_blocks, width, points = phit_ref.shape
    near = part_ref.shape[1]
    if len(pieces) == owners:
        me = lax.axis_index("dev")
        odd = lax.rem(me, 2) == 1
        held = [
            (piece, lax.bitwise_xor(me, jnp.where(odd, b, a)), at)
            for piece, a, b, at in zip(pieces, EVEN_OWNERS, ODD_OWNERS, PIECE_ROWS)
        ]
    else:
        held = [(pieces[0].at[owner], owner, None) for owner in range(owners)]
    stored = held[0][0].shape[0]
    for piece, owner, at in held:
        ahead, row = chosen_row(owner, start_ref[0], owners, stored)
        window_ref[ahead] = piece[row if at is None else at]
    w_ref[...] = jnp.zeros(w_ref.shape, w_ref.dtype)
    lane = lax.broadcasted_iota(jnp.int32, (1, points), 1)
    zero = jnp.zeros((width, width), jnp.bfloat16)

    def body(b, carry):
        first = offset_ref[0, b]
        total = jnp.zeros((width, points), jnp.float32)
        for q, js in ((0, (0, 1, 2)), (2, (0, 1, 2, 3))):
            left = []
            for j in js:
                pair = [
                    window_ref[first + j, f - j + 1] if 0 <= f - j + 1 < 4 else zero
                    for f in (q, q + 1)
                ]
                left.append(jnp.concatenate(pair, axis=1))
            right = jnp.concatenate([phit_ref[b, q], phit_ref[b, q + 1]], axis=0)
            mixed = dot(jnp.concatenate(left, axis=0), right)
            for at, j in enumerate(js):
                part = mixed[at * width : (at + 1) * width]
                total = total + part * phit_ref[b, j].astype(jnp.float32)
        summed = jnp.sum(total, axis=0, keepdims=True)
        alive = lane < size_ref[0, b]
        row = jnp.where(alive, summed, 0.0)
        dens_ref[pl.ds(b, 1), :] = row
        w_ref[b, 0:near, :] = part_ref[b] * row
        return carry

    lax.fori_loop(0, batches, body, 0, unroll=4)
    weights = w_ref[...].reshape(LANES, points)
    columns = jnp.concatenate(split2(weights), axis=0)
    slot = lax.broadcasted_iota(jnp.int32, (1, 2 * LANES), 1) % LANES
    terms = jnp.zeros((ROWS, 2 * LANES), jnp.float32)
    begin = 0
    for ref in (low_ref, high_ref):
        count = ref.shape[0]
        cross = dot(ref[...].reshape(count * ROWS, points), columns, NT)
        for n in range(count):
            b, i = divmod(begin + n, near)
            here = cross[n * ROWS : (n + 1) * ROWS]
            terms = terms + jnp.where(slot == b * SLOT + i, here, 0.0)
        begin = begin + count
    result = terms[:, :LANES] + terms[:, LANES:]
    row_id = lax.broadcasted_iota(jnp.int32, (ROWS, LANES), 0)
    comps = ROWS - 7
    terms_ref[...] = jnp.where(row_id == comps, atom_ref[...].astype(jnp.float32), result)


def scatter_kernel(comps, atoms, flip, *refs):
    own, near_a, near_b, far = refs[-4:]
    pieces = [group.at[m] for group in refs[:-4] for m in range(group.shape[0])]
    row_id = lax.broadcasted_iota(jnp.int32, (3 * atoms, LANES), 0)
    total = jnp.zeros((3 * ROWS, 3 * atoms), jnp.float32)
    for m in range(0, len(pieces), 2):
        left, right = [], []
        for values in (pieces[m][...], pieces[m + 1][...]):
            chosen = values[comps : comps + 1, :].astype(jnp.int32)
            right.append((row_id == chosen).astype(jnp.float32).astype(jnp.bfloat16))
            left.append(jnp.concatenate(split3(values), axis=0))
        total = total + dot(jnp.concatenate(left, axis=1), jnp.concatenate(right, axis=1), NT)
    sums = total[:ROWS] + total[ROWS : 2 * ROWS] + total[2 * ROWS :]
    own[...] = sums
    ahead, back = sums[:, atoms:], sums[:, : 2 * atoms]
    if flip:
        odd = lax.rem(lax.axis_index("region"), 2) == 1
        near_a[...] = jnp.where(odd, back, ahead)
        near_b[...] = jnp.where(odd, ahead, back)
    else:
        near_a[...] = ahead
        near_b[...] = back
    far[:, :atoms] = sums[:, :atoms]
    far[:, atoms:] = sums[:, 2 * atoms :]


def potential_kernel(
    comps, atoms, flip, size_ref, own_ref, near_a_ref, near_b_ref, fa_ref, fb_ref, atom_ref,
    low_ref, high_ref, mom_ref, pot_ref,
):
    batches, points = pot_ref.shape
    near = 2 * low_ref.shape[0] // batches
    fields = [ref.at[n] for ref in (low_ref, high_ref) for n in range(ref.shape[0])]
    own = own_ref[...]
    near_a, near_b = near_a_ref[...], near_b_ref[...]
    if flip:
        odd = lax.rem(lax.axis_index("region"), 2) == 1
        low = jnp.where(odd, near_a, near_b)
        high = jnp.where(odd, near_b, near_a)
    else:
        low, high = near_a, near_b
    before = fa_ref[:, atoms:] + low[:, :atoms] + own[:, :atoms]
    here = low[:, atoms:] + own[:, atoms : 2 * atoms] + high[:, :atoms]
    after = own[:, 2 * atoms :] + high[:, atoms:] + fb_ref[:, :atoms]

    mine = mom_ref.shape[0]
    want = lax.broadcasted_iota(jnp.int32, (mine, atoms), 0) + lax.axis_index("dev") * mine
    keep = want == lax.broadcasted_iota(jnp.int32, (mine, atoms), 1)
    keep = keep.astype(jnp.float32).astype(jnp.bfloat16)
    taken = dot(keep, jnp.concatenate(split3(here), axis=0), NT)
    taken = taken[:, :ROWS] + taken[:, ROWS : 2 * ROWS] + taken[:, 2 * ROWS :]
    mom_ref[...] = taken[:, :comps]

    moments = jnp.concatenate([before, here, after], axis=1)
    row_id = lax.broadcasted_iota(jnp.int32, (3 * atoms, LANES), 0)
    pick = (row_id == atom_ref[...]).astype(jnp.float32).astype(jnp.bfloat16)
    got = dot(jnp.concatenate(split3(moments), axis=0), pick)
    chosen = got[:ROWS] + got[ROWS : 2 * ROWS] + got[2 * ROWS :]
    chosen = chosen[:comps]
    lane = lax.broadcasted_iota(jnp.int32, (1, points), 1)
    for b in range(batches):
        total = jnp.zeros((comps, points), jnp.float32)
        for i in range(near):
            column = chosen[:, b * SLOT + i : b * SLOT + i + 1]
            total = total + column * fields[b * near + i][...]
        row = jnp.sum(total, axis=0, keepdims=True)
        pot_ref[b : b + 1, :] = jnp.where(lane < size_ref[0, b], row, 0.0)


def held_in_hbm(*values):
    return [pltpu.with_memory_space_constraint(value, pltpu.HBM) for value in values]


def crossed(value, axis, m):
    return lax.ppermute(value, axis, [(i, i ^ m) for i in range(lax.axis_size(axis))])


def turned(value, even, odd):
    count = lax.axis_size("dev")
    return lax.ppermute(value, "dev", [(i, i ^ (odd if i % 2 else even)) for i in range(count)])


def shifted(value, axis, step):
    count = lax.axis_size(axis)
    return lax.ppermute(value, axis, [(i, (i + step) % count) for i in range(count)])


def per_device(
    basis_values,
    density_rows,
    block_mask,
    window_start,
    batch_offsets,
    batch_sizes,
    atom_near,
    harmonics,
    partition,
    radius,
    radial_table,
):
    dev_count = lax.axis_size("dev")
    region_count = lax.axis_size("region")
    blocks_dev, band, width = density_rows.shape[:3]
    batches, near, comps, points = harmonics.shape
    near_blocks = basis_values.shape[1]
    mine = 16
    atoms = mine * dev_count
    f32, bf16 = jnp.float32, jnp.bfloat16

    masked = pl.pallas_call(
        mask_kernel,
        out_shape=pltpu.VMEM(density_rows.shape, bf16),
        in_specs=[HBM, HBM],
        out_specs=VMEM,
        scratch_shapes=[
            pltpu.VMEM(block_mask.shape, jnp.int32),
            pltpu.VMEM(density_rows.shape, bf16),
            pltpu.SemaphoreType.DMA((blocks_dev + 1,)),
        ],
        compiler_params=PARAMS,
        name="mask",
    )(*held_in_hbm(block_mask, density_rows))

    half = batches // 2

    def field(begin, after):
        return pl.pallas_call(
            functools.partial(field_kernel, begin),
            out_shape=(
                pltpu.VMEM((half * near, comps, points), f32),
                pltpu.VMEM((half * near, ROWS, points), bf16),
                pltpu.VMEM((1, LANES), jnp.int32),
            ),
            in_specs=[HBM, SMEM] + [HBM] * 3,
            out_specs=(VMEM,) * 3,
            scratch_shapes=[
                pltpu.VMEM(radial_table.shape[::-1], f32),
                pltpu.VMEM((half,) + radius.shape[1:], f32),
                pltpu.VMEM((half,) + harmonics.shape[1:], bf16),
                pltpu.SemaphoreType.DMA((3,)),
            ],
            compiler_params=WIDE,
            cost_estimate=pl.CostEstimate(
                flops=2_000_000_000, bytes_accessed=8_000_000, transcendentals=0
            ),
            name="field",
        )(after, atom_near.T, *held_in_hbm(radial_table.T, radius, harmonics))

    def turned_basis(after):
        return pl.pallas_call(
            turn_kernel,
            out_shape=(
                pltpu.VMEM((batches, near_blocks, width, points), bf16),
                pltpu.VMEM(partition.shape, f32),
            ),
            in_specs=[HBM] * 3,
            out_specs=(VMEM,) * 2,
            scratch_shapes=[pltpu.VMEM(basis_values.shape, bf16), pltpu.SemaphoreType.DMA((3,))],
            compiler_params=WIDE,
            cost_estimate=pl.CostEstimate(
                flops=2_000_000_000, bytes_accessed=8_000_000, transcendentals=0
            ),
            name="turn",
        )(after, *held_in_hbm(basis_values, partition))

    def selected(even, odd, starts, rows):
        return pl.pallas_call(
            functools.partial(select_kernel, even, odd, dev_count),
            out_shape=pltpu.VMEM((2,) + density_rows.shape[1:], bf16),
            in_specs=[SMEM, VMEM],
            out_specs=VMEM,
            compiler_params=PARAMS,
            name="select",
        )(starts, rows)

    if dev_count == 8:
        beside = crossed(window_start, "dev", 1)
        beside, _ = lax.optimization_barrier((beside, masked))
        first = turned(masked, 4, 2)
        pair = jnp.concatenate([window_start, beside])
        starts = turned(pair, 2, 4)
        g_low, hpad_low, atom_rows = field(0, pair)
        starts, g_low = lax.optimization_barrier((starts, g_low))
        chosen = selected(0, 0, starts, masked)
        second = turned(chosen, 2, 4)
        g_high, hpad_high, _ = field(half, chosen)
        first, g_high = lax.optimization_barrier((first, g_high))
        chosen = selected(4, 2, starts, first)
        third = turned(chosen, 2, 4)
        phit, weights = turned_basis(chosen)
        second, phit = lax.optimization_barrier((second, phit))
        sent = (masked, first, second, third)
        pieces = [piece for value in sent for piece in (value, crossed(value, "dev", 1))]
    else:
        g_low, hpad_low, atom_rows = field(0, masked)
        g_high, hpad_high, _ = field(half, masked)
        phit, weights = turned_basis(masked)
        pieces = [lax.all_gather(masked, "dev", axis=0)]

    density, terms = pl.pallas_call(
        density_kernel,
        out_shape=(
            jax.ShapeDtypeStruct((batches, points), f32),
            jax.ShapeDtypeStruct((ROWS, LANES), f32),
        ),
        in_specs=[SMEM] * 3 + [VMEM] * (5 + len(pieces)),
        out_specs=(VMEM, VMEM),
        scratch_shapes=[
            pltpu.VMEM((dev_count, band, width, width), bf16),
            pltpu.VMEM((LANES // SLOT, SLOT, points), f32),
        ],
        compiler_params=PARAMS,
        cost_estimate=pl.CostEstimate(flops=2_000_000_000, bytes_accessed=6_000_000, transcendentals=0),
        name="density",
    )(
        window_start, batch_offsets, batch_sizes, atom_rows, phit, weights, hpad_low, hpad_high,
        *pieces,
    )

    if dev_count == 8:
        both = jnp.stack([terms, crossed(terms, "dev", 1)])
        groups = [both] + [crossed(both, "dev", m) for m in (2, 4, 6)]
    else:
        groups = [lax.all_gather(terms, "dev", axis=0)]
    flip = region_count == 4
    own, near_a, near_b, far = pl.pallas_call(
        functools.partial(scatter_kernel, comps, atoms, flip),
        out_shape=tuple(jax.ShapeDtypeStruct((ROWS, n * atoms), f32) for n in (3, 2, 2, 2)),
        in_specs=[VMEM] * len(groups),
        out_specs=(VMEM,) * 4,
        compiler_params=PARAMS,
        name="scatter",
    )(*groups)
    if flip:
        far_a = far_b = crossed(far, "region", 2)
        near_a = crossed(near_a, "region", 1)
        near_b = crossed(near_b, "region", 3)
    else:
        far_a = shifted(far, "region", 2)
        far_b = shifted(far, "region", -2)
        near_a = shifted(near_a, "region", 1)
        near_b = shifted(near_b, "region", -1)

    moments, potential = pl.pallas_call(
        functools.partial(potential_kernel, comps, atoms, flip),
        out_shape=(
            jax.ShapeDtypeStruct((mine, comps), f32),
            jax.ShapeDtypeStruct((batches, points), f32),
        ),
        in_specs=[SMEM] + [VMEM] * 8,
        out_specs=(VMEM, VMEM),
        compiler_params=PARAMS,
        name="potential",
    )(batch_sizes, own, near_a, near_b, far_a, far_b, atom_rows, g_low, g_high)
    return (density, moments.T, potential)


def solution(mesh):
    both = ("region", "dev")
    placed = (
        P(both, None, None, None),
        P(both, None, None, None),
        P(both, None),
        P(both),
        P(both, None),
        P(both, None),
        P(both, None),
        P(both, None, None, None),
        P(both, None, None),
        P(both, None, None),
        P(),
    )
    return jax.shard_map(
        per_device,
        mesh=mesh,
        in_specs=placed,
        out_specs=(P(both, None), P(None, both), P(both, None)),
        check_vma=False,
    )
```

```python
import functools
import jax
import jax.numpy as jnp
from jax import lax
from jax.experimental import pallas as pl
from jax.experimental.pallas import tpu as pltpu
from jax.sharding import PartitionSpec as P

EVEN_OWNERS = (0, 1, 4, 3, 2, 5, 6, 7)
ODD_OWNERS = (0, 1, 2, 5, 4, 3, 6, 7)
PIECE_ROWS = (None, None, None, None, 0, 1, 0, 1)
LANES = 128
ROWS = 32
SLOT = 8
NT = (((1,), (1,)), ((), ()))
NN = (((1,), (0,)), ((), ()))
VMEM = pl.BlockSpec(memory_space=pltpu.VMEM)
SMEM = pl.BlockSpec(memory_space=pltpu.SMEM)
HBM = pl.BlockSpec(memory_space=pltpu.HBM)
WIDE = pltpu.CompilerParams(vmem_limit_bytes=16 * 1024 * 1024)
PARAMS = pltpu.CompilerParams(vmem_limit_bytes=16 * 1024 * 1024)


def dot(a, b, dims=NN):
    return lax.dot_general(a, b, dims, preferred_element_type=jnp.float32)


def split2(x):
    hi = x.astype(jnp.bfloat16)
    lo = (x - hi.astype(jnp.float32)).astype(jnp.bfloat16)
    return hi, lo


def split3(x):
    hi, mid = split2(x)
    rest = x - hi.astype(jnp.float32) - mid.astype(jnp.float32)
    return hi, mid, rest.astype(jnp.bfloat16)


def cubic(distance):
    inner = 2.0 / 3.0 - distance * distance + 0.5 * distance * distance * distance
    remote = 2.0 - distance
    outer = remote * remote * remote * (1.0 / 6.0)
    return jnp.where(distance < 1.0, inner, jnp.where(distance < 2.0, outer, 0.0))


def chosen_row(owner, start, owners, stored):
    ahead = lax.rem(owner - start + stored * owners, owners)
    return ahead, lax.rem(start + ahead, stored * owners) // owners


def select_kernel(even, odd, owners, starts_ref, rows_ref, out_ref):
    me = lax.axis_index("dev")
    owner = lax.bitwise_xor(me, jnp.where(lax.rem(me, 2) == 1, odd, even))
    for n in range(out_ref.shape[0]):
        row = chosen_row(owner, starts_ref[n], owners, rows_ref.shape[0])[1]
        out_ref[n] = rows_ref[row]


def mask_kernel(mask_hbm, rows_hbm, out_ref, mask, rows, sems):
    stored, band = rows.shape[:2]
    fetch = pltpu.make_async_copy(mask_hbm, mask, sems.at[stored])
    copies = [
        pltpu.make_async_copy(rows_hbm.at[t], rows.at[t], sems.at[t]) for t in range(stored)
    ]
    fetch.start()
    for copy in copies:
        copy.start()
    fetch.wait()
    factors = mask[...].astype(jnp.float32)
    for t, copy in enumerate(copies):
        copy.wait()
        for k in range(band):
            factor = jnp.broadcast_to(factors[t : t + 1, k : k + 1], rows.shape[2:])
            out_ref[t, k] = rows[t, k] * factor.astype(jnp.bfloat16)


def field_kernel(
    begin, after_hbm, near_ref, table_hbm, radius_hbm, harm_hbm,
    g_ref, hpad_ref, atom_ref, table_ref, radius_ref, harm_ref, sems,
):
    batches, near, comps, points = harm_ref.shape
    knots = table_ref.shape[0]
    span = pl.ds(begin, batches)
    moves = (
        (table_hbm, table_ref), (radius_hbm.at[span], radius_ref), (harm_hbm.at[span], harm_ref)
    )
    copies = [pltpu.make_async_copy(a, b, sems.at[n]) for n, (a, b) in enumerate(moves)]
    for copy in copies:
        copy.start()
    lane = lax.broadcasted_iota(jnp.int32, atom_ref.shape, 1)
    atom = jnp.full(atom_ref.shape, -1, jnp.int32)
    for b in range(near_ref.shape[1]):
        for i in range(near):
            atom = jnp.where(lane == b * SLOT + i, near_ref[i, b], atom)
    atom_ref[...] = atom
    for n in range(batches * near):
        hpad_ref[n, ROWS // 2 :, :] = jnp.zeros((ROWS // 2, points), jnp.bfloat16)
    knot = lax.broadcasted_iota(jnp.int32, (knots, points), 0).astype(jnp.float32)
    for copy in copies:
        copy.wait()
    r_hi, r_lo = split2(table_ref[...].T)
    coeffs = jnp.concatenate([r_hi, r_hi, r_lo], axis=1)

    def body(b, carry):
        rows = radius_ref[b]
        for i in range(near):
            spline = cubic(jnp.abs(rows[i : i + 1, :] - knot))
            s_hi, s_lo = split2(spline)
            radial = dot(coeffs, jnp.concatenate([s_hi, s_lo, s_hi], axis=0))
            h = harm_ref[b, i]
            g_ref[b * near + i] = radial * h.astype(jnp.float32)
            hpad_ref[b * near + i, 0:comps, :] = h
        return carry

    lax.fori_loop(0, batches, body, 0, unroll=2)


def turn_kernel(after_hbm, basis_hbm, part_hbm, phit_ref, part_ref, basis, sems):
    batches, near_blocks = basis.shape[:2]
    halves = [pl.ds(0, batches // 2), pl.ds(batches // 2, batches - batches // 2)]
    copies = [
        pltpu.make_async_copy(basis_hbm.at[half], basis.at[half], sems.at[n])
        for n, half in enumerate(halves)
    ]
    copies.append(pltpu.make_async_copy(part_hbm, part_ref, sems.at[2]))
    for copy in copies:
        copy.start()

    def turn(b, carry):
        for j in range(near_blocks):
            phit_ref[b, j] = basis[b, j].T
        return carry

    copies[0].wait()
    lax.fori_loop(0, batches // 2, turn, 0)
    copies[1].wait()
    lax.fori_loop(batches // 2, batches, turn, 0)
    copies[2].wait()


def density_kernel(
    start_ref, offset_ref, size_ref, atom_ref, phit_ref, part_ref, low_ref, high_ref, *refs
):
    dens_ref, terms_ref, window_ref, w_ref = refs[-4:]
    pieces = refs[:-4]
    owners = window_ref.shape[0]
    batches, near_blocks, width, points = phit_ref.shape
    near = part_ref.shape[1]
    if len(pieces) == owners:
        me = lax.axis_index("dev")
        odd = lax.rem(me, 2) == 1
        held = [
            (piece, lax.bitwise_xor(me, jnp.where(odd, b, a)), at)
            for piece, a, b, at in zip(pieces, EVEN_OWNERS, ODD_OWNERS, PIECE_ROWS)
        ]
    else:
        held = [(pieces[0].at[owner], owner, None) for owner in range(owners)]
    stored = held[0][0].shape[0]
    for piece, owner, at in held:
        ahead, row = chosen_row(owner, start_ref[0], owners, stored)
        window_ref[ahead] = piece[row if at is None else at]
    w_ref[...] = jnp.zeros(w_ref.shape, w_ref.dtype)
    lane = lax.broadcasted_iota(jnp.int32, (1, points), 1)
    zero = jnp.zeros((width, width), jnp.bfloat16)

    def body(b, carry):
        first = offset_ref[0, b]
        total = jnp.zeros((width, points), jnp.float32)
        for q, js in ((0, (0, 1, 2)), (2, (0, 1, 2, 3))):
            left = []
            for j in js:
                pair = [
                    window_ref[first + j, f - j + 1] if 0 <= f - j + 1 < 4 else zero
                    for f in (q, q + 1)
                ]
                left.append(jnp.concatenate(pair, axis=1))
            right = jnp.concatenate([phit_ref[b, q], phit_ref[b, q + 1]], axis=0)
            mixed = dot(jnp.concatenate(left, axis=0), right)
            for at, j in enumerate(js):
                part = mixed[at * width : (at + 1) * width]
                total = total + part * phit_ref[b, j].astype(jnp.float32)
        summed = jnp.sum(total, axis=0, keepdims=True)
        alive = lane < size_ref[0, b]
        row = jnp.where(alive, summed, 0.0)
        dens_ref[pl.ds(b, 1), :] = row
        w_ref[b, 0:near, :] = part_ref[b] * row
        return carry

    lax.fori_loop(0, batches, body, 0, unroll=4)
    weights = w_ref[...].reshape(LANES, points)
    columns = jnp.concatenate(split2(weights), axis=0)
    slot = lax.broadcasted_iota(jnp.int32, (1, 2 * LANES), 1) % LANES
    terms = jnp.zeros((ROWS, 2 * LANES), jnp.float32)
    begin = 0
    for ref in (low_ref, high_ref):
        count = ref.shape[0]
        cross = dot(ref[...].reshape(count * ROWS, points), columns, NT)
        for n in range(count):
            b, i = divmod(begin + n, near)
            here = cross[n * ROWS : (n + 1) * ROWS]
            terms = terms + jnp.where(slot == b * SLOT + i, here, 0.0)
        begin = begin + count
    result = terms[:, :LANES] + terms[:, LANES:]
    row_id = lax.broadcasted_iota(jnp.int32, (ROWS, LANES), 0)
    comps = ROWS - 7
    terms_ref[...] = jnp.where(row_id == comps, atom_ref[...].astype(jnp.float32), result)


def scatter_kernel(comps, atoms, flip, groups, own, send):
    pieces = [groups.at[m, n] for m in range(groups.shape[0]) for n in range(groups.shape[1])]
    row_id = lax.broadcasted_iota(jnp.int32, (3 * atoms, LANES), 0)
    total = jnp.zeros((3 * ROWS, 3 * atoms), jnp.float32)
    for m in range(0, len(pieces), 2):
        left, right = [], []
        for values in (pieces[m][...], pieces[m + 1][...]):
            chosen = values[comps : comps + 1, :].astype(jnp.int32)
            right.append((row_id == chosen).astype(jnp.float32).astype(jnp.bfloat16))
            left.append(jnp.concatenate(split3(values), axis=0))
        total = total + dot(jnp.concatenate(left, axis=1), jnp.concatenate(right, axis=1), NT)
    sums = total[:ROWS] + total[ROWS : 2 * ROWS] + total[2 * ROWS :]
    own[...] = sums
    ahead, back = sums[:, atoms:], sums[:, : 2 * atoms]
    far = jnp.concatenate([sums[:, :atoms], sums[:, 2 * atoms :]], axis=1)
    if flip:
        for slot in range(send.shape[0]):
            away = lax.rem(slot - lax.axis_index("region") + 4, 4)
            send[slot] = jnp.where(away == 1, ahead, jnp.where(away == 3, back, far))
    else:
        send[0], send[1], send[2] = ahead, back, far


def potential_kernel(
    comps, atoms, flip, size_ref, own_ref, got_ref, atom_ref, low_ref, high_ref, mom_ref, pot_ref
):
    batches, points = pot_ref.shape
    near = 2 * low_ref.shape[0] // batches
    fields = [ref.at[n] for ref in (low_ref, high_ref) for n in range(ref.shape[0])]
    own = own_ref[...]
    slots = range(4)
    if flip:
        slots = [lax.rem(lax.axis_index("region") + d, 4) for d in (3, 1, 2, 2)]
    low, high, far_a, far_b = [got_ref[slot] for slot in slots]
    before = far_a[:, atoms:] + low[:, :atoms] + own[:, :atoms]
    here = low[:, atoms:] + own[:, atoms : 2 * atoms] + high[:, :atoms]
    after = own[:, 2 * atoms :] + high[:, atoms:] + far_b[:, :atoms]

    mine = mom_ref.shape[0]
    want = lax.broadcasted_iota(jnp.int32, (mine, atoms), 0) + lax.axis_index("dev") * mine
    keep = want == lax.broadcasted_iota(jnp.int32, (mine, atoms), 1)
    keep = keep.astype(jnp.float32).astype(jnp.bfloat16)
    taken = dot(keep, jnp.concatenate(split3(here), axis=0), NT)
    taken = taken[:, :ROWS] + taken[:, ROWS : 2 * ROWS] + taken[:, 2 * ROWS :]
    mom_ref[...] = taken[:, :comps]

    moments = jnp.concatenate([before, here, after], axis=1)
    row_id = lax.broadcasted_iota(jnp.int32, (3 * atoms, LANES), 0)
    pick = (row_id == atom_ref[...]).astype(jnp.float32).astype(jnp.bfloat16)
    got = dot(jnp.concatenate(split3(moments), axis=0), pick)
    chosen = got[:ROWS] + got[ROWS : 2 * ROWS] + got[2 * ROWS :]
    chosen = chosen[:comps]
    lane = lax.broadcasted_iota(jnp.int32, (1, points), 1)
    for b in range(batches):
        total = jnp.zeros((comps, points), jnp.float32)
        for i in range(near):
            column = chosen[:, b * SLOT + i : b * SLOT + i + 1]
            total = total + column * fields[b * near + i][...]
        row = jnp.sum(total, axis=0, keepdims=True)
        pot_ref[b : b + 1, :] = jnp.where(lane < size_ref[0, b], row, 0.0)


def held_in_hbm(*values):
    return [pltpu.with_memory_space_constraint(value, pltpu.HBM) for value in values]


def crossed(value, axis, m):
    return lax.ppermute(value, axis, [(i, i ^ m) for i in range(lax.axis_size(axis))])


def turned(value, even, odd):
    count = lax.axis_size("dev")
    return lax.ppermute(value, "dev", [(i, i ^ (odd if i % 2 else even)) for i in range(count)])


def shifted(value, axis, step):
    count = lax.axis_size(axis)
    return lax.ppermute(value, axis, [(i, (i + step) % count) for i in range(count)])


def per_device(
    basis_values,
    density_rows,
    block_mask,
    window_start,
    batch_offsets,
    batch_sizes,
    atom_near,
    harmonics,
    partition,
    radius,
    radial_table,
):
    dev_count = lax.axis_size("dev")
    region_count = lax.axis_size("region")
    blocks_dev, band, width = density_rows.shape[:3]
    batches, near, comps, points = harmonics.shape
    near_blocks = basis_values.shape[1]
    mine = 16
    atoms = mine * dev_count
    f32, bf16 = jnp.float32, jnp.bfloat16

    masked = pl.pallas_call(
        mask_kernel,
        out_shape=pltpu.VMEM(density_rows.shape, bf16),
        in_specs=[HBM, HBM],
        out_specs=VMEM,
        scratch_shapes=[
            pltpu.VMEM(block_mask.shape, jnp.int32),
            pltpu.VMEM(density_rows.shape, bf16),
            pltpu.SemaphoreType.DMA((blocks_dev + 1,)),
        ],
        compiler_params=PARAMS,
        name="mask",
    )(*held_in_hbm(block_mask, density_rows))

    half = batches // 2

    def field(begin, after):
        return pl.pallas_call(
            functools.partial(field_kernel, begin),
            out_shape=(
                pltpu.VMEM((half * near, comps, points), f32),
                pltpu.VMEM((half * near, ROWS, points), bf16),
                pltpu.VMEM((1, LANES), jnp.int32),
            ),
            in_specs=[HBM, SMEM] + [HBM] * 3,
            out_specs=(VMEM,) * 3,
            scratch_shapes=[
                pltpu.VMEM(radial_table.shape[::-1], f32),
                pltpu.VMEM((half,) + radius.shape[1:], f32),
                pltpu.VMEM((half,) + harmonics.shape[1:], bf16),
                pltpu.SemaphoreType.DMA((3,)),
            ],
            compiler_params=WIDE,
            cost_estimate=pl.CostEstimate(
                flops=2_000_000_000, bytes_accessed=8_000_000, transcendentals=0
            ),
            name="field",
        )(after, atom_near.T, *held_in_hbm(radial_table.T, radius, harmonics))

    def turned_basis(after):
        return pl.pallas_call(
            turn_kernel,
            out_shape=(
                pltpu.VMEM((batches, near_blocks, width, points), bf16),
                pltpu.VMEM(partition.shape, f32),
            ),
            in_specs=[HBM] * 3,
            out_specs=(VMEM,) * 2,
            scratch_shapes=[pltpu.VMEM(basis_values.shape, bf16), pltpu.SemaphoreType.DMA((3,))],
            compiler_params=WIDE,
            cost_estimate=pl.CostEstimate(
                flops=2_000_000_000, bytes_accessed=8_000_000, transcendentals=0
            ),
            name="turn",
        )(after, *held_in_hbm(basis_values, partition))

    def selected(even, odd, starts, rows):
        return pl.pallas_call(
            functools.partial(select_kernel, even, odd, dev_count),
            out_shape=pltpu.VMEM((2,) + density_rows.shape[1:], bf16),
            in_specs=[SMEM, VMEM],
            out_specs=VMEM,
            compiler_params=PARAMS,
            name="select",
        )(starts, rows)

    if dev_count == 8:
        beside = crossed(window_start, "dev", 1)
        beside, _ = lax.optimization_barrier((beside, masked))
        first = turned(masked, 4, 2)
        pair = jnp.concatenate([window_start, beside])
        starts = turned(pair, 2, 4)
        g_low, hpad_low, atom_rows = field(0, pair)
        starts, g_low = lax.optimization_barrier((starts, g_low))
        chosen = selected(0, 0, starts, masked)
        second = turned(chosen, 2, 4)
        first, later, _ = lax.optimization_barrier((first, masked, chosen))
        chosen = selected(4, 2, starts, first)
        third = turned(chosen, 2, 4)
        g_high, hpad_high, _ = field(half, chosen)
        phit, weights = turned_basis(g_high)
        second, phit = lax.optimization_barrier((second, phit))
        sent = (later, first, second, third)
        pieces = [piece for value in sent for piece in (value, crossed(value, "dev", 1))]
    else:
        g_low, hpad_low, atom_rows = field(0, masked)
        g_high, hpad_high, _ = field(half, masked)
        phit, weights = turned_basis(masked)
        pieces = [lax.all_gather(masked, "dev", axis=0)]

    density, terms = pl.pallas_call(
        density_kernel,
        out_shape=(
            jax.ShapeDtypeStruct((batches, points), f32),
            jax.ShapeDtypeStruct((ROWS, LANES), f32),
        ),
        in_specs=[SMEM] * 3 + [VMEM] * (5 + len(pieces)),
        out_specs=(VMEM, VMEM),
        scratch_shapes=[
            pltpu.VMEM((dev_count, band, width, width), bf16),
            pltpu.VMEM((LANES // SLOT, SLOT, points), f32),
        ],
        compiler_params=PARAMS,
        cost_estimate=pl.CostEstimate(flops=2_000_000_000, bytes_accessed=6_000_000, transcendentals=0),
        name="density",
    )(
        window_start, batch_offsets, batch_sizes, atom_rows, phit, weights, hpad_low, hpad_high,
        *pieces,
    )

    if dev_count == 8:
        both = jnp.stack([terms, crossed(terms, "dev", 1)])
        quads = [[i for i in range(dev_count) if i % 2 == core] for core in range(2)]
        copies = jnp.broadcast_to(both[None], (4,) + both.shape)
        groups = lax.all_to_all(copies, "dev", 0, 0, axis_index_groups=quads)
    else:
        groups = lax.all_gather(terms, "dev", axis=0).reshape(-1, 2, *terms.shape)
    flip = region_count == 4
    own, send = pl.pallas_call(
        functools.partial(scatter_kernel, comps, atoms, flip),
        out_shape=(
            jax.ShapeDtypeStruct((ROWS, 3 * atoms), f32),
            jax.ShapeDtypeStruct((4 if flip else 3, ROWS, 2 * atoms), f32),
        ),
        in_specs=[VMEM],
        out_specs=(VMEM,) * 2,
        compiler_params=PARAMS,
        name="scatter",
    )(groups)
    if flip:
        got = lax.all_to_all(send, "region", 0, 0)
    else:
        steps = ((0, 1), (1, -1), (2, 2), (2, -2))
        got = jnp.stack([shifted(send[slot], "region", step) for slot, step in steps])

    moments, potential = pl.pallas_call(
        functools.partial(potential_kernel, comps, atoms, flip),
        out_shape=(
            jax.ShapeDtypeStruct((mine, comps), f32),
            jax.ShapeDtypeStruct((batches, points), f32),
        ),
        in_specs=[SMEM] + [VMEM] * 5,
        out_specs=(VMEM, VMEM),
        compiler_params=PARAMS,
        name="potential",
    )(batch_sizes, own, got, atom_rows, g_low, g_high)
    return (density, moments.T, potential)


def solution(mesh):
    both = ("region", "dev")
    placed = (
        P(both, None, None, None),
        P(both, None, None, None),
        P(both, None),
        P(both),
        P(both, None),
        P(both, None),
        P(both, None),
        P(both, None, None, None),
        P(both, None, None),
        P(both, None, None),
        P(),
    )
    return jax.shard_map(
        per_device,
        mesh=mesh,
        in_specs=placed,
        out_specs=(P(both, None), P(None, both), P(both, None)),
        check_vma=False,
    )
```

```python
import functools
import jax
import jax.numpy as jnp
from jax import lax
from jax.experimental import pallas as pl
from jax.experimental.pallas import tpu as pltpu
from jax.sharding import PartitionSpec as P

EVEN_OWNERS = (0, 1, 4, 3, 2, 5, 6, 7)
ODD_OWNERS = (0, 1, 2, 5, 4, 3, 6, 7)
PIECE_ROWS = (None, None, None, None, 0, 1, 0, 1)
LANES = 128
ROWS = 32
SLOT = 8
NT = (((1,), (1,)), ((), ()))
NN = (((1,), (0,)), ((), ()))
VMEM = pl.BlockSpec(memory_space=pltpu.VMEM)
SMEM = pl.BlockSpec(memory_space=pltpu.SMEM)
HBM = pl.BlockSpec(memory_space=pltpu.HBM)
WIDE = pltpu.CompilerParams(vmem_limit_bytes=16 * 1024 * 1024)
PARAMS = pltpu.CompilerParams(vmem_limit_bytes=16 * 1024 * 1024)


def dot(a, b, dims=NN):
    return lax.dot_general(a, b, dims, preferred_element_type=jnp.float32)


def split2(x):
    hi = x.astype(jnp.bfloat16)
    lo = (x - hi.astype(jnp.float32)).astype(jnp.bfloat16)
    return hi, lo


def split3(x):
    hi, mid = split2(x)
    rest = x - hi.astype(jnp.float32) - mid.astype(jnp.float32)
    return hi, mid, rest.astype(jnp.bfloat16)


def cubic(distance):
    inner = 2.0 / 3.0 - distance * distance + 0.5 * distance * distance * distance
    remote = 2.0 - distance
    outer = remote * remote * remote * (1.0 / 6.0)
    return jnp.where(distance < 1.0, inner, jnp.where(distance < 2.0, outer, 0.0))


def chosen_row(owner, start, owners, stored):
    ahead = lax.rem(owner - start + stored * owners, owners)
    return ahead, lax.rem(start + ahead, stored * owners) // owners


def select_kernel(even, odd, owners, starts_ref, rows_ref, out_ref):
    me = lax.axis_index("dev")
    owner = lax.bitwise_xor(me, jnp.where(lax.rem(me, 2) == 1, odd, even))
    for n in range(out_ref.shape[0]):
        row = chosen_row(owner, starts_ref[n], owners, rows_ref.shape[0])[1]
        out_ref[n] = rows_ref[row]


def mask_kernel(mask_hbm, rows_hbm, out_ref, mask, rows, sems):
    stored, band = rows.shape[:2]
    fetch = pltpu.make_async_copy(mask_hbm, mask, sems.at[stored])
    copies = [
        pltpu.make_async_copy(rows_hbm.at[t], rows.at[t], sems.at[t]) for t in range(stored)
    ]
    fetch.start()
    for copy in copies:
        copy.start()
    fetch.wait()
    factors = mask[...].astype(jnp.float32)
    for t, copy in enumerate(copies):
        copy.wait()
        for k in range(band):
            factor = jnp.broadcast_to(factors[t : t + 1, k : k + 1], rows.shape[2:])
            out_ref[t, k] = rows[t, k] * factor.astype(jnp.bfloat16)


def field_kernel(
    begin, after_hbm, table_hbm, radius_hbm, harm_hbm, g_ref, table_ref, radius_ref, harm_ref, sems
):
    batches, near, comps, points = harm_ref.shape
    knots = table_ref.shape[0]
    span = pl.ds(begin, batches)
    moves = (
        (table_hbm, table_ref), (radius_hbm.at[span], radius_ref), (harm_hbm.at[span], harm_ref)
    )
    copies = [pltpu.make_async_copy(a, b, sems.at[n]) for n, (a, b) in enumerate(moves)]
    for copy in copies:
        copy.start()
    knot = lax.broadcasted_iota(jnp.int32, (knots, points), 0).astype(jnp.float32)
    for copy in copies:
        copy.wait()
    r_hi, r_lo = split2(table_ref[...].T)
    coeffs = jnp.concatenate([r_hi, r_hi, r_lo], axis=1)

    def body(b, carry):
        rows = radius_ref[b]
        for i in range(near):
            spline = cubic(jnp.abs(rows[i : i + 1, :] - knot))
            s_hi, s_lo = split2(spline)
            radial = dot(coeffs, jnp.concatenate([s_hi, s_lo, s_hi], axis=0))
            g_ref[b * near + i] = radial * harm_ref[b, i].astype(jnp.float32)
        return carry

    lax.fori_loop(0, batches, body, 0, unroll=2)


def turn_kernel(
    after_hbm, near_ref, basis_hbm, part_hbm, harm_hbm,
    phit_ref, part_ref, hpad_ref, atom_ref, basis, harm_ref, sems,
):
    batches, near_blocks = basis.shape[:2]
    near, comps, points = harm_ref.shape[1:]
    halves = [pl.ds(0, batches // 2), pl.ds(batches // 2, batches - batches // 2)]
    copies = [
        pltpu.make_async_copy(basis_hbm.at[half], basis.at[half], sems.at[n])
        for n, half in enumerate(halves)
    ]
    copies.append(pltpu.make_async_copy(harm_hbm, harm_ref, sems.at[2]))
    copies.append(pltpu.make_async_copy(part_hbm, part_ref, sems.at[3]))
    for copy in copies:
        copy.start()
    lane = lax.broadcasted_iota(jnp.int32, atom_ref.shape, 1)
    atom = jnp.full(atom_ref.shape, -1, jnp.int32)
    for b in range(near_ref.shape[1]):
        for i in range(near):
            atom = jnp.where(lane == b * SLOT + i, near_ref[i, b], atom)
    atom_ref[...] = atom
    for n in range(batches * near):
        hpad_ref[n, ROWS // 2 :, :] = jnp.zeros((ROWS // 2, points), jnp.bfloat16)

    def turn(b, carry):
        for j in range(near_blocks):
            phit_ref[b, j] = basis[b, j].T
        return carry

    def pad(b, carry):
        for i in range(near):
            hpad_ref[b * near + i, 0:comps, :] = harm_ref[b, i]
        return carry

    copies[0].wait()
    lax.fori_loop(0, batches // 2, turn, 0)
    copies[1].wait()
    lax.fori_loop(batches // 2, batches, turn, 0)
    copies[2].wait()
    lax.fori_loop(0, batches, pad, 0)
    copies[3].wait()


def density_kernel(
    start_ref, offset_ref, size_ref, atom_ref, phit_ref, part_ref, hpad_ref, *refs
):
    dens_ref, terms_ref, window_ref, w_ref = refs[-4:]
    pieces = refs[:-4]
    owners = window_ref.shape[0]
    batches, near_blocks, width, points = phit_ref.shape
    near = part_ref.shape[1]
    if len(pieces) == owners:
        me = lax.axis_index("dev")
        odd = lax.rem(me, 2) == 1
        held = [
            (piece, lax.bitwise_xor(me, jnp.where(odd, b, a)), at)
            for piece, a, b, at in zip(pieces, EVEN_OWNERS, ODD_OWNERS, PIECE_ROWS)
        ]
    else:
        held = [(pieces[0].at[owner], owner, None) for owner in range(owners)]
    stored = held[0][0].shape[0]
    for piece, owner, at in held:
        ahead, row = chosen_row(owner, start_ref[0], owners, stored)
        window_ref[ahead] = piece[row if at is None else at]
    w_ref[...] = jnp.zeros(w_ref.shape, w_ref.dtype)
    lane = lax.broadcasted_iota(jnp.int32, (1, points), 1)
    zero = jnp.zeros((width, width), jnp.bfloat16)

    def body(b, carry):
        first = offset_ref[0, b]
        left = []
        for j in range(near_blocks):
            row = [
                window_ref[first + j, f - j + 1] if 0 <= f - j + 1 < 4 else zero
                for f in range(near_blocks)
            ]
            left.append(jnp.concatenate(row, axis=1))
        right = phit_ref[b].reshape(near_blocks * width, points)
        mixed = dot(jnp.concatenate(left, axis=0), right)
        total = jnp.zeros((width, points), jnp.float32)
        for j in range(near_blocks):
            part = mixed[j * width : (j + 1) * width]
            total = total + part * phit_ref[b, j].astype(jnp.float32)
        summed = jnp.sum(total, axis=0, keepdims=True)
        alive = lane < size_ref[0, b]
        row = jnp.where(alive, summed, 0.0)
        dens_ref[pl.ds(b, 1), :] = row
        w_ref[b, 0:near, :] = part_ref[b] * row
        return carry

    lax.fori_loop(0, batches, body, 0, unroll=4)
    weights = w_ref[...].reshape(LANES, points)
    columns = jnp.concatenate(split2(weights), axis=0)
    slot = lax.broadcasted_iota(jnp.int32, (1, 2 * LANES), 1) % LANES
    terms = jnp.zeros((ROWS, 2 * LANES), jnp.float32)
    cross = dot(hpad_ref[...].reshape(batches * near * ROWS, points), columns, NT)
    for n in range(batches * near):
        b, i = divmod(n, near)
        here = cross[n * ROWS : (n + 1) * ROWS]
        terms = terms + jnp.where(slot == b * SLOT + i, here, 0.0)
    result = terms[:, :LANES] + terms[:, LANES:]
    row_id = lax.broadcasted_iota(jnp.int32, (ROWS, LANES), 0)
    comps = ROWS - 7
    terms_ref[...] = jnp.where(row_id == comps, atom_ref[...].astype(jnp.float32), result)


def scatter_kernel(comps, atoms, flip, *refs):
    own, near_a, near_b, far = refs[-4:]
    pieces = [group.at[m] for group in refs[:-4] for m in range(group.shape[0])]
    row_id = lax.broadcasted_iota(jnp.int32, (3 * atoms, LANES), 0)
    total = jnp.zeros((3 * ROWS, 3 * atoms), jnp.float32)
    for m in range(0, len(pieces), 2):
        left, right = [], []
        for values in (pieces[m][...], pieces[m + 1][...]):
            chosen = values[comps : comps + 1, :].astype(jnp.int32)
            right.append((row_id == chosen).astype(jnp.float32).astype(jnp.bfloat16))
            left.append(jnp.concatenate(split3(values), axis=0))
        total = total + dot(jnp.concatenate(left, axis=1), jnp.concatenate(right, axis=1), NT)
    sums = total[:ROWS] + total[ROWS : 2 * ROWS] + total[2 * ROWS :]
    own[...] = sums
    ahead, back = sums[:, atoms:], sums[:, : 2 * atoms]
    if flip:
        odd = lax.rem(lax.axis_index("region"), 2) == 1
        near_a[...] = jnp.where(odd, back, ahead)
        near_b[...] = jnp.where(odd, ahead, back)
    else:
        near_a[...] = ahead
        near_b[...] = back
    far[:, :atoms] = sums[:, :atoms]
    far[:, atoms:] = sums[:, 2 * atoms :]


def potential_kernel(
    comps, atoms, flip, size_ref, own_ref, near_a_ref, near_b_ref, fa_ref, fb_ref, atom_ref,
    low_ref, high_ref, mom_ref, pot_ref,
):
    batches, points = pot_ref.shape
    near = 2 * low_ref.shape[0] // batches
    fields = [ref.at[n] for ref in (low_ref, high_ref) for n in range(ref.shape[0])]
    own = own_ref[...]
    near_a, near_b = near_a_ref[...], near_b_ref[...]
    if flip:
        odd = lax.rem(lax.axis_index("region"), 2) == 1
        low = jnp.where(odd, near_a, near_b)
        high = jnp.where(odd, near_b, near_a)
    else:
        low, high = near_a, near_b
    before = fa_ref[:, atoms:] + low[:, :atoms] + own[:, :atoms]
    here = low[:, atoms:] + own[:, atoms : 2 * atoms] + high[:, :atoms]
    after = own[:, 2 * atoms :] + high[:, atoms:] + fb_ref[:, :atoms]

    mine = mom_ref.shape[0]
    want = lax.broadcasted_iota(jnp.int32, (mine, atoms), 0) + lax.axis_index("dev") * mine
    keep = want == lax.broadcasted_iota(jnp.int32, (mine, atoms), 1)
    keep = keep.astype(jnp.float32).astype(jnp.bfloat16)
    taken = dot(keep, jnp.concatenate(split3(here), axis=0), NT)
    taken = taken[:, :ROWS] + taken[:, ROWS : 2 * ROWS] + taken[:, 2 * ROWS :]
    mom_ref[...] = taken[:, :comps]

    moments = jnp.concatenate([before, here, after], axis=1)
    row_id = lax.broadcasted_iota(jnp.int32, (3 * atoms, LANES), 0)
    pick = (row_id == atom_ref[...]).astype(jnp.float32).astype(jnp.bfloat16)
    got = dot(jnp.concatenate(split3(moments), axis=0), pick)
    chosen = got[:ROWS] + got[ROWS : 2 * ROWS] + got[2 * ROWS :]
    chosen = chosen[:comps]
    lane = lax.broadcasted_iota(jnp.int32, (1, points), 1)
    for b in range(batches):
        total = jnp.zeros((comps, points), jnp.float32)
        for i in range(near):
            column = chosen[:, b * SLOT + i : b * SLOT + i + 1]
            total = total + column * fields[b * near + i][...]
        row = jnp.sum(total, axis=0, keepdims=True)
        pot_ref[b : b + 1, :] = jnp.where(lane < size_ref[0, b], row, 0.0)


def held_in_hbm(*values):
    return [pltpu.with_memory_space_constraint(value, pltpu.HBM) for value in values]


def crossed(value, axis, m):
    return lax.ppermute(value, axis, [(i, i ^ m) for i in range(lax.axis_size(axis))])


def turned(value, even, odd):
    count = lax.axis_size("dev")
    return lax.ppermute(value, "dev", [(i, i ^ (odd if i % 2 else even)) for i in range(count)])


def shifted(value, axis, step):
    count = lax.axis_size(axis)
    return lax.ppermute(value, axis, [(i, (i + step) % count) for i in range(count)])


def per_device(
    basis_values,
    density_rows,
    block_mask,
    window_start,
    batch_offsets,
    batch_sizes,
    atom_near,
    harmonics,
    partition,
    radius,
    radial_table,
):
    dev_count = lax.axis_size("dev")
    region_count = lax.axis_size("region")
    blocks_dev, band, width = density_rows.shape[:3]
    batches, near, comps, points = harmonics.shape
    near_blocks = basis_values.shape[1]
    mine = 16
    atoms = mine * dev_count
    f32, bf16 = jnp.float32, jnp.bfloat16

    masked = pl.pallas_call(
        mask_kernel,
        out_shape=pltpu.VMEM(density_rows.shape, bf16),
        in_specs=[HBM, HBM],
        out_specs=VMEM,
        scratch_shapes=[
            pltpu.VMEM(block_mask.shape, jnp.int32),
            pltpu.VMEM(density_rows.shape, bf16),
            pltpu.SemaphoreType.DMA((blocks_dev + 1,)),
        ],
        compiler_params=PARAMS,
        name="mask",
    )(*held_in_hbm(block_mask, density_rows))

    half = batches // 2
    work = pl.CostEstimate(flops=2_000_000_000, bytes_accessed=8_000_000, transcendentals=0)

    def field(begin, after):
        return pl.pallas_call(
            functools.partial(field_kernel, begin),
            out_shape=pltpu.VMEM((half * near, comps, points), f32),
            in_specs=[HBM] * 4,
            out_specs=VMEM,
            scratch_shapes=[
                pltpu.VMEM(radial_table.shape[::-1], f32),
                pltpu.VMEM((half,) + radius.shape[1:], f32),
                pltpu.VMEM((half,) + harmonics.shape[1:], bf16),
                pltpu.SemaphoreType.DMA((3,)),
            ],
            compiler_params=WIDE,
            cost_estimate=work,
            name="field",
        )(after, *held_in_hbm(radial_table.T, radius, harmonics))

    def turned_basis(after):
        return pl.pallas_call(
            turn_kernel,
            out_shape=(
                pltpu.VMEM((batches, near_blocks, width, points), bf16),
                pltpu.VMEM(partition.shape, f32),
                pltpu.VMEM((batches * near, ROWS, points), bf16),
                pltpu.VMEM((1, LANES), jnp.int32),
            ),
            in_specs=[HBM, SMEM] + [HBM] * 3,
            out_specs=(VMEM,) * 4,
            scratch_shapes=[
                pltpu.VMEM(basis_values.shape, bf16),
                pltpu.VMEM(harmonics.shape, bf16),
                pltpu.SemaphoreType.DMA((4,)),
            ],
            compiler_params=WIDE,
            cost_estimate=work,
            name="turn",
        )(after, atom_near.T, *held_in_hbm(basis_values, partition, harmonics))

    def selected(even, odd, starts, rows):
        return pl.pallas_call(
            functools.partial(select_kernel, even, odd, dev_count),
            out_shape=pltpu.VMEM((2,) + density_rows.shape[1:], bf16),
            in_specs=[SMEM, VMEM],
            out_specs=VMEM,
            compiler_params=PARAMS,
            name="select",
        )(starts, rows)

    if dev_count == 8:
        beside = crossed(window_start, "dev", 1)
        beside, _ = lax.optimization_barrier((beside, masked))
        first = turned(masked, 4, 2)
        pair = jnp.concatenate([window_start, beside])
        starts = turned(pair, 2, 4)
        chosen = selected(0, 0, starts, masked)
        second = turned(chosen, 2, 4)
        first, later, _ = lax.optimization_barrier((first, masked, chosen))
        chosen = selected(4, 2, starts, first)
        third = turned(chosen, 2, 4)
        phit, weights, hpad, atom_rows = turned_basis(chosen)
        second, phit = lax.optimization_barrier((second, phit))
        sent = (later, first, second, third)
        pieces = [piece for value in sent for piece in (value, crossed(value, "dev", 1))]
    else:
        phit, weights, hpad, atom_rows = turned_basis(masked)
        pieces = [lax.all_gather(masked, "dev", axis=0)]

    density, terms = pl.pallas_call(
        density_kernel,
        out_shape=(
            pltpu.VMEM((batches, points), f32),
            pltpu.VMEM((ROWS, LANES), f32),
        ),
        in_specs=[SMEM] * 3 + [VMEM] * (4 + len(pieces)),
        out_specs=(VMEM, VMEM),
        scratch_shapes=[
            pltpu.VMEM((dev_count, band, width, width), bf16),
            pltpu.VMEM((LANES // SLOT, SLOT, points), f32),
        ],
        compiler_params=PARAMS,
        cost_estimate=pl.CostEstimate(flops=2_000_000_000, bytes_accessed=6_000_000, transcendentals=0),
        name="density",
    )(
        window_start, batch_offsets, batch_sizes, atom_rows, phit, weights, hpad,
        *pieces,
    )

    if dev_count == 8:
        both = jnp.stack([terms, crossed(terms, "dev", 1)])
        groups = [both] + [crossed(both, "dev", m) for m in (2, 4, 6)]
    else:
        groups = [lax.all_gather(terms, "dev", axis=0)]
    g_low = field(0, groups[0])
    *groups, g_low = lax.optimization_barrier((*groups, g_low))
    flip = region_count == 4
    own, near_a, near_b, far = pl.pallas_call(
        functools.partial(scatter_kernel, comps, atoms, flip),
        out_shape=tuple(jax.ShapeDtypeStruct((ROWS, n * atoms), f32) for n in (3, 2, 2, 2)),
        in_specs=[VMEM] * len(groups),
        out_specs=(VMEM,) * 4,
        compiler_params=PARAMS,
        name="scatter",
    )(*groups)
    g_high = field(half, own)
    if flip:
        near_a = crossed(near_a, "region", 1)
        far_a = far_b = crossed(far, "region", 2)
        near_b = crossed(near_b, "region", 3)
    else:
        far_a = shifted(far, "region", 2)
        far_b = shifted(far, "region", -2)
        near_a = shifted(near_a, "region", 1)
        near_b = shifted(near_b, "region", -1)

    near_a, near_b, far_a, far_b, g_high = lax.optimization_barrier(
        (near_a, near_b, far_a, far_b, g_high)
    )

    moments, potential = pl.pallas_call(
        functools.partial(potential_kernel, comps, atoms, flip),
        out_shape=(
            jax.ShapeDtypeStruct((mine, comps), f32),
            jax.ShapeDtypeStruct((batches, points), f32),
        ),
        in_specs=[SMEM] + [VMEM] * 8,
        out_specs=(VMEM, VMEM),
        compiler_params=PARAMS,
        name="potential",
    )(batch_sizes, own, near_a, near_b, far_a, far_b, atom_rows, g_low, g_high)
    return (density, moments.T, potential)


def solution(mesh):
    both = ("region", "dev")
    placed = (
        P(both, None, None, None),
        P(both, None, None, None),
        P(both, None),
        P(both),
        P(both, None),
        P(both, None),
        P(both, None),
        P(both, None, None, None),
        P(both, None, None),
        P(both, None, None),
        P(),
    )
    return jax.shard_map(
        per_device,
        mesh=mesh,
        in_specs=placed,
        out_specs=(P(both, None), P(None, both), P(both, None)),
        check_vma=False,
    )
```

```python
import functools
import jax
import jax.numpy as jnp
from jax import lax
from jax.experimental import pallas as pl
from jax.experimental.pallas import tpu as pltpu
from jax.sharding import PartitionSpec as P

EVEN_OWNERS = (0, 1, 4, 3, 2, 5, 6, 7)
ODD_OWNERS = (0, 1, 2, 5, 4, 3, 6, 7)
PIECE_ROWS = (None, None, None, None, 0, 1, 0, 1)
LANES = 128
ROWS = 32
SLOT = 8
NT = (((1,), (1,)), ((), ()))
NN = (((1,), (0,)), ((), ()))
VMEM = pl.BlockSpec(memory_space=pltpu.VMEM)
SMEM = pl.BlockSpec(memory_space=pltpu.SMEM)
HBM = pl.BlockSpec(memory_space=pltpu.HBM)
WIDE = pltpu.CompilerParams(vmem_limit_bytes=16 * 1024 * 1024)
PARAMS = pltpu.CompilerParams(vmem_limit_bytes=16 * 1024 * 1024)


def dot(a, b, dims=NN):
    return lax.dot_general(a, b, dims, preferred_element_type=jnp.float32)


def split2(x):
    hi = x.astype(jnp.bfloat16)
    lo = (x - hi.astype(jnp.float32)).astype(jnp.bfloat16)
    return hi, lo


def split3(x):
    hi, mid = split2(x)
    rest = x - hi.astype(jnp.float32) - mid.astype(jnp.float32)
    return hi, mid, rest.astype(jnp.bfloat16)


def cubic(distance):
    inner = 2.0 / 3.0 - distance * distance + 0.5 * distance * distance * distance
    remote = 2.0 - distance
    outer = remote * remote * remote * (1.0 / 6.0)
    return jnp.where(distance < 1.0, inner, jnp.where(distance < 2.0, outer, 0.0))


def chosen_row(owner, start, owners, stored):
    ahead = lax.rem(owner - start + stored * owners, owners)
    return ahead, lax.rem(start + ahead, stored * owners) // owners


def select_kernel(even, odd, owners, start_ref, beside_ref, rows_ref, out_ref):
    me = lax.axis_index("dev")
    owner = lax.bitwise_xor(me, jnp.where(lax.rem(me, 2) == 1, odd, even))
    for n, ref in enumerate((start_ref, beside_ref)):
        row = chosen_row(owner, ref[0], owners, rows_ref.shape[0])[1]
        out_ref[n] = rows_ref[row]


def mask_kernel(mask_hbm, rows_hbm, out_ref, mask, rows, sems):
    stored, band = rows.shape[:2]
    fetch = pltpu.make_async_copy(mask_hbm, mask, sems.at[stored])
    copies = [
        pltpu.make_async_copy(rows_hbm.at[t], rows.at[t], sems.at[t]) for t in range(stored)
    ]
    fetch.start()
    for copy in copies:
        copy.start()
    fetch.wait()
    factors = mask[...].astype(jnp.float32)
    for t, copy in enumerate(copies):
        copy.wait()
        for k in range(band):
            factor = jnp.broadcast_to(factors[t : t + 1, k : k + 1], rows.shape[2:])
            out_ref[t, k] = rows[t, k] * factor.astype(jnp.bfloat16)


def field_kernel(
    begin, after_hbm, table_hbm, radius_hbm, harm_hbm, g_ref, table_ref, radius_ref, harm_ref, sems
):
    batches, near, comps, points = harm_ref.shape
    knots = table_ref.shape[0]
    span = pl.ds(begin, batches)
    moves = (
        (table_hbm, table_ref), (radius_hbm.at[span], radius_ref), (harm_hbm.at[span], harm_ref)
    )
    copies = [pltpu.make_async_copy(a, b, sems.at[n]) for n, (a, b) in enumerate(moves)]
    for copy in copies:
        copy.start()
    knot = lax.broadcasted_iota(jnp.int32, (knots, points), 0).astype(jnp.float32)
    for copy in copies:
        copy.wait()
    r_hi, r_lo = split2(table_ref[...].T)
    coeffs = jnp.concatenate([r_hi, r_hi, r_lo], axis=1)

    def body(b, carry):
        rows = radius_ref[b]
        for i in range(near):
            spline = cubic(jnp.abs(rows[i : i + 1, :] - knot))
            s_hi, s_lo = split2(spline)
            radial = dot(coeffs, jnp.concatenate([s_hi, s_lo, s_hi], axis=0))
            g_ref[b * near + i] = radial * harm_ref[b, i].astype(jnp.float32)
        return carry

    lax.fori_loop(0, batches, body, 0, unroll=2)


def turn_kernel(
    after_hbm, near_ref, basis_hbm, part_hbm, harm_hbm,
    phit_ref, part_ref, hpad_ref, atom_ref, basis, harm_ref, sems,
):
    batches, near_blocks = basis.shape[:2]
    near, comps, points = harm_ref.shape[1:]
    halves = [pl.ds(0, batches // 2), pl.ds(batches // 2, batches - batches // 2)]
    copies = [
        pltpu.make_async_copy(basis_hbm.at[half], basis.at[half], sems.at[n])
        for n, half in enumerate(halves)
    ]
    copies.append(pltpu.make_async_copy(harm_hbm, harm_ref, sems.at[2]))
    copies.append(pltpu.make_async_copy(part_hbm, part_ref, sems.at[3]))
    for copy in copies:
        copy.start()
    lane = lax.broadcasted_iota(jnp.int32, atom_ref.shape, 1)
    atom = jnp.full(atom_ref.shape, -1, jnp.int32)
    for b in range(near_ref.shape[1]):
        for i in range(near):
            atom = jnp.where(lane == b * SLOT + i, near_ref[i, b], atom)
    atom_ref[...] = atom
    for n in range(batches * near):
        hpad_ref[n, ROWS // 2 :, :] = jnp.zeros((ROWS // 2, points), jnp.bfloat16)

    def turn(b, carry):
        for j in range(near_blocks):
            phit_ref[b, j] = basis[b, j].T
        return carry

    def pad(b, carry):
        for i in range(near):
            hpad_ref[b * near + i, 0:comps, :] = harm_ref[b, i]
        return carry

    copies[0].wait()
    lax.fori_loop(0, batches // 2, turn, 0)
    copies[1].wait()
    lax.fori_loop(batches // 2, batches, turn, 0)
    copies[2].wait()
    lax.fori_loop(0, batches, pad, 0)
    copies[3].wait()


def density_kernel(
    start_ref, offset_ref, size_ref, atom_ref, phit_ref, part_ref, hpad_ref, *refs
):
    dens_ref, terms_ref, window_ref, w_ref = refs[-4:]
    pieces = refs[:-4]
    owners = window_ref.shape[0]
    batches, near_blocks, width, points = phit_ref.shape
    near = part_ref.shape[1]
    if len(pieces) == owners:
        me = lax.axis_index("dev")
        odd = lax.rem(me, 2) == 1
        held = [
            (piece, lax.bitwise_xor(me, jnp.where(odd, b, a)), at)
            for piece, a, b, at in zip(pieces, EVEN_OWNERS, ODD_OWNERS, PIECE_ROWS)
        ]
    else:
        held = [(pieces[0].at[owner], owner, None) for owner in range(owners)]
    stored = held[0][0].shape[0]
    for piece, owner, at in held:
        ahead, row = chosen_row(owner, start_ref[0], owners, stored)
        window_ref[ahead] = piece[row if at is None else at]
    w_ref[...] = jnp.zeros(w_ref.shape, w_ref.dtype)
    lane = lax.broadcasted_iota(jnp.int32, (1, points), 1)
    zero = jnp.zeros((width, width), jnp.bfloat16)

    def body(b, carry):
        first = offset_ref[0, b]
        left = []
        for j in range(near_blocks):
            row = [
                window_ref[first + j, f - j + 1] if 0 <= f - j + 1 < 4 else zero
                for f in range(near_blocks)
            ]
            left.append(jnp.concatenate(row, axis=1))
        right = phit_ref[b].reshape(near_blocks * width, points)
        mixed = dot(jnp.concatenate(left, axis=0), right)
        total = jnp.zeros((width, points), jnp.float32)
        for j in range(near_blocks):
            part = mixed[j * width : (j + 1) * width]
            total = total + part * phit_ref[b, j].astype(jnp.float32)
        summed = jnp.sum(total, axis=0, keepdims=True)
        alive = lane < size_ref[0, b]
        row = jnp.where(alive, summed, 0.0)
        dens_ref[pl.ds(b, 1), :] = row
        w_ref[b, 0:near, :] = part_ref[b] * row
        return carry

    lax.fori_loop(0, batches, body, 0, unroll=4)
    weights = w_ref[...].reshape(LANES, points)
    columns = jnp.concatenate(split2(weights), axis=0)
    slot = lax.broadcasted_iota(jnp.int32, (1, 2 * LANES), 1) % LANES
    terms = jnp.zeros((ROWS, 2 * LANES), jnp.float32)
    cross = dot(hpad_ref[...].reshape(batches * near * ROWS, points), columns, NT)
    for n in range(batches * near):
        b, i = divmod(n, near)
        here = cross[n * ROWS : (n + 1) * ROWS]
        terms = terms + jnp.where(slot == b * SLOT + i, here, 0.0)
    result = terms[:, :LANES] + terms[:, LANES:]
    row_id = lax.broadcasted_iota(jnp.int32, (ROWS, LANES), 0)
    comps = ROWS - 7
    terms_ref[...] = jnp.where(row_id == comps, atom_ref[...].astype(jnp.float32), result)


def scatter_kernel(comps, atoms, flip, *refs):
    own, near_a, near_b, far = refs[-4:]
    pieces = [group.at[m] for group in refs[:-4] for m in range(group.shape[0])]
    row_id = lax.broadcasted_iota(jnp.int32, (3 * atoms, LANES), 0)
    total = jnp.zeros((3 * ROWS, 3 * atoms), jnp.float32)
    for m in range(0, len(pieces), 2):
        left, right = [], []
        for values in (pieces[m][...], pieces[m + 1][...]):
            chosen = values[comps : comps + 1, :].astype(jnp.int32)
            right.append((row_id == chosen).astype(jnp.float32).astype(jnp.bfloat16))
            left.append(jnp.concatenate(split3(values), axis=0))
        total = total + dot(jnp.concatenate(left, axis=1), jnp.concatenate(right, axis=1), NT)
    sums = total[:ROWS] + total[ROWS : 2 * ROWS] + total[2 * ROWS :]
    own[...] = sums
    ahead, back = sums[:, atoms:], sums[:, : 2 * atoms]
    if flip:
        odd = lax.rem(lax.axis_index("region"), 2) == 1
        near_a[...] = jnp.where(odd, back, ahead)
        near_b[...] = jnp.where(odd, ahead, back)
    else:
        near_a[...] = ahead
        near_b[...] = back
    far[:, :atoms] = sums[:, :atoms]
    far[:, atoms:] = sums[:, 2 * atoms :]


def potential_kernel(
    comps, atoms, flip, size_ref, own_ref, near_b_ref, fa_ref, fb_ref, near_a_ref, atom_ref,
    low_ref, high_ref, mom_ref, pot_ref,
):
    batches, points = pot_ref.shape
    near = 2 * low_ref.shape[0] // batches
    fields = [ref.at[n] for ref in (low_ref, high_ref) for n in range(ref.shape[0])]
    own = own_ref[...]
    near_a, near_b = near_a_ref[...], near_b_ref[...]
    if flip:
        odd = lax.rem(lax.axis_index("region"), 2) == 1
        low = jnp.where(odd, near_a, near_b)
        high = jnp.where(odd, near_b, near_a)
    else:
        low, high = near_a, near_b
    before = fa_ref[:, atoms:] + low[:, :atoms] + own[:, :atoms]
    here = low[:, atoms:] + own[:, atoms : 2 * atoms] + high[:, :atoms]
    after = own[:, 2 * atoms :] + high[:, atoms:] + fb_ref[:, :atoms]

    mine = mom_ref.shape[0]
    want = lax.broadcasted_iota(jnp.int32, (mine, atoms), 0) + lax.axis_index("dev") * mine
    keep = want == lax.broadcasted_iota(jnp.int32, (mine, atoms), 1)
    keep = keep.astype(jnp.float32).astype(jnp.bfloat16)
    taken = dot(keep, jnp.concatenate(split3(here), axis=0), NT)
    taken = taken[:, :ROWS] + taken[:, ROWS : 2 * ROWS] + taken[:, 2 * ROWS :]
    mom_ref[...] = taken[:, :comps]

    moments = jnp.concatenate([before, here, after], axis=1)
    row_id = lax.broadcasted_iota(jnp.int32, (3 * atoms, LANES), 0)
    pick = (row_id == atom_ref[...]).astype(jnp.float32).astype(jnp.bfloat16)
    got = dot(jnp.concatenate(split3(moments), axis=0), pick)
    chosen = got[:ROWS] + got[ROWS : 2 * ROWS] + got[2 * ROWS :]
    chosen = chosen[:comps]
    lane = lax.broadcasted_iota(jnp.int32, (1, points), 1)
    for b in range(batches):
        total = jnp.zeros((comps, points), jnp.float32)
        for i in range(near):
            column = chosen[:, b * SLOT + i : b * SLOT + i + 1]
            total = total + column * fields[b * near + i][...]
        row = jnp.sum(total, axis=0, keepdims=True)
        pot_ref[b : b + 1, :] = jnp.where(lane < size_ref[0, b], row, 0.0)


def held_in_hbm(*values):
    return [pltpu.with_memory_space_constraint(value, pltpu.HBM) for value in values]


def crossed(value, axis, m):
    return lax.ppermute(value, axis, [(i, i ^ m) for i in range(lax.axis_size(axis))])


def turned(value, even, odd):
    count = lax.axis_size("dev")
    return lax.ppermute(value, "dev", [(i, i ^ (odd if i % 2 else even)) for i in range(count)])


def shifted(value, axis, step):
    count = lax.axis_size(axis)
    return lax.ppermute(value, axis, [(i, (i + step) % count) for i in range(count)])


def per_device(
    basis_values,
    density_rows,
    block_mask,
    window_start,
    batch_offsets,
    batch_sizes,
    atom_near,
    harmonics,
    partition,
    radius,
    radial_table,
):
    dev_count = lax.axis_size("dev")
    region_count = lax.axis_size("region")
    blocks_dev, band, width = density_rows.shape[:3]
    batches, near, comps, points = harmonics.shape
    near_blocks = basis_values.shape[1]
    mine = 16
    atoms = mine * dev_count
    f32, bf16 = jnp.float32, jnp.bfloat16

    masked = pl.pallas_call(
        mask_kernel,
        out_shape=pltpu.VMEM(density_rows.shape, bf16),
        in_specs=[HBM, HBM],
        out_specs=VMEM,
        scratch_shapes=[
            pltpu.VMEM(block_mask.shape, jnp.int32),
            pltpu.VMEM(density_rows.shape, bf16),
            pltpu.SemaphoreType.DMA((blocks_dev + 1,)),
        ],
        compiler_params=PARAMS,
        name="mask",
    )(*held_in_hbm(block_mask, density_rows))

    half = batches // 2
    work = pl.CostEstimate(flops=2_000_000_000, bytes_accessed=8_000_000, transcendentals=0)

    def field(begin, after):
        return pl.pallas_call(
            functools.partial(field_kernel, begin),
            out_shape=pltpu.VMEM((half * near, comps, points), f32),
            in_specs=[HBM] * 4,
            out_specs=VMEM,
            scratch_shapes=[
                pltpu.VMEM(radial_table.shape[::-1], f32),
                pltpu.VMEM((half,) + radius.shape[1:], f32),
                pltpu.VMEM((half,) + harmonics.shape[1:], bf16),
                pltpu.SemaphoreType.DMA((3,)),
            ],
            compiler_params=WIDE,
            cost_estimate=work,
            name="field",
        )(after, *held_in_hbm(radial_table.T, radius, harmonics))

    def turned_basis(after):
        return pl.pallas_call(
            turn_kernel,
            out_shape=(
                pltpu.VMEM((batches, near_blocks, width, points), bf16),
                pltpu.VMEM(partition.shape, f32),
                pltpu.VMEM((batches * near, ROWS, points), bf16),
                pltpu.VMEM((1, LANES), jnp.int32),
            ),
            in_specs=[HBM, SMEM] + [HBM] * 3,
            out_specs=(VMEM,) * 4,
            scratch_shapes=[
                pltpu.VMEM(basis_values.shape, bf16),
                pltpu.VMEM(harmonics.shape, bf16),
                pltpu.SemaphoreType.DMA((4,)),
            ],
            compiler_params=WIDE,
            cost_estimate=work,
            name="turn",
        )(after, atom_near.T, *held_in_hbm(basis_values, partition, harmonics))

    def selected(even, odd, starts, rows):
        return pl.pallas_call(
            functools.partial(select_kernel, even, odd, dev_count),
            out_shape=pltpu.VMEM((2,) + density_rows.shape[1:], bf16),
            in_specs=[SMEM, SMEM, VMEM],
            out_specs=VMEM,
            compiler_params=PARAMS,
            name="select",
        )(*starts, rows)

    if dev_count == 8:
        starts = (turned(window_start, 2, 4), turned(window_start, 5, 3))
        first = turned(masked, 4, 2)
        chosen = selected(0, 0, starts, masked)
        second = turned(chosen, 2, 4)
        first, later, _ = lax.optimization_barrier((first, masked, chosen))
        chosen = selected(4, 2, starts, first)
        third = turned(chosen, 2, 4)
        phit, weights, hpad, atom_rows = turned_basis(chosen)
        second, phit = lax.optimization_barrier((second, phit))
        sent = (later, first, second, third)
        pieces = [piece for value in sent for piece in (value, crossed(value, "dev", 1))]
    else:
        phit, weights, hpad, atom_rows = turned_basis(masked)
        pieces = [lax.all_gather(masked, "dev", axis=0)]

    density, terms = pl.pallas_call(
        density_kernel,
        out_shape=(
            pltpu.VMEM((batches, points), f32),
            pltpu.VMEM((ROWS, LANES), f32),
        ),
        in_specs=[SMEM] * 3 + [VMEM] * (4 + len(pieces)),
        out_specs=(VMEM, VMEM),
        scratch_shapes=[
            pltpu.VMEM((dev_count, band, width, width), bf16),
            pltpu.VMEM((LANES // SLOT, SLOT, points), f32),
        ],
        compiler_params=PARAMS,
        cost_estimate=pl.CostEstimate(flops=2_000_000_000, bytes_accessed=6_000_000, transcendentals=0),
        name="density",
    )(
        window_start, batch_offsets, batch_sizes, atom_rows, phit, weights, hpad,
        *pieces,
    )

    if dev_count == 8:
        both = jnp.stack([terms, crossed(terms, "dev", 1)])
        groups = [both] + [crossed(both, "dev", m) for m in (2, 4, 6)]
    else:
        groups = [lax.all_gather(terms, "dev", axis=0)]
    g_low = field(0, groups[0])
    *groups, g_low = lax.optimization_barrier((*groups, g_low))
    flip = region_count == 4
    own, near_a, near_b, far = pl.pallas_call(
        functools.partial(scatter_kernel, comps, atoms, flip),
        out_shape=tuple(jax.ShapeDtypeStruct((ROWS, n * atoms), f32) for n in (3, 2, 2, 2)),
        in_specs=[VMEM] * len(groups),
        out_specs=(VMEM,) * 4,
        compiler_params=PARAMS,
        name="scatter",
    )(*groups)
    g_high = field(half, own)
    if flip:
        near_b = crossed(near_b, "region", 3)
        far_a = far_b = crossed(far, "region", 2)
        near_a = crossed(near_a, "region", 1)
    else:
        far_a = shifted(far, "region", 2)
        far_b = shifted(far, "region", -2)
        near_a = shifted(near_a, "region", 1)
        near_b = shifted(near_b, "region", -1)

    near_b, far_a, far_b, near_a, g_high = lax.optimization_barrier(
        (near_b, far_a, far_b, near_a, g_high)
    )

    moments, potential = pl.pallas_call(
        functools.partial(potential_kernel, comps, atoms, flip),
        out_shape=(
            jax.ShapeDtypeStruct((mine, comps), f32),
            jax.ShapeDtypeStruct((batches, points), f32),
        ),
        in_specs=[SMEM] + [VMEM] * 8,
        out_specs=(VMEM, VMEM),
        compiler_params=PARAMS,
        name="potential",
    )(batch_sizes, own, near_b, far_a, far_b, near_a, atom_rows, g_low, g_high)
    return (density, moments.T, potential)


def solution(mesh):
    both = ("region", "dev")
    placed = (
        P(both, None, None, None),
        P(both, None, None, None),
        P(both, None),
        P(both),
        P(both, None),
        P(both, None),
        P(both, None),
        P(both, None, None, None),
        P(both, None, None),
        P(both, None, None),
        P(),
    )
    return jax.shard_map(
        per_device,
        mesh=mesh,
        in_specs=placed,
        out_specs=(P(both, None), P(None, both), P(both, None)),
        check_vma=False,
    )
```

```python
import functools
import jax
import jax.numpy as jnp
from jax import lax
from jax.experimental import pallas as pl
from jax.experimental.pallas import tpu as pltpu
from jax.sharding import PartitionSpec as P

EVEN_OWNERS = (0, 1, 4, 3, 2, 5, 6, 7)
ODD_OWNERS = (0, 1, 2, 5, 4, 3, 6, 7)
PIECE_ROWS = (None, None, None, None, 0, 1, 0, 1)
LANES = 128
ROWS = 32
SLOT = 8
NT = (((1,), (1,)), ((), ()))
NN = (((1,), (0,)), ((), ()))
VMEM = pl.BlockSpec(memory_space=pltpu.VMEM)
SMEM = pl.BlockSpec(memory_space=pltpu.SMEM)
HBM = pl.BlockSpec(memory_space=pltpu.HBM)
WIDE = pltpu.CompilerParams(vmem_limit_bytes=16 * 1024 * 1024)
PARAMS = pltpu.CompilerParams(vmem_limit_bytes=16 * 1024 * 1024)


def dot(a, b, dims=NN):
    return lax.dot_general(a, b, dims, preferred_element_type=jnp.float32)


def split2(x):
    hi = x.astype(jnp.bfloat16)
    lo = (x - hi.astype(jnp.float32)).astype(jnp.bfloat16)
    return hi, lo


def split3(x):
    hi, mid = split2(x)
    rest = x - hi.astype(jnp.float32) - mid.astype(jnp.float32)
    return hi, mid, rest.astype(jnp.bfloat16)


def cubic(distance):
    inner = 2.0 / 3.0 - distance * distance + 0.5 * distance * distance * distance
    remote = 2.0 - distance
    outer = remote * remote * remote * (1.0 / 6.0)
    return jnp.where(distance < 1.0, inner, jnp.where(distance < 2.0, outer, 0.0))


def chosen_row(owner, start, owners, stored):
    ahead = lax.rem(owner - start + stored * owners, owners)
    return ahead, lax.rem(start + ahead, stored * owners) // owners


def select_kernel(even, odd, owners, starts_ref, rows_ref, out_ref):
    me = lax.axis_index("dev")
    owner = lax.bitwise_xor(me, jnp.where(lax.rem(me, 2) == 1, odd, even))
    for n in range(out_ref.shape[0]):
        row = chosen_row(owner, starts_ref[n], owners, rows_ref.shape[0])[1]
        out_ref[n] = rows_ref[row]


def mask_kernel(mask_hbm, rows_hbm, out_ref, mask, rows, sems):
    stored, band = rows.shape[:2]
    fetch = pltpu.make_async_copy(mask_hbm, mask, sems.at[stored])
    copies = [
        pltpu.make_async_copy(rows_hbm.at[t], rows.at[t], sems.at[t]) for t in range(stored)
    ]
    fetch.start()
    for copy in copies:
        copy.start()
    fetch.wait()
    factors = mask[...].astype(jnp.float32)
    for t, copy in enumerate(copies):
        copy.wait()
        for k in range(band):
            factor = jnp.broadcast_to(factors[t : t + 1, k : k + 1], rows.shape[2:])
            out_ref[t, k] = rows[t, k] * factor.astype(jnp.bfloat16)


def field_kernel(
    begin, after_hbm, table_hbm, radius_hbm, harm_hbm, g_ref, table_ref, radius_ref, harm_ref, sems
):
    batches, near, comps, points = harm_ref.shape
    knots = table_ref.shape[0]
    span = pl.ds(begin, batches)
    moves = (
        (table_hbm, table_ref), (radius_hbm.at[span], radius_ref), (harm_hbm.at[span], harm_ref)
    )
    copies = [pltpu.make_async_copy(a, b, sems.at[n]) for n, (a, b) in enumerate(moves)]
    for copy in copies:
        copy.start()
    knot = lax.broadcasted_iota(jnp.int32, (knots, points), 0).astype(jnp.float32)
    for copy in copies:
        copy.wait()
    r_hi, r_lo = split2(table_ref[...].T)
    coeffs = jnp.concatenate([r_hi, r_hi, r_lo], axis=1)

    def body(b, carry):
        rows = radius_ref[b]
        for i in range(near):
            spline = cubic(jnp.abs(rows[i : i + 1, :] - knot))
            s_hi, s_lo = split2(spline)
            radial = dot(coeffs, jnp.concatenate([s_hi, s_lo, s_hi], axis=0))
            g_ref[b * near + i] = radial * harm_ref[b, i].astype(jnp.float32)
        return carry

    lax.fori_loop(0, batches, body, 0, unroll=2)


def turn_kernel(
    after_hbm, near_ref, basis_hbm, part_hbm, harm_hbm,
    phit_ref, part_ref, hpad_ref, atom_ref, basis, harm_ref, sems,
):
    batches, near_blocks = basis.shape[:2]
    near, comps, points = harm_ref.shape[1:]
    halves = [pl.ds(0, batches // 2), pl.ds(batches // 2, batches - batches // 2)]
    copies = [
        pltpu.make_async_copy(basis_hbm.at[half], basis.at[half], sems.at[n])
        for n, half in enumerate(halves)
    ]
    copies.append(pltpu.make_async_copy(harm_hbm, harm_ref, sems.at[2]))
    copies.append(pltpu.make_async_copy(part_hbm, part_ref, sems.at[3]))
    for copy in copies:
        copy.start()
    lane = lax.broadcasted_iota(jnp.int32, atom_ref.shape, 1)
    atom = jnp.full(atom_ref.shape, -1, jnp.int32)
    for b in range(near_ref.shape[1]):
        for i in range(near):
            atom = jnp.where(lane == b * SLOT + i, near_ref[i, b], atom)
    atom_ref[...] = atom
    for n in range(batches * near):
        hpad_ref[n, ROWS // 2 :, :] = jnp.zeros((ROWS // 2, points), jnp.bfloat16)

    def turn(b, carry):
        for j in range(near_blocks):
            phit_ref[b, j] = basis[b, j].T
        return carry

    def pad(b, carry):
        for i in range(near):
            hpad_ref[b * near + i, 0:comps, :] = harm_ref[b, i]
        return carry

    copies[0].wait()
    lax.fori_loop(0, batches // 2, turn, 0)
    copies[1].wait()
    lax.fori_loop(batches // 2, batches, turn, 0)
    copies[2].wait()
    lax.fori_loop(0, batches, pad, 0)
    copies[3].wait()


def density_kernel(
    start_ref, offset_ref, size_ref, atom_ref, phit_ref, part_ref, hpad_ref, *refs
):
    dens_ref, terms_ref, window_ref, w_ref = refs[-4:]
    pieces = refs[:-4]
    owners = window_ref.shape[0]
    batches, near_blocks, width, points = phit_ref.shape
    near = part_ref.shape[1]
    if len(pieces) == owners:
        me = lax.axis_index("dev")
        odd = lax.rem(me, 2) == 1
        held = [
            (piece, lax.bitwise_xor(me, jnp.where(odd, b, a)), at)
            for piece, a, b, at in zip(pieces, EVEN_OWNERS, ODD_OWNERS, PIECE_ROWS)
        ]
    else:
        held = [(pieces[0].at[owner], owner, None) for owner in range(owners)]
    stored = held[0][0].shape[0]
    for piece, owner, at in held:
        ahead, row = chosen_row(owner, start_ref[0], owners, stored)
        window_ref[ahead] = piece[row if at is None else at]
    w_ref[...] = jnp.zeros(w_ref.shape, w_ref.dtype)
    lane = lax.broadcasted_iota(jnp.int32, (1, points), 1)
    zero = jnp.zeros((width, width), jnp.bfloat16)

    def body(b, carry):
        first = offset_ref[0, b]
        left = []
        for j in range(near_blocks):
            row = [
                window_ref[first + j, f - j + 1] if 0 <= f - j + 1 < 4 else zero
                for f in range(near_blocks)
            ]
            left.append(jnp.concatenate(row, axis=1))
        right = phit_ref[b].reshape(near_blocks * width, points)
        mixed = dot(jnp.concatenate(left, axis=0), right)
        total = jnp.zeros((width, points), jnp.float32)
        for j in range(near_blocks):
            part = mixed[j * width : (j + 1) * width]
            total = total + part * phit_ref[b, j].astype(jnp.float32)
        summed = jnp.sum(total, axis=0, keepdims=True)
        alive = lane < size_ref[0, b]
        row = jnp.where(alive, summed, 0.0)
        dens_ref[pl.ds(b, 1), :] = row
        w_ref[b, 0:near, :] = part_ref[b] * row
        return carry

    lax.fori_loop(0, batches, body, 0, unroll=4)
    weights = w_ref[...].reshape(LANES, points)
    columns = jnp.concatenate(split2(weights), axis=0)
    slot = lax.broadcasted_iota(jnp.int32, (1, 2 * LANES), 1) % LANES
    terms = jnp.zeros((ROWS, 2 * LANES), jnp.float32)
    cross = dot(hpad_ref[...].reshape(batches * near * ROWS, points), columns, NT)
    for n in range(batches * near):
        b, i = divmod(n, near)
        here = cross[n * ROWS : (n + 1) * ROWS]
        terms = terms + jnp.where(slot == b * SLOT + i, here, 0.0)
    result = terms[:, :LANES] + terms[:, LANES:]
    row_id = lax.broadcasted_iota(jnp.int32, (ROWS, LANES), 0)
    comps = ROWS - 7
    terms_ref[...] = jnp.where(row_id == comps, atom_ref[...].astype(jnp.float32), result)


def scatter_kernel(comps, atoms, flip, *refs):
    own, near_a, near_b, far = refs[-4:]
    pieces = [group.at[m] for group in refs[:-4] for m in range(group.shape[0])]
    row_id = lax.broadcasted_iota(jnp.int32, (3 * atoms, LANES), 0)
    total = jnp.zeros((3 * ROWS, 3 * atoms), jnp.float32)
    for m in range(0, len(pieces), 2):
        left, right = [], []
        for values in (pieces[m][...], pieces[m + 1][...]):
            chosen = values[comps : comps + 1, :].astype(jnp.int32)
            right.append((row_id == chosen).astype(jnp.float32).astype(jnp.bfloat16))
            left.append(jnp.concatenate(split3(values), axis=0))
        total = total + dot(jnp.concatenate(left, axis=1), jnp.concatenate(right, axis=1), NT)
    sums = total[:ROWS] + total[ROWS : 2 * ROWS] + total[2 * ROWS :]
    own[...] = sums
    ahead, back = sums[:, atoms:], sums[:, : 2 * atoms]
    if flip:
        odd = lax.rem(lax.axis_index("region"), 2) == 1
        near_a[...] = jnp.where(odd, back, ahead)
        near_b[...] = jnp.where(odd, ahead, back)
    else:
        near_a[...] = ahead
        near_b[...] = back
    far[:, :atoms] = sums[:, :atoms]
    far[:, atoms:] = sums[:, 2 * atoms :]


def potential_kernel(
    comps, atoms, flip, size_ref, own_ref, near_b_ref, fa_ref, fb_ref, near_a_ref, atom_ref,
    low_ref, high_ref, mom_ref, pot_ref,
):
    batches, points = pot_ref.shape
    near = 2 * low_ref.shape[0] // batches
    fields = [ref.at[n] for ref in (low_ref, high_ref) for n in range(ref.shape[0])]
    own = own_ref[...]
    near_a, near_b = near_a_ref[...], near_b_ref[...]
    if flip:
        odd = lax.rem(lax.axis_index("region"), 2) == 1
        low = jnp.where(odd, near_a, near_b)
        high = jnp.where(odd, near_b, near_a)
    else:
        low, high = near_a, near_b
    before = fa_ref[:, atoms:] + low[:, :atoms] + own[:, :atoms]
    here = low[:, atoms:] + own[:, atoms : 2 * atoms] + high[:, :atoms]
    after = own[:, 2 * atoms :] + high[:, atoms:] + fb_ref[:, :atoms]

    mine = mom_ref.shape[0]
    want = lax.broadcasted_iota(jnp.int32, (mine, atoms), 0) + lax.axis_index("dev") * mine
    keep = want == lax.broadcasted_iota(jnp.int32, (mine, atoms), 1)
    keep = keep.astype(jnp.float32).astype(jnp.bfloat16)
    taken = dot(keep, jnp.concatenate(split3(here), axis=0), NT)
    taken = taken[:, :ROWS] + taken[:, ROWS : 2 * ROWS] + taken[:, 2 * ROWS :]
    mom_ref[...] = taken[:, :comps]

    moments = jnp.concatenate([before, here, after], axis=1)
    row_id = lax.broadcasted_iota(jnp.int32, (3 * atoms, LANES), 0)
    pick = (row_id == atom_ref[...]).astype(jnp.float32).astype(jnp.bfloat16)
    got = dot(jnp.concatenate(split3(moments), axis=0), pick)
    chosen = got[:ROWS] + got[ROWS : 2 * ROWS] + got[2 * ROWS :]
    chosen = chosen[:comps]
    lane = lax.broadcasted_iota(jnp.int32, (1, points), 1)
    for b in range(batches):
        total = jnp.zeros((comps, points), jnp.float32)
        for i in range(near):
            column = chosen[:, b * SLOT + i : b * SLOT + i + 1]
            total = total + column * fields[b * near + i][...]
        row = jnp.sum(total, axis=0, keepdims=True)
        pot_ref[b : b + 1, :] = jnp.where(lane < size_ref[0, b], row, 0.0)


def held_in_hbm(*values):
    return [pltpu.with_memory_space_constraint(value, pltpu.HBM) for value in values]


def crossed(value, axis, m):
    return lax.ppermute(value, axis, [(i, i ^ m) for i in range(lax.axis_size(axis))])


def turned(value, even, odd):
    count = lax.axis_size("dev")
    return lax.ppermute(value, "dev", [(i, i ^ (odd if i % 2 else even)) for i in range(count)])


def shifted(value, axis, step):
    count = lax.axis_size(axis)
    return lax.ppermute(value, axis, [(i, (i + step) % count) for i in range(count)])


def per_device(
    basis_values,
    density_rows,
    block_mask,
    window_start,
    batch_offsets,
    batch_sizes,
    atom_near,
    harmonics,
    partition,
    radius,
    radial_table,
):
    dev_count = lax.axis_size("dev")
    region_count = lax.axis_size("region")
    blocks_dev, band, width = density_rows.shape[:3]
    batches, near, comps, points = harmonics.shape
    near_blocks = basis_values.shape[1]
    mine = 16
    atoms = mine * dev_count
    f32, bf16 = jnp.float32, jnp.bfloat16

    work = pl.CostEstimate(flops=2_000_000_000, bytes_accessed=8_000_000, transcendentals=0)
    masked = pl.pallas_call(
        mask_kernel,
        out_shape=pltpu.VMEM(density_rows.shape, bf16),
        in_specs=[HBM, HBM],
        out_specs=VMEM,
        scratch_shapes=[
            pltpu.VMEM(block_mask.shape, jnp.int32),
            pltpu.VMEM(density_rows.shape, bf16),
            pltpu.SemaphoreType.DMA((blocks_dev + 1,)),
        ],
        compiler_params=PARAMS,
        cost_estimate=work,
        name="mask",
    )(*held_in_hbm(block_mask, density_rows))

    half = batches // 2

    def field(begin, after):
        return pl.pallas_call(
            functools.partial(field_kernel, begin),
            out_shape=pltpu.VMEM((half * near, comps, points), f32),
            in_specs=[HBM] * 4,
            out_specs=VMEM,
            scratch_shapes=[
                pltpu.VMEM(radial_table.shape[::-1], f32),
                pltpu.VMEM((half,) + radius.shape[1:], f32),
                pltpu.VMEM((half,) + harmonics.shape[1:], bf16),
                pltpu.SemaphoreType.DMA((3,)),
            ],
            compiler_params=WIDE,
            cost_estimate=work,
            name="field",
        )(after, *held_in_hbm(radial_table.T, radius, harmonics))

    def turned_basis(after):
        return pl.pallas_call(
            turn_kernel,
            out_shape=(
                pltpu.VMEM((batches, near_blocks, width, points), bf16),
                pltpu.VMEM(partition.shape, f32),
                pltpu.VMEM((batches * near, ROWS, points), bf16),
                pltpu.VMEM((1, LANES), jnp.int32),
            ),
            in_specs=[HBM, SMEM] + [HBM] * 3,
            out_specs=(VMEM,) * 4,
            scratch_shapes=[
                pltpu.VMEM(basis_values.shape, bf16),
                pltpu.VMEM(harmonics.shape, bf16),
                pltpu.SemaphoreType.DMA((4,)),
            ],
            compiler_params=WIDE,
            cost_estimate=work,
            name="turn",
        )(after, atom_near.T, *held_in_hbm(basis_values, partition, harmonics))

    def selected(even, odd, starts, rows):
        return pl.pallas_call(
            functools.partial(select_kernel, even, odd, dev_count),
            out_shape=pltpu.VMEM((2,) + density_rows.shape[1:], bf16),
            in_specs=[SMEM, VMEM],
            out_specs=VMEM,
            compiler_params=PARAMS,
            name="select",
        )(starts, rows)

    if dev_count == 8:
        beside = crossed(window_start, "dev", 1)
        beside, rows = lax.optimization_barrier((beside, masked))
        first = turned(rows, 4, 2)
        starts = turned(jnp.concatenate([window_start, beside]), 2, 4)
        chosen = selected(0, 0, starts, masked)
        second = turned(chosen, 2, 4)
        first, later, _ = lax.optimization_barrier((first, masked, chosen))
        chosen = selected(4, 2, starts, first)
        third = turned(chosen, 2, 4)
        phit, weights, hpad, atom_rows = turned_basis(chosen)
        second, phit = lax.optimization_barrier((second, phit))
        sent = (later, first, second, third)
        pieces = [piece for value in sent for piece in (value, crossed(value, "dev", 1))]
    else:
        phit, weights, hpad, atom_rows = turned_basis(masked)
        pieces = [lax.all_gather(masked, "dev", axis=0)]

    density, terms = pl.pallas_call(
        density_kernel,
        out_shape=(
            pltpu.VMEM((batches, points), f32),
            pltpu.VMEM((ROWS, LANES), f32),
        ),
        in_specs=[SMEM] * 3 + [VMEM] * (4 + len(pieces)),
        out_specs=(VMEM, VMEM),
        scratch_shapes=[
            pltpu.VMEM((dev_count, band, width, width), bf16),
            pltpu.VMEM((LANES // SLOT, SLOT, points), f32),
        ],
        compiler_params=PARAMS,
        cost_estimate=pl.CostEstimate(flops=2_000_000_000, bytes_accessed=6_000_000, transcendentals=0),
        name="density",
    )(
        window_start, batch_offsets, batch_sizes, atom_rows, phit, weights, hpad,
        *pieces,
    )

    if dev_count == 8:
        both = jnp.stack([terms, crossed(terms, "dev", 1)])
        groups = [both] + [crossed(both, "dev", m) for m in (2, 4, 6)]
    else:
        groups = [lax.all_gather(terms, "dev", axis=0)]
    g_low = field(0, groups[0])
    *groups, g_low = lax.optimization_barrier((*groups, g_low))
    flip = region_count == 4
    own, near_a, near_b, far = pl.pallas_call(
        functools.partial(scatter_kernel, comps, atoms, flip),
        out_shape=tuple(jax.ShapeDtypeStruct((ROWS, n * atoms), f32) for n in (3, 2, 2, 2)),
        in_specs=[VMEM] * len(groups),
        out_specs=(VMEM,) * 4,
        compiler_params=PARAMS,
        name="scatter",
    )(*groups)
    g_high = field(half, own)
    if flip:
        near_b = crossed(near_b, "region", 3)
        far_a = far_b = crossed(far, "region", 2)
        near_a = crossed(near_a, "region", 1)
    else:
        far_a = shifted(far, "region", 2)
        far_b = shifted(far, "region", -2)
        near_a = shifted(near_a, "region", 1)
        near_b = shifted(near_b, "region", -1)

    near_b, far_a, far_b, near_a, g_high = lax.optimization_barrier(
        (near_b, far_a, far_b, near_a, g_high)
    )

    moments, potential = pl.pallas_call(
        functools.partial(potential_kernel, comps, atoms, flip),
        out_shape=(
            jax.ShapeDtypeStruct((mine, comps), f32),
            jax.ShapeDtypeStruct((batches, points), f32),
        ),
        in_specs=[SMEM] + [VMEM] * 8,
        out_specs=(VMEM, VMEM),
        compiler_params=PARAMS,
        name="potential",
    )(batch_sizes, own, near_b, far_a, far_b, near_a, atom_rows, g_low, g_high)
    return (density, moments.T, potential)


def solution(mesh):
    both = ("region", "dev")
    placed = (
        P(both, None, None, None),
        P(both, None, None, None),
        P(both, None),
        P(both),
        P(both, None),
        P(both, None),
        P(both, None),
        P(both, None, None, None),
        P(both, None, None),
        P(both, None, None),
        P(),
    )
    return jax.shard_map(
        per_device,
        mesh=mesh,
        in_specs=placed,
        out_specs=(P(both, None), P(None, both), P(both, None)),
        check_vma=False,
    )
```

```python
import functools
import jax
import jax.numpy as jnp
from jax import lax
from jax.experimental import pallas as pl
from jax.experimental.pallas import tpu as pltpu
from jax.sharding import PartitionSpec as P

EVEN_OWNERS = (0, 1, 4, 3, 2, 5, 6, 7)
ODD_OWNERS = (0, 1, 2, 5, 4, 3, 6, 7)
PIECE_ROWS = (None, None, None, None, 0, 1, 0, 1)
LANES = 128
ROWS = 32
SLOT = 8
NT = (((1,), (1,)), ((), ()))
NN = (((1,), (0,)), ((), ()))
VMEM = pl.BlockSpec(memory_space=pltpu.VMEM)
SMEM = pl.BlockSpec(memory_space=pltpu.SMEM)
HBM = pl.BlockSpec(memory_space=pltpu.HBM)
WIDE = pltpu.CompilerParams(vmem_limit_bytes=16 * 1024 * 1024)
PARAMS = pltpu.CompilerParams(vmem_limit_bytes=16 * 1024 * 1024)


def dot(a, b, dims=NN):
    return lax.dot_general(a, b, dims, preferred_element_type=jnp.float32)


def split2(x):
    hi = x.astype(jnp.bfloat16)
    lo = (x - hi.astype(jnp.float32)).astype(jnp.bfloat16)
    return hi, lo


def split3(x):
    hi, mid = split2(x)
    rest = x - hi.astype(jnp.float32) - mid.astype(jnp.float32)
    return hi, mid, rest.astype(jnp.bfloat16)


def cubic(distance):
    inner = 2.0 / 3.0 - distance * distance + 0.5 * distance * distance * distance
    remote = 2.0 - distance
    outer = remote * remote * remote * (1.0 / 6.0)
    return jnp.where(distance < 1.0, inner, jnp.where(distance < 2.0, outer, 0.0))


def chosen_row(owner, start, owners, stored):
    ahead = lax.rem(owner - start + stored * owners, owners)
    return ahead, lax.rem(start + ahead, stored * owners) // owners


def select_kernel(even, odd, owners, starts_ref, rows_ref, out_ref):
    me = lax.axis_index("dev")
    owner = lax.bitwise_xor(me, jnp.where(lax.rem(me, 2) == 1, odd, even))
    for n in range(out_ref.shape[0]):
        row = chosen_row(owner, starts_ref[n], owners, rows_ref.shape[0])[1]
        out_ref[n] = rows_ref[row]


def mask_kernel(mask_hbm, rows_hbm, out_ref, mask, rows, sems):
    stored, band = rows.shape[:2]
    fetch = pltpu.make_async_copy(mask_hbm, mask, sems.at[stored])
    copies = [
        pltpu.make_async_copy(rows_hbm.at[t], rows.at[t], sems.at[t]) for t in range(stored)
    ]
    fetch.start()
    for copy in copies:
        copy.start()
    fetch.wait()
    factors = mask[...].astype(jnp.float32)
    for t, copy in enumerate(copies):
        copy.wait()
        for k in range(band):
            factor = jnp.broadcast_to(factors[t : t + 1, k : k + 1], rows.shape[2:])
            out_ref[t, k] = rows[t, k] * factor.astype(jnp.bfloat16)


def field_kernel(
    begin, after_hbm, alive_ref, table_hbm, radius_hbm, harm_hbm,
    g_ref, table_ref, radius_ref, harm_ref, sems,
):
    batches, near, comps, points = harm_ref.shape
    knots = table_ref.shape[0]
    span = pl.ds(begin, batches)
    moves = (
        (table_hbm, table_ref), (radius_hbm.at[span], radius_ref), (harm_hbm.at[span], harm_ref)
    )
    copies = [pltpu.make_async_copy(a, b, sems.at[n]) for n, (a, b) in enumerate(moves)]
    for copy in copies:
        copy.start()
    knot = lax.broadcasted_iota(jnp.int32, (knots, points), 0).astype(jnp.float32)
    for copy in copies:
        copy.wait()
    r_hi, r_lo = split2(table_ref[...].T)
    coeffs = jnp.concatenate([r_hi, r_hi, r_lo], axis=1)

    def body(b, carry):
        rows = radius_ref[b]
        alive = alive_ref[pl.ds(begin + b, 1), :]
        for i in range(near):
            spline = cubic(jnp.abs(rows[i : i + 1, :] - knot))
            s_hi, s_lo = split2(spline)
            radial = dot(coeffs, jnp.concatenate([s_hi, s_lo, s_hi], axis=0))
            g_ref[b * near + i] = radial * (harm_ref[b, i].astype(jnp.float32) * alive)
        return carry

    lax.fori_loop(0, batches, body, 0, unroll=2)


def turn_kernel(
    after_hbm, near_ref, size_ref, basis_hbm, part_hbm, harm_hbm,
    phit_ref, part_ref, hpad_ref, atom_ref, alive_ref, basis, harm_ref, sems,
):
    batches, near_blocks = basis.shape[:2]
    near, comps, points = harm_ref.shape[1:]
    halves = [pl.ds(0, batches // 2), pl.ds(batches // 2, batches - batches // 2)]
    copies = [
        pltpu.make_async_copy(basis_hbm.at[half], basis.at[half], sems.at[n])
        for n, half in enumerate(halves)
    ]
    copies.append(pltpu.make_async_copy(harm_hbm, harm_ref, sems.at[2]))
    copies.append(pltpu.make_async_copy(part_hbm, part_ref, sems.at[3]))
    for copy in copies:
        copy.start()
    lane = lax.broadcasted_iota(jnp.int32, atom_ref.shape, 1)
    atom = jnp.full(atom_ref.shape, -1, jnp.int32)
    for b in range(near_ref.shape[1]):
        for i in range(near):
            atom = jnp.where(lane == b * SLOT + i, near_ref[i, b], atom)
    atom_ref[...] = atom
    point = lax.broadcasted_iota(jnp.int32, (1, points), 1)
    for b in range(batches):
        alive_ref[b : b + 1, :] = (point < size_ref[0, b]).astype(jnp.float32)
    for n in range(batches * near):
        hpad_ref[n, ROWS // 2 :, :] = jnp.zeros((ROWS // 2, points), jnp.bfloat16)

    def turn(b, carry):
        for j in range(near_blocks):
            phit_ref[b, j] = basis[b, j].T
        return carry

    def pad(b, carry):
        for i in range(near):
            hpad_ref[b * near + i, 0:comps, :] = harm_ref[b, i]
        return carry

    copies[0].wait()
    lax.fori_loop(0, batches // 2, turn, 0)
    copies[1].wait()
    lax.fori_loop(batches // 2, batches, turn, 0)
    copies[2].wait()
    lax.fori_loop(0, batches, pad, 0)
    copies[3].wait()


def density_kernel(
    start_ref, offset_ref, atom_ref, alive_ref, phit_ref, part_ref, hpad_ref, *refs
):
    dens_ref, terms_ref, window_ref, w_ref = refs[-4:]
    pieces = refs[:-4]
    owners = window_ref.shape[0]
    batches, near_blocks, width, points = phit_ref.shape
    near = part_ref.shape[1]
    if len(pieces) == owners:
        me = lax.axis_index("dev")
        odd = lax.rem(me, 2) == 1
        held = [
            (piece, lax.bitwise_xor(me, jnp.where(odd, b, a)), at)
            for piece, a, b, at in zip(pieces, EVEN_OWNERS, ODD_OWNERS, PIECE_ROWS)
        ]
    else:
        held = [(pieces[0].at[owner], owner, None) for owner in range(owners)]
    stored = held[0][0].shape[0]
    for piece, owner, at in held:
        ahead, row = chosen_row(owner, start_ref[0], owners, stored)
        window_ref[ahead] = piece[row if at is None else at]
    w_ref[...] = jnp.zeros(w_ref.shape, w_ref.dtype)
    zero = jnp.zeros((width, width), jnp.bfloat16)

    def body(b, carry):
        first = offset_ref[0, b]
        left = []
        for j in range(near_blocks):
            row = [
                window_ref[first + j, f - j + 1] if 0 <= f - j + 1 < 4 else zero
                for f in range(near_blocks)
            ]
            left.append(jnp.concatenate(row, axis=1))
        right = phit_ref[b].reshape(near_blocks * width, points)
        mixed = dot(jnp.concatenate(left, axis=0), right)
        total = jnp.zeros((width, points), jnp.float32)
        for j in range(near_blocks):
            part = mixed[j * width : (j + 1) * width]
            total = total + part * phit_ref[b, j].astype(jnp.float32)
        summed = jnp.sum(total, axis=0, keepdims=True)
        row = summed * alive_ref[pl.ds(b, 1), :]
        dens_ref[pl.ds(b, 1), :] = row
        w_ref[b, 0:near, :] = part_ref[b] * row
        return carry

    for b in range(batches):
        body(b, 0)
    weights = w_ref[...].reshape(LANES, points)
    columns = jnp.concatenate(split2(weights), axis=0)
    slot = lax.broadcasted_iota(jnp.int32, (1, 2 * LANES), 1) % LANES
    terms = jnp.zeros((ROWS, 2 * LANES), jnp.float32)
    cross = dot(hpad_ref[...].reshape(batches * near * ROWS, points), columns, NT)
    for n in range(batches * near):
        b, i = divmod(n, near)
        here = cross[n * ROWS : (n + 1) * ROWS]
        terms = terms + jnp.where(slot == b * SLOT + i, here, 0.0)
    result = terms[:, :LANES] + terms[:, LANES:]
    row_id = lax.broadcasted_iota(jnp.int32, (ROWS, LANES), 0)
    comps = ROWS - 7
    terms_ref[...] = jnp.where(row_id == comps, atom_ref[...].astype(jnp.float32), result)


def scatter_kernel(comps, atoms, flip, *refs):
    own, near_a, near_b, far = refs[-4:]
    pieces = [group.at[m] for group in refs[:-4] for m in range(group.shape[0])]
    row_id = lax.broadcasted_iota(jnp.int32, (3 * atoms, LANES), 0)
    total = jnp.zeros((3 * ROWS, 3 * atoms), jnp.float32)
    for m in range(0, len(pieces), 2):
        left, right = [], []
        for values in (pieces[m][...], pieces[m + 1][...]):
            chosen = values[comps : comps + 1, :].astype(jnp.int32)
            right.append((row_id == chosen).astype(jnp.float32).astype(jnp.bfloat16))
            left.append(jnp.concatenate(split3(values), axis=0))
        total = total + dot(jnp.concatenate(left, axis=1), jnp.concatenate(right, axis=1), NT)
    sums = total[:ROWS] + total[ROWS : 2 * ROWS] + total[2 * ROWS :]
    own[...] = sums
    ahead, back = sums[:, atoms:], sums[:, : 2 * atoms]
    if flip:
        odd = lax.rem(lax.axis_index("region"), 2) == 1
        near_a[...] = jnp.where(odd, back, ahead)
        near_b[...] = jnp.where(odd, ahead, back)
    else:
        near_a[...] = ahead
        near_b[...] = back
    far[:, :atoms] = sums[:, :atoms]
    far[:, atoms:] = sums[:, 2 * atoms :]


def potential_kernel(
    comps, atoms, flip, own_ref, near_b_ref, fa_ref, fb_ref, near_a_ref, atom_ref,
    low_ref, high_ref, mom_ref, pot_ref,
):
    batches, points = pot_ref.shape
    near = 2 * low_ref.shape[0] // batches
    fields = [ref.at[n] for ref in (low_ref, high_ref) for n in range(ref.shape[0])]
    own = own_ref[...]
    near_a, near_b = near_a_ref[...], near_b_ref[...]
    if flip:
        odd = lax.rem(lax.axis_index("region"), 2) == 1
        low = jnp.where(odd, near_a, near_b)
        high = jnp.where(odd, near_b, near_a)
    else:
        low, high = near_a, near_b
    before = fa_ref[:, atoms:] + low[:, :atoms] + own[:, :atoms]
    here = low[:, atoms:] + own[:, atoms : 2 * atoms] + high[:, :atoms]
    after = own[:, 2 * atoms :] + high[:, atoms:] + fb_ref[:, :atoms]

    mine = mom_ref.shape[0]
    want = lax.broadcasted_iota(jnp.int32, (mine, atoms), 0) + lax.axis_index("dev") * mine
    keep = want == lax.broadcasted_iota(jnp.int32, (mine, atoms), 1)
    keep = keep.astype(jnp.float32).astype(jnp.bfloat16)
    taken = dot(keep, jnp.concatenate(split3(here), axis=0), NT)
    taken = taken[:, :ROWS] + taken[:, ROWS : 2 * ROWS] + taken[:, 2 * ROWS :]
    mom_ref[...] = taken[:, :comps]

    moments = jnp.concatenate([before, here, after], axis=1)
    row_id = lax.broadcasted_iota(jnp.int32, (3 * atoms, LANES), 0)
    pick = (row_id == atom_ref[...]).astype(jnp.float32).astype(jnp.bfloat16)
    got = dot(jnp.concatenate(split3(moments), axis=0), pick)
    chosen = got[:ROWS] + got[ROWS : 2 * ROWS] + got[2 * ROWS :]
    chosen = chosen[:comps]
    for b in range(batches):
        total = jnp.zeros((comps, points), jnp.float32)
        for i in range(near):
            column = chosen[:, b * SLOT + i : b * SLOT + i + 1]
            total = total + column * fields[b * near + i][...]
        pot_ref[b : b + 1, :] = jnp.sum(total, axis=0, keepdims=True)


def held_in_hbm(*values):
    return [pltpu.with_memory_space_constraint(value, pltpu.HBM) for value in values]


def crossed(value, axis, m):
    return lax.ppermute(value, axis, [(i, i ^ m) for i in range(lax.axis_size(axis))])


def turned(value, even, odd):
    count = lax.axis_size("dev")
    return lax.ppermute(value, "dev", [(i, i ^ (odd if i % 2 else even)) for i in range(count)])


def shifted(value, axis, step):
    count = lax.axis_size(axis)
    return lax.ppermute(value, axis, [(i, (i + step) % count) for i in range(count)])


def per_device(
    basis_values,
    density_rows,
    block_mask,
    window_start,
    batch_offsets,
    batch_sizes,
    atom_near,
    harmonics,
    partition,
    radius,
    radial_table,
):
    dev_count = lax.axis_size("dev")
    region_count = lax.axis_size("region")
    blocks_dev, band, width = density_rows.shape[:3]
    batches, near, comps, points = harmonics.shape
    near_blocks = basis_values.shape[1]
    mine = 16
    atoms = mine * dev_count
    f32, bf16 = jnp.float32, jnp.bfloat16

    work = pl.CostEstimate(flops=2_000_000_000, bytes_accessed=8_000_000, transcendentals=0)
    masked = pl.pallas_call(
        mask_kernel,
        out_shape=pltpu.VMEM(density_rows.shape, bf16),
        in_specs=[HBM, HBM],
        out_specs=VMEM,
        scratch_shapes=[
            pltpu.VMEM(block_mask.shape, jnp.int32),
            pltpu.VMEM(density_rows.shape, bf16),
            pltpu.SemaphoreType.DMA((blocks_dev + 1,)),
        ],
        compiler_params=PARAMS,
        cost_estimate=work,
        name="mask",
    )(*held_in_hbm(block_mask, density_rows))

    half = batches // 2

    def field(begin, after):
        return pl.pallas_call(
            functools.partial(field_kernel, begin),
            out_shape=pltpu.VMEM((half * near, comps, points), f32),
            in_specs=[HBM, VMEM] + [HBM] * 3,
            out_specs=VMEM,
            scratch_shapes=[
                pltpu.VMEM(radial_table.shape[::-1], f32),
                pltpu.VMEM((half,) + radius.shape[1:], f32),
                pltpu.VMEM((half,) + harmonics.shape[1:], bf16),
                pltpu.SemaphoreType.DMA((3,)),
            ],
            compiler_params=WIDE,
            cost_estimate=work,
            name="field",
        )(after, alive, *held_in_hbm(radial_table.T, radius, harmonics))

    def turned_basis(after):
        return pl.pallas_call(
            turn_kernel,
            out_shape=(
                pltpu.VMEM((batches, near_blocks, width, points), bf16),
                pltpu.VMEM(partition.shape, f32),
                pltpu.VMEM((batches * near, ROWS, points), bf16),
                pltpu.VMEM((1, LANES), jnp.int32),
                pltpu.VMEM((batches, points), f32),
            ),
            in_specs=[HBM, SMEM, SMEM] + [HBM] * 3,
            out_specs=(VMEM,) * 5,
            scratch_shapes=[
                pltpu.VMEM(basis_values.shape, bf16),
                pltpu.VMEM(harmonics.shape, bf16),
                pltpu.SemaphoreType.DMA((4,)),
            ],
            compiler_params=WIDE,
            cost_estimate=work,
            name="turn",
        )(after, atom_near.T, batch_sizes, *held_in_hbm(basis_values, partition, harmonics))

    def selected(even, odd, starts, rows):
        return pl.pallas_call(
            functools.partial(select_kernel, even, odd, dev_count),
            out_shape=pltpu.VMEM((2,) + density_rows.shape[1:], bf16),
            in_specs=[SMEM, VMEM],
            out_specs=VMEM,
            compiler_params=PARAMS,
            name="select",
        )(starts, rows)

    if dev_count == 8:
        beside = crossed(window_start, "dev", 1)
        beside, rows = lax.optimization_barrier((beside, masked))
        first = turned(rows, 4, 2)
        starts = turned(jnp.concatenate([window_start, beside]), 2, 4)
        chosen = selected(0, 0, starts, masked)
        second = turned(chosen, 2, 4)
        first, later, _ = lax.optimization_barrier((first, masked, chosen))
        chosen = selected(4, 2, starts, first)
        third = turned(chosen, 2, 4)
        phit, weights, hpad, atom_rows, alive = turned_basis(chosen)
        second, phit = lax.optimization_barrier((second, phit))
        sent = (later, first, second, third)
        pieces = [piece for value in sent for piece in (value, crossed(value, "dev", 1))]
    else:
        phit, weights, hpad, atom_rows, alive = turned_basis(masked)
        pieces = [lax.all_gather(masked, "dev", axis=0)]

    density, terms = pl.pallas_call(
        density_kernel,
        out_shape=(
            pltpu.VMEM((batches, points), f32),
            pltpu.VMEM((ROWS, LANES), f32),
        ),
        in_specs=[SMEM] * 2 + [VMEM] * (5 + len(pieces)),
        out_specs=(VMEM, VMEM),
        scratch_shapes=[
            pltpu.VMEM((dev_count, band, width, width), bf16),
            pltpu.VMEM((LANES // SLOT, SLOT, points), f32),
        ],
        compiler_params=PARAMS,
        cost_estimate=pl.CostEstimate(flops=2_000_000_000, bytes_accessed=6_000_000, transcendentals=0),
        name="density",
    )(
        window_start, batch_offsets, atom_rows, alive, phit, weights, hpad,
        *pieces,
    )

    if dev_count == 8:
        both = jnp.stack([terms, crossed(terms, "dev", 1)])
        groups = [both] + [crossed(both, "dev", m) for m in (2, 4, 6)]
    else:
        groups = [lax.all_gather(terms, "dev", axis=0)]
    g_low = field(0, groups[0])
    *groups, g_low = lax.optimization_barrier((*groups, g_low))
    flip = region_count == 4
    own, near_a, near_b, far = pl.pallas_call(
        functools.partial(scatter_kernel, comps, atoms, flip),
        out_shape=tuple(jax.ShapeDtypeStruct((ROWS, n * atoms), f32) for n in (3, 2, 2, 2)),
        in_specs=[VMEM] * len(groups),
        out_specs=(VMEM,) * 4,
        compiler_params=PARAMS,
        name="scatter",
    )(*groups)
    g_high = field(half, own)
    if flip:
        near_b = crossed(near_b, "region", 3)
        far_a = far_b = crossed(far, "region", 2)
        near_a = crossed(near_a, "region", 1)
    else:
        far_a = shifted(far, "region", 2)
        far_b = shifted(far, "region", -2)
        near_a = shifted(near_a, "region", 1)
        near_b = shifted(near_b, "region", -1)

    near_b, far_a, far_b, near_a, g_high = lax.optimization_barrier(
        (near_b, far_a, far_b, near_a, g_high)
    )

    moments, potential = pl.pallas_call(
        functools.partial(potential_kernel, comps, atoms, flip),
        out_shape=(
            jax.ShapeDtypeStruct((mine, comps), f32),
            jax.ShapeDtypeStruct((batches, points), f32),
        ),
        in_specs=[VMEM] * 8,
        out_specs=(VMEM, VMEM),
        compiler_params=PARAMS,
        name="potential",
    )(own, near_b, far_a, far_b, near_a, atom_rows, g_low, g_high)
    return (density, moments.T, potential)


def solution(mesh):
    both = ("region", "dev")
    placed = (
        P(both, None, None, None),
        P(both, None, None, None),
        P(both, None),
        P(both),
        P(both, None),
        P(both, None),
        P(both, None),
        P(both, None, None, None),
        P(both, None, None),
        P(both, None, None),
        P(),
    )
    return jax.shard_map(
        per_device,
        mesh=mesh,
        in_specs=placed,
        out_specs=(P(both, None), P(None, both), P(both, None)),
        check_vma=False,
    )
```

```python
import functools
import jax
import jax.numpy as jnp
from jax import lax
from jax.experimental import pallas as pl
from jax.experimental.pallas import tpu as pltpu
from jax.sharding import PartitionSpec as P

EVEN_OWNERS = (0, 1, 4, 3, 2, 5, 6, 7)
ODD_OWNERS = (0, 1, 2, 5, 4, 3, 6, 7)
PIECE_ROWS = (None, None, None, None, 0, 1, 0, 1)
LANES = 128
ROWS = 32
SLOT = 8
NT = (((1,), (1,)), ((), ()))
NN = (((1,), (0,)), ((), ()))
VMEM = pl.BlockSpec(memory_space=pltpu.VMEM)
SMEM = pl.BlockSpec(memory_space=pltpu.SMEM)
HBM = pl.BlockSpec(memory_space=pltpu.HBM)
WIDE = pltpu.CompilerParams(vmem_limit_bytes=16 * 1024 * 1024)
PARAMS = pltpu.CompilerParams(vmem_limit_bytes=16 * 1024 * 1024)


def dot(a, b, dims=NN):
    return lax.dot_general(a, b, dims, preferred_element_type=jnp.float32)


def split2(x):
    hi = x.astype(jnp.bfloat16)
    lo = (x - hi.astype(jnp.float32)).astype(jnp.bfloat16)
    return hi, lo


def split3(x):
    hi, mid = split2(x)
    rest = x - hi.astype(jnp.float32) - mid.astype(jnp.float32)
    return hi, mid, rest.astype(jnp.bfloat16)


def cubic(distance):
    inner = 2.0 / 3.0 - distance * distance + 0.5 * distance * distance * distance
    remote = 2.0 - distance
    outer = remote * remote * remote * (1.0 / 6.0)
    return jnp.where(distance < 1.0, inner, jnp.where(distance < 2.0, outer, 0.0))


def chosen_row(owner, start, owners, stored):
    ahead = lax.rem(owner - start + stored * owners, owners)
    return ahead, lax.rem(start + ahead, stored * owners) // owners


def select_kernel(even, odd, owners, starts_ref, rows_ref, out_ref):
    me = lax.axis_index("dev")
    owner = lax.bitwise_xor(me, jnp.where(lax.rem(me, 2) == 1, odd, even))
    for n in range(out_ref.shape[0]):
        row = chosen_row(owner, starts_ref[n], owners, rows_ref.shape[0])[1]
        out_ref[n] = rows_ref[row]


def mask_kernel(mask_hbm, rows_hbm, out_ref, mask, rows, sems):
    stored, band = rows.shape[:2]
    fetch = pltpu.make_async_copy(mask_hbm, mask, sems.at[stored])
    copies = [
        pltpu.make_async_copy(rows_hbm.at[t], rows.at[t], sems.at[t]) for t in range(stored)
    ]
    fetch.start()
    for copy in copies:
        copy.start()
    fetch.wait()
    factors = mask[...].astype(jnp.float32)
    for t, copy in enumerate(copies):
        copy.wait()
        for k in range(band):
            factor = jnp.broadcast_to(factors[t : t + 1, k : k + 1], rows.shape[2:])
            out_ref[t, k] = rows[t, k] * factor.astype(jnp.bfloat16)


def field_kernel(
    begin, after_hbm, alive_ref, table_hbm, radius_hbm, harm_hbm,
    g_ref, table_ref, radius_ref, harm_ref, sems,
):
    batches, near, comps, points = harm_ref.shape
    knots = table_ref.shape[0]
    span = pl.ds(begin, batches)
    moves = (
        (table_hbm, table_ref), (radius_hbm.at[span], radius_ref), (harm_hbm.at[span], harm_ref)
    )
    copies = [pltpu.make_async_copy(a, b, sems.at[n]) for n, (a, b) in enumerate(moves)]
    for copy in copies:
        copy.start()
    knot = lax.broadcasted_iota(jnp.int32, (knots, points), 0).astype(jnp.float32)
    for copy in copies:
        copy.wait()
    r_hi, r_lo = split2(table_ref[...].T)
    coeffs = jnp.concatenate([r_hi, r_hi, r_lo], axis=1)

    def body(b, carry):
        rows = radius_ref[b]
        alive = alive_ref[pl.ds(begin + b, 1), :]
        for i in range(near):
            spline = cubic(jnp.abs(rows[i : i + 1, :] - knot))
            s_hi, s_lo = split2(spline)
            radial = dot(coeffs, jnp.concatenate([s_hi, s_lo, s_hi], axis=0))
            g_ref[b * near + i] = radial * (harm_ref[b, i].astype(jnp.float32) * alive)
        return carry

    lax.fori_loop(0, batches, body, 0, unroll=2)


def turn_kernel(
    after_hbm, near_ref, size_ref, start_ref, offset_ref, basis_hbm, part_hbm, harm_hbm,
    phit_ref, part_ref, hpad_ref, atom_ref, alive_ref, place_ref, basis, harm_ref, sems,
):
    batches, near_blocks = basis.shape[:2]
    near, comps, points = harm_ref.shape[1:]
    halves = [pl.ds(0, batches // 2), pl.ds(batches // 2, batches - batches // 2)]
    copies = [
        pltpu.make_async_copy(basis_hbm.at[half], basis.at[half], sems.at[n])
        for n, half in enumerate(halves)
    ]
    copies.append(pltpu.make_async_copy(harm_hbm, harm_ref, sems.at[2]))
    copies.append(pltpu.make_async_copy(part_hbm, part_ref, sems.at[3]))
    for copy in copies:
        copy.start()
    lane = lax.broadcasted_iota(jnp.int32, atom_ref.shape, 1)
    atom = jnp.full(atom_ref.shape, -1, jnp.int32)
    for b in range(near_ref.shape[1]):
        for i in range(near):
            atom = jnp.where(lane == b * SLOT + i, near_ref[i, b], atom)
    atom_ref[...] = atom
    place = jnp.full(place_ref.shape, start_ref[0], jnp.int32)
    for b in range(batches):
        place = jnp.where(lane == b + 1, offset_ref[0, b], place)
    place_ref[...] = place
    point = lax.broadcasted_iota(jnp.int32, (1, points), 1)
    for b in range(batches):
        alive_ref[b : b + 1, :] = (point < size_ref[0, b]).astype(jnp.float32)
    for n in range(batches * near):
        hpad_ref[n, ROWS // 2 :, :] = jnp.zeros((ROWS // 2, points), jnp.bfloat16)

    def turn(b, carry):
        for j in range(near_blocks):
            phit_ref[b, j] = basis[b, j].T
        return carry

    def pad(b, carry):
        for i in range(near):
            hpad_ref[b * near + i, 0:comps, :] = harm_ref[b, i]
        return carry

    copies[0].wait()
    lax.fori_loop(0, batches // 2, turn, 0)
    copies[1].wait()
    lax.fori_loop(batches // 2, batches, turn, 0)
    copies[2].wait()
    lax.fori_loop(0, batches, pad, 0)
    copies[3].wait()


def density_kernel(
    place_ref, atom_ref, alive_ref, phit_ref, part_ref, hpad_ref, *refs
):
    dens_ref, terms_ref, window_ref, w_ref = refs[-4:]
    pieces = refs[:-4]
    owners = window_ref.shape[0]
    batches, near_blocks, width, points = phit_ref.shape
    near = part_ref.shape[1]
    if len(pieces) == owners:
        me = lax.axis_index("dev")
        odd = lax.rem(me, 2) == 1
        held = [
            (piece, lax.bitwise_xor(me, jnp.where(odd, b, a)), at)
            for piece, a, b, at in zip(pieces, EVEN_OWNERS, ODD_OWNERS, PIECE_ROWS)
        ]
    else:
        held = [(pieces[0].at[owner], owner, None) for owner in range(owners)]
    stored = held[0][0].shape[0]
    for piece, owner, at in held:
        ahead, row = chosen_row(owner, place_ref[0, 0], owners, stored)
        window_ref[ahead] = piece[row if at is None else at]
    w_ref[...] = jnp.zeros(w_ref.shape, w_ref.dtype)
    zero = jnp.zeros((width, width), jnp.bfloat16)

    def body(b, carry):
        first = place_ref[0, b + 1]
        left = []
        for j in range(near_blocks):
            row = [
                window_ref[first + j, f - j + 1] if 0 <= f - j + 1 < 4 else zero
                for f in range(near_blocks)
            ]
            left.append(jnp.concatenate(row, axis=1))
        right = phit_ref[b].reshape(near_blocks * width, points)
        mixed = dot(jnp.concatenate(left, axis=0), right)
        total = jnp.zeros((width, points), jnp.float32)
        for j in range(near_blocks):
            part = mixed[j * width : (j + 1) * width]
            total = total + part * phit_ref[b, j].astype(jnp.float32)
        summed = jnp.sum(total, axis=0, keepdims=True)
        row = summed * alive_ref[pl.ds(b, 1), :]
        dens_ref[pl.ds(b, 1), :] = row
        w_ref[b, 0:near, :] = part_ref[b] * row
        return carry

    for b in range(batches):
        body(b, 0)
    weights = w_ref[...].reshape(LANES, points)
    columns = jnp.concatenate(split2(weights), axis=0)
    slot = lax.broadcasted_iota(jnp.int32, (1, 2 * LANES), 1) % LANES
    terms = jnp.zeros((ROWS, 2 * LANES), jnp.float32)
    cross = dot(hpad_ref[...].reshape(batches * near * ROWS, points), columns, NT)
    for n in range(batches * near):
        b, i = divmod(n, near)
        here = cross[n * ROWS : (n + 1) * ROWS]
        terms = terms + jnp.where(slot == b * SLOT + i, here, 0.0)
    result = terms[:, :LANES] + terms[:, LANES:]
    row_id = lax.broadcasted_iota(jnp.int32, (ROWS, LANES), 0)
    comps = ROWS - 7
    terms_ref[...] = jnp.where(row_id == comps, atom_ref[...].astype(jnp.float32), result)


def scatter_kernel(comps, atoms, steps, *refs):
    pieces, sums = refs[:-1], refs[-1]
    row_id = lax.broadcasted_iota(jnp.int32, (3 * atoms, LANES), 0)
    region = lax.axis_index("region")
    total = jnp.zeros((3 * ROWS, 3 * atoms), jnp.float32)
    for n in range(0, len(pieces), 2):
        left, right = [], []
        for piece, step in zip(pieces[n : n + 2], steps[n : n + 2]):
            values = piece[...]
            chosen = values[comps : comps + 1, :].astype(jnp.int32)
            if step:
                away = lax.rem(lax.bitwise_xor(region, step) - region + 4, 4)
                chosen = lax.rem(chosen + away * atoms, 4 * atoms)
            right.append((row_id == chosen).astype(jnp.float32).astype(jnp.bfloat16))
            left.append(jnp.concatenate(split3(values), axis=0))
        total = total + dot(jnp.concatenate(left, axis=1), jnp.concatenate(right, axis=1), NT)
    sums[...] = total[:ROWS] + total[ROWS : 2 * ROWS] + total[2 * ROWS :]


def potential_kernel(comps, atoms, atom_ref, low_ref, high_ref, *refs):
    mom_ref, pot_ref = refs[-2:]
    batches, points = pot_ref.shape
    near = 2 * low_ref.shape[0] // batches
    fields = [ref.at[n] for ref in (low_ref, high_ref) for n in range(ref.shape[0])]
    moments = refs[0][...]
    for ref in refs[1:-2]:
        moments = moments + ref[...]
    parts = jnp.concatenate(split3(moments), axis=0)

    mine = mom_ref.shape[0]
    want = lax.broadcasted_iota(jnp.int32, (mine, atoms), 0) + lax.axis_index("dev") * mine
    keep = want == lax.broadcasted_iota(jnp.int32, (mine, atoms), 1)
    keep = keep.astype(jnp.float32).astype(jnp.bfloat16)
    taken = dot(keep, parts[:, atoms : 2 * atoms], NT)
    taken = taken[:, :ROWS] + taken[:, ROWS : 2 * ROWS] + taken[:, 2 * ROWS :]
    mom_ref[...] = taken[:, :comps]

    row_id = lax.broadcasted_iota(jnp.int32, (3 * atoms, LANES), 0)
    pick = (row_id == atom_ref[...]).astype(jnp.float32).astype(jnp.bfloat16)
    got = dot(parts, pick)
    chosen = got[:ROWS] + got[ROWS : 2 * ROWS] + got[2 * ROWS :]
    chosen = chosen[:comps]
    for b in range(batches):
        total = jnp.zeros((comps, points), jnp.float32)
        for i in range(near):
            column = chosen[:, b * SLOT + i : b * SLOT + i + 1]
            total = total + column * fields[b * near + i][...]
        pot_ref[b : b + 1, :] = jnp.sum(total, axis=0, keepdims=True)


def held_in_hbm(*values):
    return [pltpu.with_memory_space_constraint(value, pltpu.HBM) for value in values]


def crossed(value, axis, m):
    return lax.ppermute(value, axis, [(i, i ^ m) for i in range(lax.axis_size(axis))])


def turned(value, even, odd):
    count = lax.axis_size("dev")
    return lax.ppermute(value, "dev", [(i, i ^ (odd if i % 2 else even)) for i in range(count)])


def shifted(value, axis, step):
    count = lax.axis_size(axis)
    return lax.ppermute(value, axis, [(i, (i + step) % count) for i in range(count)])


def per_device(
    basis_values,
    density_rows,
    block_mask,
    window_start,
    batch_offsets,
    batch_sizes,
    atom_near,
    harmonics,
    partition,
    radius,
    radial_table,
):
    dev_count = lax.axis_size("dev")
    region_count = lax.axis_size("region")
    blocks_dev, band, width = density_rows.shape[:3]
    batches, near, comps, points = harmonics.shape
    near_blocks = basis_values.shape[1]
    mine = 16
    atoms = mine * dev_count
    f32, bf16 = jnp.float32, jnp.bfloat16

    work = pl.CostEstimate(flops=2_000_000_000, bytes_accessed=8_000_000, transcendentals=0)
    masked = pl.pallas_call(
        mask_kernel,
        out_shape=pltpu.VMEM(density_rows.shape, bf16),
        in_specs=[HBM, HBM],
        out_specs=VMEM,
        scratch_shapes=[
            pltpu.VMEM(block_mask.shape, jnp.int32),
            pltpu.VMEM(density_rows.shape, bf16),
            pltpu.SemaphoreType.DMA((blocks_dev + 1,)),
        ],
        compiler_params=PARAMS,
        cost_estimate=work,
        name="mask",
    )(*held_in_hbm(block_mask, density_rows))

    half = batches // 2

    def field(begin, after):
        return pl.pallas_call(
            functools.partial(field_kernel, begin),
            out_shape=pltpu.VMEM((half * near, comps, points), f32),
            in_specs=[HBM, VMEM] + [HBM] * 3,
            out_specs=VMEM,
            scratch_shapes=[
                pltpu.VMEM(radial_table.shape[::-1], f32),
                pltpu.VMEM((half,) + radius.shape[1:], f32),
                pltpu.VMEM((half,) + harmonics.shape[1:], bf16),
                pltpu.SemaphoreType.DMA((3,)),
            ],
            compiler_params=WIDE,
            cost_estimate=work,
            name="field",
        )(after, alive, *held_in_hbm(radial_table.T, radius, harmonics))

    def turned_basis(after):
        return pl.pallas_call(
            turn_kernel,
            out_shape=(
                pltpu.VMEM((batches, near_blocks, width, points), bf16),
                pltpu.VMEM(partition.shape, f32),
                pltpu.VMEM((batches * near, ROWS, points), bf16),
                pltpu.VMEM((1, LANES), jnp.int32),
                pltpu.VMEM((batches, points), f32),
                pltpu.VMEM((1, LANES), jnp.int32),
            ),
            in_specs=[HBM] + [SMEM] * 4 + [HBM] * 3,
            out_specs=(VMEM,) * 6,
            scratch_shapes=[
                pltpu.VMEM(basis_values.shape, bf16),
                pltpu.VMEM(harmonics.shape, bf16),
                pltpu.SemaphoreType.DMA((4,)),
            ],
            compiler_params=WIDE,
            cost_estimate=work,
            name="turn",
        )(
            after, atom_near.T, batch_sizes, window_start, batch_offsets,
            *held_in_hbm(basis_values, partition, harmonics),
        )

    def selected(even, odd, starts, rows):
        return pl.pallas_call(
            functools.partial(select_kernel, even, odd, dev_count),
            out_shape=pltpu.VMEM((2,) + density_rows.shape[1:], bf16),
            in_specs=[SMEM, VMEM],
            out_specs=VMEM,
            compiler_params=PARAMS,
            name="select",
        )(starts, rows)

    if dev_count == 8:
        beside = crossed(window_start, "dev", 1)
        beside, rows = lax.optimization_barrier((beside, masked))
        first = turned(rows, 4, 2)
        starts = turned(jnp.concatenate([window_start, beside]), 2, 4)
        chosen = selected(0, 0, starts, masked)
        second = turned(chosen, 2, 4)
        first, later, _ = lax.optimization_barrier((first, masked, chosen))
        chosen = selected(4, 2, starts, first)
        third = turned(chosen, 2, 4)
        phit, weights, hpad, atom_rows, alive, places = turned_basis(chosen)
        second, phit = lax.optimization_barrier((second, phit))
        sent = (later, first, second, third)
        pieces = [piece for value in sent for piece in (value, crossed(value, "dev", 1))]
    else:
        phit, weights, hpad, atom_rows, alive, places = turned_basis(masked)
        pieces = [lax.all_gather(masked, "dev", axis=0)]

    density, terms = pl.pallas_call(
        density_kernel,
        out_shape=(
            pltpu.VMEM((batches, points), f32),
            pltpu.VMEM((ROWS, LANES), f32),
        ),
        in_specs=[SMEM] + [VMEM] * (5 + len(pieces)),
        out_specs=(VMEM, VMEM),
        scratch_shapes=[
            pltpu.VMEM((dev_count, band, width, width), bf16),
            pltpu.VMEM((LANES // SLOT, SLOT, points), f32),
        ],
        compiler_params=PARAMS,
        cost_estimate=pl.CostEstimate(flops=2_000_000_000, bytes_accessed=6_000_000, transcendentals=0),
        name="density",
    )(
        places, atom_rows, alive, phit, weights, hpad,
        *pieces,
    )

    def scattered(steps, pieces):
        return pl.pallas_call(
            functools.partial(scatter_kernel, comps, atoms, steps),
            out_shape=jax.ShapeDtypeStruct((ROWS, 3 * atoms), f32),
            in_specs=[VMEM] * len(pieces),
            out_specs=VMEM,
            compiler_params=PARAMS,
            name="scatter",
        )(*pieces)

    g_low = field(0, terms)
    if dev_count == 8 and region_count == 4:
        steps = (1, 2, 3)
        others = [crossed(terms, "region", m) for m in steps]
        *others, g_low = lax.optimization_barrier((*others, g_low))
        sums = scattered((0,) + steps, [terms] + others)
        sums = sums + crossed(sums, "dev", 1)
        groups = [sums] + [crossed(sums, "dev", m) for m in (2, 4, 6)]
        g_high = field(half, sums)
        *groups, g_high = lax.optimization_barrier((*groups, g_high))
    else:
        gathered = lax.all_gather(terms, "dev", axis=0)
        sums = scattered((0,) * dev_count, [gathered[m] for m in range(dev_count)])
        before, here, after = [sums[:, n * atoms : (n + 1) * atoms] for n in range(3)]
        low, high = shifted(sums, "region", 1), shifted(sums, "region", -1)
        before = before + low[:, atoms : 2 * atoms] + shifted(after, "region", 2)
        here = here + low[:, 2 * atoms :] + high[:, :atoms]
        after = after + high[:, atoms : 2 * atoms] + shifted(sums[:, :atoms], "region", -2)
        groups = [jnp.concatenate([before, here, after], axis=1)]
        g_high = field(half, terms)

    moments, potential = pl.pallas_call(
        functools.partial(potential_kernel, comps, atoms),
        out_shape=(
            jax.ShapeDtypeStruct((mine, comps), f32),
            jax.ShapeDtypeStruct((batches, points), f32),
        ),
        in_specs=[VMEM] * (3 + len(groups)),
        out_specs=(VMEM, VMEM),
        compiler_params=PARAMS,
        name="potential",
    )(atom_rows, g_low, g_high, *groups)
    return (density, moments.T, potential)


def solution(mesh):
    both = ("region", "dev")
    placed = (
        P(both, None, None, None),
        P(both, None, None, None),
        P(both, None),
        P(both),
        P(both, None),
        P(both, None),
        P(both, None),
        P(both, None, None, None),
        P(both, None, None),
        P(both, None, None),
        P(),
    )
    return jax.shard_map(
        per_device,
        mesh=mesh,
        in_specs=placed,
        out_specs=(P(both, None), P(None, both), P(both, None)),
        check_vma=False,
    )
```

```python
import functools
import jax
import jax.numpy as jnp
from jax import lax
from jax.experimental import pallas as pl
from jax.experimental.pallas import tpu as pltpu
from jax.sharding import PartitionSpec as P

EVEN_OWNERS = (0, 1, 4, 3, 2, 5, 6, 7)
ODD_OWNERS = (0, 1, 2, 5, 4, 3, 6, 7)
PIECE_ROWS = (None, None, None, None, 0, 1, 0, 1)
LANES = 128
ROWS = 32
SLOT = 8
NT = (((1,), (1,)), ((), ()))
NN = (((1,), (0,)), ((), ()))
VMEM = pl.BlockSpec(memory_space=pltpu.VMEM)
SMEM = pl.BlockSpec(memory_space=pltpu.SMEM)
HBM = pl.BlockSpec(memory_space=pltpu.HBM)
WIDE = pltpu.CompilerParams(vmem_limit_bytes=16 * 1024 * 1024)
PARAMS = pltpu.CompilerParams(vmem_limit_bytes=16 * 1024 * 1024)


def dot(a, b, dims=NN):
    return lax.dot_general(a, b, dims, preferred_element_type=jnp.float32)


def split2(x):
    hi = x.astype(jnp.bfloat16)
    lo = (x - hi.astype(jnp.float32)).astype(jnp.bfloat16)
    return hi, lo


def split3(x):
    hi, mid = split2(x)
    rest = x - hi.astype(jnp.float32) - mid.astype(jnp.float32)
    return hi, mid, rest.astype(jnp.bfloat16)


def cubic(distance):
    inner = 2.0 / 3.0 - distance * distance + 0.5 * distance * distance * distance
    remote = 2.0 - distance
    outer = remote * remote * remote * (1.0 / 6.0)
    return jnp.where(distance < 1.0, inner, jnp.where(distance < 2.0, outer, 0.0))


def chosen_row(owner, start, owners, stored):
    ahead = lax.rem(owner - start + stored * owners, owners)
    return ahead, lax.rem(start + ahead, stored * owners) // owners


def select_kernel(even, odd, owners, starts_ref, rows_ref, out_ref):
    me = lax.axis_index("dev")
    owner = lax.bitwise_xor(me, jnp.where(lax.rem(me, 2) == 1, odd, even))
    stored, band, width = rows_ref.shape[:3]
    starts = starts_ref[...]
    reach = starts + lax.bitwise_and(owner - starts, owners - 1)
    reach = jnp.where(reach >= stored * owners, reach - stored * owners, reach)
    for n in range(out_ref.shape[0]):
        spot = jnp.broadcast_to(reach[:, n : n + 1], (width, width))
        factors = [
            jnp.where((spot >= t * owners) & (spot < (t + 1) * owners), 1.0, 0.0).astype(jnp.bfloat16)
            for t in range(stored)
        ]
        for k in range(band):
            total = rows_ref[0, k] * factors[0]
            for t in range(1, stored):
                total = total + rows_ref[t, k] * factors[t]
            out_ref[n, k] = total


def mask_kernel(mask_hbm, rows_hbm, out_ref, mask, rows, sems):
    stored, band = rows.shape[:2]
    fetch = pltpu.make_async_copy(mask_hbm, mask, sems.at[stored])
    copies = [
        pltpu.make_async_copy(rows_hbm.at[t], rows.at[t], sems.at[t]) for t in range(stored)
    ]
    fetch.start()
    for copy in copies:
        copy.start()
    fetch.wait()
    factors = mask[...].astype(jnp.float32)
    for t, copy in enumerate(copies):
        copy.wait()
        for k in range(band):
            factor = jnp.broadcast_to(factors[t : t + 1, k : k + 1], rows.shape[2:])
            out_ref[t, k] = rows[t, k] * factor.astype(jnp.bfloat16)


def field_kernel(
    begin, after_hbm, alive_ref, table_hbm, radius_hbm, harm_hbm,
    g_ref, table_ref, radius_ref, harm_ref, sems,
):
    batches, near, comps, points = harm_ref.shape
    knots = table_ref.shape[0]
    span = pl.ds(begin, batches)
    moves = (
        (table_hbm, table_ref), (radius_hbm.at[span], radius_ref), (harm_hbm.at[span], harm_ref)
    )
    copies = [pltpu.make_async_copy(a, b, sems.at[n]) for n, (a, b) in enumerate(moves)]
    for copy in copies:
        copy.start()
    knot = lax.broadcasted_iota(jnp.int32, (knots, points), 0).astype(jnp.float32)
    for copy in copies:
        copy.wait()
    r_hi, r_lo = split2(table_ref[...].T)
    coeffs = jnp.concatenate([r_hi, r_hi, r_lo], axis=1)

    def body(b, carry):
        rows = radius_ref[b]
        alive = alive_ref[pl.ds(begin + b, 1), :]
        for i in range(near):
            spline = cubic(jnp.abs(rows[i : i + 1, :] - knot))
            s_hi, s_lo = split2(spline)
            radial = dot(coeffs, jnp.concatenate([s_hi, s_lo, s_hi], axis=0))
            g_ref[b * near + i] = radial * (harm_ref[b, i].astype(jnp.float32) * alive)
        return carry

    lax.fori_loop(0, batches, body, 0, unroll=2)


def turn_kernel(
    after_hbm, near_ref, size_ref, basis_hbm, part_hbm, harm_hbm,
    phit_ref, part_ref, hpad_ref, atom_ref, alive_ref, basis, harm_ref, sems,
):
    batches, near_blocks = basis.shape[:2]
    near, comps, points = harm_ref.shape[1:]
    halves = [pl.ds(0, batches // 2), pl.ds(batches // 2, batches - batches // 2)]
    copies = [
        pltpu.make_async_copy(basis_hbm.at[half], basis.at[half], sems.at[n])
        for n, half in enumerate(halves)
    ]
    copies.append(pltpu.make_async_copy(harm_hbm, harm_ref, sems.at[2]))
    copies.append(pltpu.make_async_copy(part_hbm, part_ref, sems.at[3]))
    for copy in copies:
        copy.start()
    lane = lax.broadcasted_iota(jnp.int32, atom_ref.shape, 1)
    atom = jnp.full(atom_ref.shape, -1, jnp.int32)
    for b in range(near_ref.shape[1]):
        for i in range(near):
            atom = jnp.where(lane == b * SLOT + i, near_ref[i, b], atom)
    atom_ref[...] = atom
    point = lax.broadcasted_iota(jnp.int32, (1, points), 1)
    for b in range(batches):
        alive_ref[b : b + 1, :] = (point < size_ref[0, b]).astype(jnp.float32)
    for n in range(batches * near):
        hpad_ref[n, ROWS // 2 :, :] = jnp.zeros((ROWS // 2, points), jnp.bfloat16)

    def turn(b, carry):
        for j in range(near_blocks):
            phit_ref[b, j] = basis[b, j].T
        return carry

    def pad(b, carry):
        for i in range(near):
            hpad_ref[b * near + i, 0:comps, :] = harm_ref[b, i]
        return carry

    copies[0].wait()
    lax.fori_loop(0, batches // 2, turn, 0)
    copies[1].wait()
    lax.fori_loop(batches // 2, batches, turn, 0)
    copies[2].wait()
    lax.fori_loop(0, batches, pad, 0)
    copies[3].wait()


def density_kernel(
    start_ref, offset_ref, atom_ref, alive_ref, phit_ref, part_ref, hpad_ref, *refs
):
    dens_ref, terms_ref, window_ref, w_ref = refs[-4:]
    pieces = refs[:-4]
    owners = window_ref.shape[0]
    batches, near_blocks, width, points = phit_ref.shape
    near = part_ref.shape[1]
    if len(pieces) == owners:
        me = lax.axis_index("dev")
        odd = lax.rem(me, 2) == 1
        held = [
            (piece, lax.bitwise_xor(me, jnp.where(odd, b, a)), at)
            for piece, a, b, at in zip(pieces, EVEN_OWNERS, ODD_OWNERS, PIECE_ROWS)
        ]
    else:
        held = [(pieces[0].at[owner], owner, None) for owner in range(owners)]
    stored = held[0][0].shape[0]
    for piece, owner, at in held:
        ahead, row = chosen_row(owner, start_ref[0], owners, stored)
        window_ref[ahead] = piece[row if at is None else at]
    w_ref[...] = jnp.zeros(w_ref.shape, w_ref.dtype)
    zero = jnp.zeros((width, width), jnp.bfloat16)

    def body(b, carry):
        first = offset_ref[0, b]
        left = []
        for j in range(near_blocks):
            row = [
                window_ref[first + j, f - j + 1] if 0 <= f - j + 1 < 4 else zero
                for f in range(near_blocks)
            ]
            left.append(jnp.concatenate(row, axis=1))
        right = phit_ref[b].reshape(near_blocks * width, points)
        mixed = dot(jnp.concatenate(left, axis=0), right)
        total = jnp.zeros((width, points), jnp.float32)
        for j in range(near_blocks):
            part = mixed[j * width : (j + 1) * width]
            total = total + part * phit_ref[b, j].astype(jnp.float32)
        summed = jnp.sum(total, axis=0, keepdims=True)
        row = summed * alive_ref[pl.ds(b, 1), :]
        dens_ref[pl.ds(b, 1), :] = row
        w_ref[b, 0:near, :] = part_ref[b] * row
        return carry

    for b in range(batches):
        body(b, 0)
    weights = w_ref[...].reshape(LANES, points)
    columns = jnp.concatenate(split2(weights), axis=0)
    slot = lax.broadcasted_iota(jnp.int32, (1, 2 * LANES), 1) % LANES
    terms = jnp.zeros((ROWS, 2 * LANES), jnp.float32)
    cross = dot(hpad_ref[...].reshape(batches * near * ROWS, points), columns, NT)
    for n in range(batches * near):
        b, i = divmod(n, near)
        here = cross[n * ROWS : (n + 1) * ROWS]
        terms = terms + jnp.where(slot == b * SLOT + i, here, 0.0)
    result = terms[:, :LANES] + terms[:, LANES:]
    row_id = lax.broadcasted_iota(jnp.int32, (ROWS, LANES), 0)
    comps = ROWS - 7
    terms_ref[...] = jnp.where(row_id == comps, atom_ref[...].astype(jnp.float32), result)


def scatter_kernel(comps, atoms, flip, *refs):
    own, near_a, near_b, far = refs[-4:]
    pieces = [group.at[m] for group in refs[:-4] for m in range(group.shape[0])]
    row_id = lax.broadcasted_iota(jnp.int32, (3 * atoms, LANES), 0)
    total = jnp.zeros((3 * ROWS, 3 * atoms), jnp.float32)
    for m in range(0, len(pieces), 2):
        left, right = [], []
        for values in (pieces[m][...], pieces[m + 1][...]):
            chosen = values[comps : comps + 1, :].astype(jnp.int32)
            right.append((row_id == chosen).astype(jnp.float32).astype(jnp.bfloat16))
            left.append(jnp.concatenate(split3(values), axis=0))
        total = total + dot(jnp.concatenate(left, axis=1), jnp.concatenate(right, axis=1), NT)
    sums = total[:ROWS] + total[ROWS : 2 * ROWS] + total[2 * ROWS :]
    own[...] = sums
    ahead, back = sums[:, atoms:], sums[:, : 2 * atoms]
    if flip:
        odd = lax.rem(lax.axis_index("region"), 2) == 1
        near_a[...] = jnp.where(odd, back, ahead)
        near_b[...] = jnp.where(odd, ahead, back)
    else:
        near_a[...] = ahead
        near_b[...] = back
    far[:, :atoms] = sums[:, :atoms]
    far[:, atoms:] = sums[:, 2 * atoms :]


def potential_kernel(
    comps, atoms, flip, own_ref, near_b_ref, fa_ref, fb_ref, near_a_ref, atom_ref,
    low_ref, high_ref, mom_ref, pot_ref,
):
    batches, points = pot_ref.shape
    near = 2 * low_ref.shape[0] // batches
    fields = [ref.at[n] for ref in (low_ref, high_ref) for n in range(ref.shape[0])]
    own = own_ref[...]
    near_a, near_b = near_a_ref[...], near_b_ref[...]
    if flip:
        odd = lax.rem(lax.axis_index("region"), 2) == 1
        low = jnp.where(odd, near_a, near_b)
        high = jnp.where(odd, near_b, near_a)
    else:
        low, high = near_a, near_b
    before = fa_ref[:, atoms:] + low[:, :atoms] + own[:, :atoms]
    here = low[:, atoms:] + own[:, atoms : 2 * atoms] + high[:, :atoms]
    after = own[:, 2 * atoms :] + high[:, atoms:] + fb_ref[:, :atoms]

    mine = mom_ref.shape[0]
    want = lax.broadcasted_iota(jnp.int32, (mine, atoms), 0) + lax.axis_index("dev") * mine
    keep = want == lax.broadcasted_iota(jnp.int32, (mine, atoms), 1)
    keep = keep.astype(jnp.float32).astype(jnp.bfloat16)
    taken = dot(keep, jnp.concatenate(split3(here), axis=0), NT)
    taken = taken[:, :ROWS] + taken[:, ROWS : 2 * ROWS] + taken[:, 2 * ROWS :]
    mom_ref[...] = taken[:, :comps]

    moments = jnp.concatenate([before, here, after], axis=1)
    row_id = lax.broadcasted_iota(jnp.int32, (3 * atoms, LANES), 0)
    pick = (row_id == atom_ref[...]).astype(jnp.float32).astype(jnp.bfloat16)
    got = dot(jnp.concatenate(split3(moments), axis=0), pick)
    chosen = got[:ROWS] + got[ROWS : 2 * ROWS] + got[2 * ROWS :]
    chosen = chosen[:comps]
    for b in range(batches):
        total = jnp.zeros((comps, points), jnp.float32)
        for i in range(near):
            column = chosen[:, b * SLOT + i : b * SLOT + i + 1]
            total = total + column * fields[b * near + i][...]
        pot_ref[b : b + 1, :] = jnp.sum(total, axis=0, keepdims=True)


def held_in_hbm(*values):
    return [pltpu.with_memory_space_constraint(value, pltpu.HBM) for value in values]


def crossed(value, axis, m):
    return lax.ppermute(value, axis, [(i, i ^ m) for i in range(lax.axis_size(axis))])


def turned(value, even, odd):
    count = lax.axis_size("dev")
    return lax.ppermute(value, "dev", [(i, i ^ (odd if i % 2 else even)) for i in range(count)])


def shifted(value, axis, step):
    count = lax.axis_size(axis)
    return lax.ppermute(value, axis, [(i, (i + step) % count) for i in range(count)])


def per_device(
    basis_values,
    density_rows,
    block_mask,
    window_start,
    batch_offsets,
    batch_sizes,
    atom_near,
    harmonics,
    partition,
    radius,
    radial_table,
):
    dev_count = lax.axis_size("dev")
    region_count = lax.axis_size("region")
    blocks_dev, band, width = density_rows.shape[:3]
    batches, near, comps, points = harmonics.shape
    near_blocks = basis_values.shape[1]
    mine = 16
    atoms = mine * dev_count
    f32, bf16 = jnp.float32, jnp.bfloat16

    work = pl.CostEstimate(flops=2_000_000_000, bytes_accessed=8_000_000, transcendentals=0)
    masked = pl.pallas_call(
        mask_kernel,
        out_shape=pltpu.VMEM(density_rows.shape, bf16),
        in_specs=[HBM, HBM],
        out_specs=VMEM,
        scratch_shapes=[
            pltpu.VMEM(block_mask.shape, jnp.int32),
            pltpu.VMEM(density_rows.shape, bf16),
            pltpu.SemaphoreType.DMA((blocks_dev + 1,)),
        ],
        compiler_params=PARAMS,
        cost_estimate=work,
        name="mask",
    )(*held_in_hbm(block_mask, density_rows))

    half = batches // 2

    def field(begin, after):
        return pl.pallas_call(
            functools.partial(field_kernel, begin),
            out_shape=pltpu.VMEM((half * near, comps, points), f32),
            in_specs=[HBM, VMEM] + [HBM] * 3,
            out_specs=VMEM,
            scratch_shapes=[
                pltpu.VMEM(radial_table.shape[::-1], f32),
                pltpu.VMEM((half,) + radius.shape[1:], f32),
                pltpu.VMEM((half,) + harmonics.shape[1:], bf16),
                pltpu.SemaphoreType.DMA((3,)),
            ],
            compiler_params=WIDE,
            cost_estimate=work,
            name="field",
        )(after, alive, *held_in_hbm(radial_table.T, radius, harmonics))

    def turned_basis(after):
        return pl.pallas_call(
            turn_kernel,
            out_shape=(
                pltpu.VMEM((batches, near_blocks, width, points), bf16),
                pltpu.VMEM(partition.shape, f32),
                pltpu.VMEM((batches * near, ROWS, points), bf16),
                pltpu.VMEM((1, LANES), jnp.int32),
                pltpu.VMEM((batches, points), f32),
            ),
            in_specs=[HBM, SMEM, SMEM] + [HBM] * 3,
            out_specs=(VMEM,) * 5,
            scratch_shapes=[
                pltpu.VMEM(basis_values.shape, bf16),
                pltpu.VMEM(harmonics.shape, bf16),
                pltpu.SemaphoreType.DMA((4,)),
            ],
            compiler_params=WIDE,
            cost_estimate=work,
            name="turn",
        )(after, atom_near.T, batch_sizes, *held_in_hbm(basis_values, partition, harmonics))

    def selected(even, odd, starts, rows):
        return pl.pallas_call(
            functools.partial(select_kernel, even, odd, dev_count),
            out_shape=pltpu.VMEM((2,) + density_rows.shape[1:], bf16),
            in_specs=[VMEM, VMEM],
            out_specs=VMEM,
            compiler_params=PARAMS,
            name="select",
        )(starts, rows)

    if dev_count == 8:
        opening = window_start[None]
        beside = crossed(opening, "dev", 1)
        beside, rows = lax.optimization_barrier((beside, masked))
        first = turned(rows, 4, 2)
        starts = turned(jnp.concatenate([opening, beside], axis=1), 2, 4)
        chosen = selected(0, 0, starts, masked)
        second = turned(chosen, 2, 4)
        first, later, _ = lax.optimization_barrier((first, masked, chosen))
        chosen = selected(4, 2, starts, first)
        third = turned(chosen, 2, 4)
        phit, weights, hpad, atom_rows, alive = turned_basis(chosen)
        second, phit = lax.optimization_barrier((second, phit))
        sent = (later, first, second, third)
        pieces = [piece for value in sent for piece in (value, crossed(value, "dev", 1))]
    else:
        phit, weights, hpad, atom_rows, alive = turned_basis(masked)
        pieces = [lax.all_gather(masked, "dev", axis=0)]

    density, terms = pl.pallas_call(
        density_kernel,
        out_shape=(
            pltpu.VMEM((batches, points), f32),
            pltpu.VMEM((ROWS, LANES), f32),
        ),
        in_specs=[SMEM] * 2 + [VMEM] * (5 + len(pieces)),
        out_specs=(VMEM, VMEM),
        scratch_shapes=[
            pltpu.VMEM((dev_count, band, width, width), bf16),
            pltpu.VMEM((LANES // SLOT, SLOT, points), f32),
        ],
        compiler_params=PARAMS,
        cost_estimate=pl.CostEstimate(flops=2_000_000_000, bytes_accessed=6_000_000, transcendentals=0),
        name="density",
    )(
        window_start, batch_offsets, atom_rows, alive, phit, weights, hpad,
        *pieces,
    )

    if dev_count == 8:
        both = jnp.stack([terms, crossed(terms, "dev", 1)])
        groups = [both] + [crossed(both, "dev", m) for m in (2, 4, 6)]
    else:
        groups = [lax.all_gather(terms, "dev", axis=0)]
    g_low = field(0, groups[0])
    *groups, g_low = lax.optimization_barrier((*groups, g_low))
    flip = region_count == 4
    own, near_a, near_b, far = pl.pallas_call(
        functools.partial(scatter_kernel, comps, atoms, flip),
        out_shape=tuple(jax.ShapeDtypeStruct((ROWS, n * atoms), f32) for n in (3, 2, 2, 2)),
        in_specs=[VMEM] * len(groups),
        out_specs=(VMEM,) * 4,
        compiler_params=PARAMS,
        name="scatter",
    )(*groups)
    g_high = field(half, own)
    if flip:
        near_b = crossed(near_b, "region", 3)
        far_a = far_b = crossed(far, "region", 2)
        near_a = crossed(near_a, "region", 1)
    else:
        far_a = shifted(far, "region", 2)
        far_b = shifted(far, "region", -2)
        near_a = shifted(near_a, "region", 1)
        near_b = shifted(near_b, "region", -1)

    near_b, far_a, far_b, near_a, g_high = lax.optimization_barrier(
        (near_b, far_a, far_b, near_a, g_high)
    )

    moments, potential = pl.pallas_call(
        functools.partial(potential_kernel, comps, atoms, flip),
        out_shape=(
            jax.ShapeDtypeStruct((mine, comps), f32),
            jax.ShapeDtypeStruct((batches, points), f32),
        ),
        in_specs=[VMEM] * 8,
        out_specs=(VMEM, VMEM),
        compiler_params=PARAMS,
        name="potential",
    )(own, near_b, far_a, far_b, near_a, atom_rows, g_low, g_high)
    return (density, moments.T, potential)


def solution(mesh):
    both = ("region", "dev")
    placed = (
        P(both, None, None, None),
        P(both, None, None, None),
        P(both, None),
        P(both),
        P(both, None),
        P(both, None),
        P(both, None),
        P(both, None, None, None),
        P(both, None, None),
        P(both, None, None),
        P(),
    )
    return jax.shard_map(
        per_device,
        mesh=mesh,
        in_specs=placed,
        out_specs=(P(both, None), P(None, both), P(both, None)),
        check_vma=False,
    )
```

```python
import functools
import jax
import jax.numpy as jnp
from jax import lax
from jax.experimental import pallas as pl
from jax.experimental.pallas import tpu as pltpu
from jax.sharding import PartitionSpec as P

EVEN_OWNERS = (0, 1, 4, 3, 2, 5, 6, 7)
ODD_OWNERS = (0, 1, 2, 5, 4, 3, 6, 7)
PIECE_ROWS = (None, None, None, None, 0, 1, 0, 1)
LANES = 128
ROWS = 32
SLOT = 8
NT = (((1,), (1,)), ((), ()))
NN = (((1,), (0,)), ((), ()))
VMEM = pl.BlockSpec(memory_space=pltpu.VMEM)
SMEM = pl.BlockSpec(memory_space=pltpu.SMEM)
HBM = pl.BlockSpec(memory_space=pltpu.HBM)
WIDE = pltpu.CompilerParams(vmem_limit_bytes=16 * 1024 * 1024)
PARAMS = pltpu.CompilerParams(vmem_limit_bytes=16 * 1024 * 1024)


def dot(a, b, dims=NN):
    return lax.dot_general(a, b, dims, preferred_element_type=jnp.float32)


def split2(x):
    hi = x.astype(jnp.bfloat16)
    lo = (x - hi.astype(jnp.float32)).astype(jnp.bfloat16)
    return hi, lo


def split3(x):
    hi, mid = split2(x)
    rest = x - hi.astype(jnp.float32) - mid.astype(jnp.float32)
    return hi, mid, rest.astype(jnp.bfloat16)


def cubic(distance):
    inner = 2.0 / 3.0 - distance * distance + 0.5 * distance * distance * distance
    remote = 2.0 - distance
    outer = remote * remote * remote * (1.0 / 6.0)
    return jnp.where(distance < 1.0, inner, jnp.where(distance < 2.0, outer, 0.0))


def chosen_row(owner, start, owners, stored):
    ahead = lax.rem(owner - start + stored * owners, owners)
    return ahead, lax.rem(start + ahead, stored * owners) // owners


def select_kernel(even, odd, owners, starts_ref, mask_ref, raw_ref, out_ref, rows_ref):
    factors = mask_ref[...].astype(jnp.float32)
    for t in range(raw_ref.shape[0]):
        for k in range(raw_ref.shape[1]):
            factor = jnp.broadcast_to(factors[t : t + 1, k : k + 1], raw_ref.shape[2:])
            rows_ref[t, k] = raw_ref[t, k] * factor.astype(jnp.bfloat16)
    pick_rows(even, odd, owners, starts_ref, rows_ref, out_ref)


def pick_rows(even, odd, owners, starts_ref, rows_ref, out_ref):
    me = lax.axis_index("dev")
    owner = lax.bitwise_xor(me, jnp.where(lax.rem(me, 2) == 1, odd, even))
    stored, band, width = rows_ref.shape[:3]
    starts = starts_ref[...]
    reach = starts + lax.bitwise_and(owner - starts, owners - 1)
    reach = jnp.where(reach >= stored * owners, reach - stored * owners, reach)
    for n in range(out_ref.shape[0]):
        spot = jnp.broadcast_to(reach[:, n : n + 1], (width, width))
        factors = [
            jnp.where((spot >= t * owners) & (spot < (t + 1) * owners), 1.0, 0.0).astype(jnp.bfloat16)
            for t in range(stored)
        ]
        for k in range(band):
            total = rows_ref[0, k] * factors[0]
            for t in range(1, stored):
                total = total + rows_ref[t, k] * factors[t]
            out_ref[n, k] = total


def mask_kernel(mask_hbm, rows_hbm, out_ref, mask, rows, sems):
    stored, band = rows.shape[:2]
    fetch = pltpu.make_async_copy(mask_hbm, mask, sems.at[stored])
    copies = [
        pltpu.make_async_copy(rows_hbm.at[t], rows.at[t], sems.at[t]) for t in range(stored)
    ]
    fetch.start()
    for copy in copies:
        copy.start()
    fetch.wait()
    factors = mask[...].astype(jnp.float32)
    for t, copy in enumerate(copies):
        copy.wait()
        for k in range(band):
            factor = jnp.broadcast_to(factors[t : t + 1, k : k + 1], rows.shape[2:])
            out_ref[t, k] = rows[t, k] * factor.astype(jnp.bfloat16)


def field_kernel(
    begin, after_hbm, alive_ref, table_hbm, radius_hbm, harm_hbm,
    g_ref, table_ref, radius_ref, harm_ref, sems,
):
    batches, near, comps, points = harm_ref.shape
    knots = table_ref.shape[0]
    span = pl.ds(begin, batches)
    moves = (
        (table_hbm, table_ref), (radius_hbm.at[span], radius_ref), (harm_hbm.at[span], harm_ref)
    )
    copies = [pltpu.make_async_copy(a, b, sems.at[n]) for n, (a, b) in enumerate(moves)]
    for copy in copies:
        copy.start()
    knot = lax.broadcasted_iota(jnp.int32, (knots, points), 0).astype(jnp.float32)
    for copy in copies:
        copy.wait()
    r_hi, r_lo = split2(table_ref[...].T)
    coeffs = jnp.concatenate([r_hi, r_hi, r_lo], axis=1)

    def body(b, carry):
        rows = radius_ref[b]
        alive = alive_ref[pl.ds(begin + b, 1), :]
        for i in range(near):
            spline = cubic(jnp.abs(rows[i : i + 1, :] - knot))
            s_hi, s_lo = split2(spline)
            radial = dot(coeffs, jnp.concatenate([s_hi, s_lo, s_hi], axis=0))
            g_ref[b * near + i] = radial * (harm_ref[b, i].astype(jnp.float32) * alive)
        return carry

    lax.fori_loop(0, batches, body, 0, unroll=2)


def turn_kernel(
    after_hbm, near_ref, size_ref, basis_hbm, part_hbm, harm_hbm,
    phit_ref, part_ref, hpad_ref, atom_ref, alive_ref, basis, harm_ref, sems,
):
    batches, near_blocks = basis.shape[:2]
    near, comps, points = harm_ref.shape[1:]
    halves = [pl.ds(0, batches // 2), pl.ds(batches // 2, batches - batches // 2)]
    copies = [
        pltpu.make_async_copy(basis_hbm.at[half], basis.at[half], sems.at[n])
        for n, half in enumerate(halves)
    ]
    copies.append(pltpu.make_async_copy(harm_hbm, harm_ref, sems.at[2]))
    copies.append(pltpu.make_async_copy(part_hbm, part_ref, sems.at[3]))
    for copy in copies:
        copy.start()
    lane = lax.broadcasted_iota(jnp.int32, atom_ref.shape, 1)
    atom = jnp.full(atom_ref.shape, -1, jnp.int32)
    for b in range(near_ref.shape[1]):
        for i in range(near):
            atom = jnp.where(lane == b * SLOT + i, near_ref[i, b], atom)
    atom_ref[...] = atom
    point = lax.broadcasted_iota(jnp.int32, (1, points), 1)
    for b in range(batches):
        alive_ref[b : b + 1, :] = (point < size_ref[0, b]).astype(jnp.float32)
    for n in range(batches * near):
        hpad_ref[n, ROWS // 2 :, :] = jnp.zeros((ROWS // 2, points), jnp.bfloat16)

    def turn(b, carry):
        for j in range(near_blocks):
            phit_ref[b, j] = basis[b, j].T
        return carry

    def pad(b, carry):
        for i in range(near):
            hpad_ref[b * near + i, 0:comps, :] = harm_ref[b, i]
        return carry

    copies[0].wait()
    lax.fori_loop(0, batches // 2, turn, 0)
    copies[1].wait()
    lax.fori_loop(batches // 2, batches, turn, 0)
    copies[2].wait()
    lax.fori_loop(0, batches, pad, 0)
    copies[3].wait()


def density_kernel(
    start_ref, offset_ref, atom_ref, alive_ref, phit_ref, part_ref, hpad_ref, *refs
):
    dens_ref, terms_ref, window_ref, w_ref = refs[-4:]
    pieces = refs[:-4]
    owners = window_ref.shape[0]
    batches, near_blocks, width, points = phit_ref.shape
    near = part_ref.shape[1]
    if len(pieces) == owners:
        me = lax.axis_index("dev")
        odd = lax.rem(me, 2) == 1
        held = [
            (piece, lax.bitwise_xor(me, jnp.where(odd, b, a)), at)
            for piece, a, b, at in zip(pieces, EVEN_OWNERS, ODD_OWNERS, PIECE_ROWS)
        ]
    else:
        held = [(pieces[0].at[owner], owner, None) for owner in range(owners)]
    stored = held[0][0].shape[0]
    for piece, owner, at in held:
        ahead, row = chosen_row(owner, start_ref[0], owners, stored)
        window_ref[ahead] = piece[row if at is None else at]
    w_ref[...] = jnp.zeros(w_ref.shape, w_ref.dtype)
    zero = jnp.zeros((width, width), jnp.bfloat16)

    def body(b, carry):
        first = offset_ref[0, b]
        left = []
        for j in range(near_blocks):
            row = [
                window_ref[first + j, f - j + 1] if 0 <= f - j + 1 < 4 else zero
                for f in range(near_blocks)
            ]
            left.append(jnp.concatenate(row, axis=1))
        right = phit_ref[b].reshape(near_blocks * width, points)
        mixed = dot(jnp.concatenate(left, axis=0), right)
        total = jnp.zeros((width, points), jnp.float32)
        for j in range(near_blocks):
            part = mixed[j * width : (j + 1) * width]
            total = total + part * phit_ref[b, j].astype(jnp.float32)
        summed = jnp.sum(total, axis=0, keepdims=True)
        row = summed * alive_ref[pl.ds(b, 1), :]
        dens_ref[pl.ds(b, 1), :] = row
        w_ref[b, 0:near, :] = part_ref[b] * row
        return carry

    for b in range(batches):
        body(b, 0)
    weights = w_ref[...].reshape(LANES, points)
    columns = jnp.concatenate(split2(weights), axis=0)
    slot = lax.broadcasted_iota(jnp.int32, (1, 2 * LANES), 1) % LANES
    terms = jnp.zeros((ROWS, 2 * LANES), jnp.float32)
    cross = dot(hpad_ref[...].reshape(batches * near * ROWS, points), columns, NT)
    for n in range(batches * near):
        b, i = divmod(n, near)
        here = cross[n * ROWS : (n + 1) * ROWS]
        terms = terms + jnp.where(slot == b * SLOT + i, here, 0.0)
    result = terms[:, :LANES] + terms[:, LANES:]
    row_id = lax.broadcasted_iota(jnp.int32, (ROWS, LANES), 0)
    comps = ROWS - 7
    terms_ref[...] = jnp.where(row_id == comps, atom_ref[...].astype(jnp.float32), result)


def scatter_kernel(comps, atoms, flip, *refs):
    own, near_a, near_b, far = refs[-4:]
    pieces = [group.at[m] for group in refs[:-4] for m in range(group.shape[0])]
    row_id = lax.broadcasted_iota(jnp.int32, (3 * atoms, LANES), 0)
    total = jnp.zeros((3 * ROWS, 3 * atoms), jnp.float32)
    for m in range(0, len(pieces), 2):
        left, right = [], []
        for values in (pieces[m][...], pieces[m + 1][...]):
            chosen = values[comps : comps + 1, :].astype(jnp.int32)
            right.append((row_id == chosen).astype(jnp.float32).astype(jnp.bfloat16))
            left.append(jnp.concatenate(split3(values), axis=0))
        total = total + dot(jnp.concatenate(left, axis=1), jnp.concatenate(right, axis=1), NT)
    sums = total[:ROWS] + total[ROWS : 2 * ROWS] + total[2 * ROWS :]
    own[...] = sums
    ahead, back = sums[:, atoms:], sums[:, : 2 * atoms]
    if flip:
        odd = lax.rem(lax.axis_index("region"), 2) == 1
        near_a[...] = jnp.where(odd, back, ahead)
        near_b[...] = jnp.where(odd, ahead, back)
    else:
        near_a[...] = ahead
        near_b[...] = back
    far[:, :atoms] = sums[:, :atoms]
    far[:, atoms:] = sums[:, 2 * atoms :]


def potential_kernel(
    comps, atoms, flip, own_ref, near_b_ref, fa_ref, fb_ref, near_a_ref, atom_ref,
    low_ref, high_ref, mom_ref, pot_ref,
):
    batches, points = pot_ref.shape
    near = 2 * low_ref.shape[0] // batches
    fields = [ref.at[n] for ref in (low_ref, high_ref) for n in range(ref.shape[0])]
    own = own_ref[...]
    near_a, near_b = near_a_ref[...], near_b_ref[...]
    if flip:
        odd = lax.rem(lax.axis_index("region"), 2) == 1
        low = jnp.where(odd, near_a, near_b)
        high = jnp.where(odd, near_b, near_a)
    else:
        low, high = near_a, near_b
    before = fa_ref[:, atoms:] + low[:, :atoms] + own[:, :atoms]
    here = low[:, atoms:] + own[:, atoms : 2 * atoms] + high[:, :atoms]
    after = own[:, 2 * atoms :] + high[:, atoms:] + fb_ref[:, :atoms]

    mine = mom_ref.shape[0]
    want = lax.broadcasted_iota(jnp.int32, (mine, atoms), 0) + lax.axis_index("dev") * mine
    keep = want == lax.broadcasted_iota(jnp.int32, (mine, atoms), 1)
    keep = keep.astype(jnp.float32).astype(jnp.bfloat16)
    taken = dot(keep, jnp.concatenate(split3(here), axis=0), NT)
    taken = taken[:, :ROWS] + taken[:, ROWS : 2 * ROWS] + taken[:, 2 * ROWS :]
    mom_ref[...] = taken[:, :comps]

    moments = jnp.concatenate([before, here, after], axis=1)
    row_id = lax.broadcasted_iota(jnp.int32, (3 * atoms, LANES), 0)
    pick = (row_id == atom_ref[...]).astype(jnp.float32).astype(jnp.bfloat16)
    got = dot(jnp.concatenate(split3(moments), axis=0), pick)
    chosen = got[:ROWS] + got[ROWS : 2 * ROWS] + got[2 * ROWS :]
    chosen = chosen[:comps]
    for b in range(batches):
        total = jnp.zeros((comps, points), jnp.float32)
        for i in range(near):
            column = chosen[:, b * SLOT + i : b * SLOT + i + 1]
            total = total + column * fields[b * near + i][...]
        pot_ref[b : b + 1, :] = jnp.sum(total, axis=0, keepdims=True)


def held_in_hbm(*values):
    return [pltpu.with_memory_space_constraint(value, pltpu.HBM) for value in values]


def crossed(value, axis, m):
    return lax.ppermute(value, axis, [(i, i ^ m) for i in range(lax.axis_size(axis))])


def turned(value, even, odd):
    count = lax.axis_size("dev")
    return lax.ppermute(value, "dev", [(i, i ^ (odd if i % 2 else even)) for i in range(count)])


def shifted(value, axis, step):
    count = lax.axis_size(axis)
    return lax.ppermute(value, axis, [(i, (i + step) % count) for i in range(count)])


def per_device(
    basis_values,
    density_rows,
    block_mask,
    window_start,
    batch_offsets,
    batch_sizes,
    atom_near,
    harmonics,
    partition,
    radius,
    radial_table,
):
    dev_count = lax.axis_size("dev")
    region_count = lax.axis_size("region")
    blocks_dev, band, width = density_rows.shape[:3]
    batches, near, comps, points = harmonics.shape
    near_blocks = basis_values.shape[1]
    mine = 16
    atoms = mine * dev_count
    f32, bf16 = jnp.float32, jnp.bfloat16

    work = pl.CostEstimate(flops=2_000_000_000, bytes_accessed=8_000_000, transcendentals=0)
    masked = pl.pallas_call(
        mask_kernel,
        out_shape=pltpu.VMEM(density_rows.shape, bf16),
        in_specs=[HBM, HBM],
        out_specs=VMEM,
        scratch_shapes=[
            pltpu.VMEM(block_mask.shape, jnp.int32),
            pltpu.VMEM(density_rows.shape, bf16),
            pltpu.SemaphoreType.DMA((blocks_dev + 1,)),
        ],
        compiler_params=PARAMS,
        cost_estimate=work,
        name="mask",
    )(*held_in_hbm(block_mask, density_rows))

    half = batches // 2

    def field(begin, after):
        return pl.pallas_call(
            functools.partial(field_kernel, begin),
            out_shape=pltpu.VMEM((half * near, comps, points), f32),
            in_specs=[HBM, VMEM] + [HBM] * 3,
            out_specs=VMEM,
            scratch_shapes=[
                pltpu.VMEM(radial_table.shape[::-1], f32),
                pltpu.VMEM((half,) + radius.shape[1:], f32),
                pltpu.VMEM((half,) + harmonics.shape[1:], bf16),
                pltpu.SemaphoreType.DMA((3,)),
            ],
            compiler_params=WIDE,
            cost_estimate=work,
            name="field",
        )(after, alive, *held_in_hbm(radial_table.T, radius, harmonics))

    def turned_basis(after):
        return pl.pallas_call(
            turn_kernel,
            out_shape=(
                pltpu.VMEM((batches, near_blocks, width, points), bf16),
                pltpu.VMEM(partition.shape, f32),
                pltpu.VMEM((batches * near, ROWS, points), bf16),
                pltpu.VMEM((1, LANES), jnp.int32),
                pltpu.VMEM((batches, points), f32),
            ),
            in_specs=[HBM, SMEM, SMEM] + [HBM] * 3,
            out_specs=(VMEM,) * 5,
            scratch_shapes=[
                pltpu.VMEM(basis_values.shape, bf16),
                pltpu.VMEM(harmonics.shape, bf16),
                pltpu.SemaphoreType.DMA((4,)),
            ],
            compiler_params=WIDE,
            cost_estimate=work,
            name="turn",
        )(after, atom_near.T, batch_sizes, *held_in_hbm(basis_values, partition, harmonics))

    def selected(even, odd, starts, rows, mask=None):
        picked = pltpu.VMEM((2,) + density_rows.shape[1:], bf16)
        kernel = pick_rows if mask is None else select_kernel
        operands = (starts, rows) if mask is None else (starts, mask, rows)
        return pl.pallas_call(
            functools.partial(kernel, even, odd, dev_count),
            out_shape=picked if mask is None else (picked, pltpu.VMEM(density_rows.shape, bf16)),
            in_specs=[VMEM] * len(operands),
            out_specs=VMEM if mask is None else (VMEM, VMEM),
            compiler_params=PARAMS,
            name="select",
        )(*operands)

    if dev_count == 8:
        opening = window_start[None]
        first = turned(density_rows, 4, 2)
        beside = crossed(opening, "dev", 1)
        beside, masked = lax.optimization_barrier((beside, masked))
        starts = turned(jnp.concatenate([opening, beside], axis=1), 2, 4)
        first_mask = turned(block_mask, 4, 2)
        chosen = selected(0, 0, starts, masked)
        second = turned(chosen, 2, 4)
        first, later, first_mask, _ = lax.optimization_barrier((first, masked, first_mask, chosen))
        chosen, first = selected(4, 2, starts, first, first_mask)
        third = turned(chosen, 2, 4)
        phit, weights, hpad, atom_rows, alive = turned_basis(chosen)
        second, phit = lax.optimization_barrier((second, phit))
        sent = (later, first, second, third)
        pieces = [piece for value in sent for piece in (value, crossed(value, "dev", 1))]
    else:
        phit, weights, hpad, atom_rows, alive = turned_basis(masked)
        pieces = [lax.all_gather(masked, "dev", axis=0)]

    density, terms = pl.pallas_call(
        density_kernel,
        out_shape=(
            pltpu.VMEM((batches, points), f32),
            pltpu.VMEM((ROWS, LANES), f32),
        ),
        in_specs=[SMEM] * 2 + [VMEM] * (5 + len(pieces)),
        out_specs=(VMEM, VMEM),
        scratch_shapes=[
            pltpu.VMEM((dev_count, band, width, width), bf16),
            pltpu.VMEM((LANES // SLOT, SLOT, points), f32),
        ],
        compiler_params=PARAMS,
        cost_estimate=pl.CostEstimate(flops=2_000_000_000, bytes_accessed=6_000_000, transcendentals=0),
        name="density",
    )(
        window_start, batch_offsets, atom_rows, alive, phit, weights, hpad,
        *pieces,
    )

    if dev_count == 8:
        both = jnp.stack([terms, crossed(terms, "dev", 1)])
        groups = [both] + [crossed(both, "dev", m) for m in (2, 4, 6)]
    else:
        groups = [lax.all_gather(terms, "dev", axis=0)]
    g_low = field(0, groups[0])
    *groups, g_low = lax.optimization_barrier((*groups, g_low))
    flip = region_count == 4
    own, near_a, near_b, far = pl.pallas_call(
        functools.partial(scatter_kernel, comps, atoms, flip),
        out_shape=tuple(jax.ShapeDtypeStruct((ROWS, n * atoms), f32) for n in (3, 2, 2, 2)),
        in_specs=[VMEM] * len(groups),
        out_specs=(VMEM,) * 4,
        compiler_params=PARAMS,
        name="scatter",
    )(*groups)
    g_high = field(half, own)
    if flip:
        near_b = crossed(near_b, "region", 3)
        far_a = far_b = crossed(far, "region", 2)
        near_a = crossed(near_a, "region", 1)
    else:
        far_a = shifted(far, "region", 2)
        far_b = shifted(far, "region", -2)
        near_a = shifted(near_a, "region", 1)
        near_b = shifted(near_b, "region", -1)

    near_b, far_a, far_b, near_a, g_high = lax.optimization_barrier(
        (near_b, far_a, far_b, near_a, g_high)
    )

    moments, potential = pl.pallas_call(
        functools.partial(potential_kernel, comps, atoms, flip),
        out_shape=(
            jax.ShapeDtypeStruct((mine, comps), f32),
            jax.ShapeDtypeStruct((batches, points), f32),
        ),
        in_specs=[VMEM] * 8,
        out_specs=(VMEM, VMEM),
        compiler_params=PARAMS,
        name="potential",
    )(own, near_b, far_a, far_b, near_a, atom_rows, g_low, g_high)
    return (density, moments.T, potential)


def solution(mesh):
    both = ("region", "dev")
    placed = (
        P(both, None, None, None),
        P(both, None, None, None),
        P(both, None),
        P(both),
        P(both, None),
        P(both, None),
        P(both, None),
        P(both, None, None, None),
        P(both, None, None),
        P(both, None, None),
        P(),
    )
    return jax.shard_map(
        per_device,
        mesh=mesh,
        in_specs=placed,
        out_specs=(P(both, None), P(None, both), P(both, None)),
        check_vma=False,
    )
```

```python
import functools
import jax
import jax.numpy as jnp
from jax import lax
from jax.experimental import pallas as pl
from jax.experimental.pallas import tpu as pltpu
from jax.sharding import PartitionSpec as P

EVEN_OWNERS = (0, 1, 4, 3, 2, 5, 6, 7)
ODD_OWNERS = (0, 1, 2, 5, 4, 3, 6, 7)
PIECE_ROWS = (None, None, None, None, 0, 1, 0, 1)
LANES = 128
ROWS = 32
SLOT = 8
NT = (((1,), (1,)), ((), ()))
NN = (((1,), (0,)), ((), ()))
VMEM = pl.BlockSpec(memory_space=pltpu.VMEM)
SMEM = pl.BlockSpec(memory_space=pltpu.SMEM)
HBM = pl.BlockSpec(memory_space=pltpu.HBM)
WIDE = pltpu.CompilerParams(vmem_limit_bytes=16 * 1024 * 1024)
PARAMS = pltpu.CompilerParams(vmem_limit_bytes=16 * 1024 * 1024)


def dot(a, b, dims=NN):
    return lax.dot_general(a, b, dims, preferred_element_type=jnp.float32)


def split2(x):
    hi = x.astype(jnp.bfloat16)
    lo = (x - hi.astype(jnp.float32)).astype(jnp.bfloat16)
    return hi, lo


def split3(x):
    hi, mid = split2(x)
    rest = x - hi.astype(jnp.float32) - mid.astype(jnp.float32)
    return hi, mid, rest.astype(jnp.bfloat16)


def cubic(distance):
    inner = 2.0 / 3.0 - distance * distance + 0.5 * distance * distance * distance
    remote = 2.0 - distance
    outer = remote * remote * remote * (1.0 / 6.0)
    return jnp.where(distance < 1.0, inner, jnp.where(distance < 2.0, outer, 0.0))


def chosen_row(owner, start, owners, stored):
    ahead = lax.rem(owner - start + stored * owners, owners)
    return ahead, lax.rem(start + ahead, stored * owners) // owners


def select_kernel(even, odd, owners, starts_ref, rows_ref, out_ref):
    me = lax.axis_index("dev")
    owner = lax.bitwise_xor(me, jnp.where(lax.rem(me, 2) == 1, odd, even))
    stored, band, width = rows_ref.shape[:3]
    starts = starts_ref[...]
    reach = starts + lax.bitwise_and(owner - starts, owners - 1)
    reach = jnp.where(reach >= stored * owners, reach - stored * owners, reach)
    for n in range(out_ref.shape[0]):
        spot = jnp.broadcast_to(reach[:, n : n + 1], (width, width))
        factors = [
            jnp.where((spot >= t * owners) & (spot < (t + 1) * owners), 1.0, 0.0).astype(jnp.bfloat16)
            for t in range(stored)
        ]
        for k in range(band):
            total = rows_ref[0, k] * factors[0]
            for t in range(1, stored):
                total = total + rows_ref[t, k] * factors[t]
            out_ref[n, k] = total


def mask_kernel(mask_hbm, rows_hbm, out_ref, mask, rows, sems):
    stored, band = rows.shape[:2]
    fetch = pltpu.make_async_copy(mask_hbm, mask, sems.at[stored])
    copies = [
        pltpu.make_async_copy(rows_hbm.at[t], rows.at[t], sems.at[t]) for t in range(stored)
    ]
    fetch.start()
    for copy in copies:
        copy.start()
    fetch.wait()
    factors = mask[...].astype(jnp.float32)
    for t, copy in enumerate(copies):
        copy.wait()
        for k in range(band):
            factor = jnp.broadcast_to(factors[t : t + 1, k : k + 1], rows.shape[2:])
            out_ref[t, k] = rows[t, k] * factor.astype(jnp.bfloat16)


def field_kernel(
    begin, after_hbm, alive_ref, table_hbm, radius_hbm, harm_hbm,
    g_ref, table_ref, radius_ref, harm_ref, sems,
):
    batches, near, comps, points = harm_ref.shape
    knots = table_ref.shape[0]
    span = pl.ds(begin, batches)
    moves = (
        (table_hbm, table_ref), (radius_hbm.at[span], radius_ref), (harm_hbm.at[span], harm_ref)
    )
    copies = [pltpu.make_async_copy(a, b, sems.at[n]) for n, (a, b) in enumerate(moves)]
    for copy in copies:
        copy.start()
    knot = lax.broadcasted_iota(jnp.int32, (knots, points), 0).astype(jnp.float32)
    for copy in copies:
        copy.wait()
    r_hi, r_lo = split2(table_ref[...].T)
    coeffs = jnp.concatenate([r_hi, r_hi, r_lo], axis=1)

    def body(b, carry):
        rows = radius_ref[b]
        alive = alive_ref[pl.ds(begin + b, 1), :]
        for i in range(near):
            spline = cubic(jnp.abs(rows[i : i + 1, :] - knot))
            s_hi, s_lo = split2(spline)
            radial = dot(coeffs, jnp.concatenate([s_hi, s_lo, s_hi], axis=0))
            g_ref[b * near + i] = radial * (harm_ref[b, i].astype(jnp.float32) * alive)
        return carry

    lax.fori_loop(0, batches, body, 0, unroll=2)


def turn_kernel(
    after_hbm, near_ref, size_ref, basis_hbm, part_hbm, harm_hbm,
    phit_ref, part_ref, hpad_ref, atom_ref, alive_ref, basis, harm_ref, sems,
):
    batches, near_blocks = basis.shape[:2]
    near, comps, points = harm_ref.shape[1:]
    halves = [pl.ds(0, batches // 2), pl.ds(batches // 2, batches - batches // 2)]
    copies = [
        pltpu.make_async_copy(basis_hbm.at[half], basis.at[half], sems.at[n])
        for n, half in enumerate(halves)
    ]
    copies.append(pltpu.make_async_copy(harm_hbm, harm_ref, sems.at[2]))
    copies.append(pltpu.make_async_copy(part_hbm, part_ref, sems.at[3]))
    for copy in copies:
        copy.start()
    lane = lax.broadcasted_iota(jnp.int32, atom_ref.shape, 1)
    atom = jnp.full(atom_ref.shape, -1, jnp.int32)
    for b in range(near_ref.shape[1]):
        for i in range(near):
            atom = jnp.where(lane == b * SLOT + i, near_ref[i, b], atom)
    atom_ref[...] = atom
    point = lax.broadcasted_iota(jnp.int32, (1, points), 1)
    for b in range(batches):
        alive_ref[b : b + 1, :] = (point < size_ref[0, b]).astype(jnp.float32)
    for n in range(batches * near):
        hpad_ref[n, ROWS // 2 :, :] = jnp.zeros((ROWS // 2, points), jnp.bfloat16)

    def turn(b, carry):
        for j in range(near_blocks):
            phit_ref[b, j] = basis[b, j].T
        return carry

    def pad(b, carry):
        for i in range(near):
            hpad_ref[b * near + i, 0:comps, :] = harm_ref[b, i]
        return carry

    copies[0].wait()
    lax.fori_loop(0, batches // 2, turn, 0)
    copies[1].wait()
    lax.fori_loop(batches // 2, batches, turn, 0)
    copies[2].wait()
    lax.fori_loop(0, batches, pad, 0)
    copies[3].wait()


def density_kernel(
    start_ref, offset_ref, atom_ref, alive_ref, phit_ref, part_ref, hpad_ref, *refs
):
    dens_ref, terms_ref, window_ref, w_ref = refs[-4:]
    pieces = refs[:-4]
    owners = window_ref.shape[0]
    batches, near_blocks, width, points = phit_ref.shape
    near = part_ref.shape[1]
    if len(pieces) == owners:
        me = lax.axis_index("dev")
        odd = lax.rem(me, 2) == 1
        held = [
            (piece, lax.bitwise_xor(me, jnp.where(odd, b, a)), at)
            for piece, a, b, at in zip(pieces, EVEN_OWNERS, ODD_OWNERS, PIECE_ROWS)
        ]
    else:
        held = [(pieces[0].at[owner], owner, None) for owner in range(owners)]
    stored = held[0][0].shape[0]
    for piece, owner, at in held:
        ahead, row = chosen_row(owner, start_ref[0], owners, stored)
        window_ref[ahead] = piece[row if at is None else at]
    w_ref[...] = jnp.zeros(w_ref.shape, w_ref.dtype)
    zero = jnp.zeros((width, width), jnp.bfloat16)

    def body(b, carry):
        first = offset_ref[0, b]
        left = []
        for j in range(near_blocks):
            row = [
                window_ref[first + j, f - j + 1] if 0 <= f - j + 1 < 4 else zero
                for f in range(near_blocks)
            ]
            left.append(jnp.concatenate(row, axis=1))
        right = phit_ref[b].reshape(near_blocks * width, points)
        mixed = dot(jnp.concatenate(left, axis=0), right)
        total = jnp.zeros((width, points), jnp.float32)
        for j in range(near_blocks):
            part = mixed[j * width : (j + 1) * width]
            total = total + part * phit_ref[b, j].astype(jnp.float32)
        summed = jnp.sum(total, axis=0, keepdims=True)
        row = summed * alive_ref[pl.ds(b, 1), :]
        dens_ref[pl.ds(b, 1), :] = row
        w_ref[b, 0:near, :] = part_ref[b] * row
        return carry

    for b in range(batches):
        body(b, 0)
    weights = w_ref[...].reshape(LANES, points)
    columns = jnp.concatenate(split2(weights), axis=0)
    slot = lax.broadcasted_iota(jnp.int32, (1, 2 * LANES), 1) % LANES
    terms = jnp.zeros((ROWS, 2 * LANES), jnp.float32)
    cross = dot(hpad_ref[...].reshape(batches * near * ROWS, points), columns, NT)
    for n in range(batches * near):
        b, i = divmod(n, near)
        here = cross[n * ROWS : (n + 1) * ROWS]
        terms = terms + jnp.where(slot == b * SLOT + i, here, 0.0)
    result = terms[:, :LANES] + terms[:, LANES:]
    row_id = lax.broadcasted_iota(jnp.int32, (ROWS, LANES), 0)
    comps = ROWS - 7
    terms_ref[...] = jnp.where(row_id == comps, atom_ref[...].astype(jnp.float32), result)


def scatter_kernel(comps, atoms, flip, *refs):
    own, near_a, near_b, far = refs[-4:]
    pieces = [group.at[m] for group in refs[:-4] for m in range(group.shape[0])]
    row_id = lax.broadcasted_iota(jnp.int32, (3 * atoms, LANES), 0)
    total = jnp.zeros((3 * ROWS, 3 * atoms), jnp.float32)
    for m in range(0, len(pieces), 2):
        left, right = [], []
        for values in (pieces[m][...], pieces[m + 1][...]):
            chosen = values[comps : comps + 1, :].astype(jnp.int32)
            right.append((row_id == chosen).astype(jnp.float32).astype(jnp.bfloat16))
            left.append(jnp.concatenate(split3(values), axis=0))
        total = total + dot(jnp.concatenate(left, axis=1), jnp.concatenate(right, axis=1), NT)
    sums = total[:ROWS] + total[ROWS : 2 * ROWS] + total[2 * ROWS :]
    own[...] = sums
    ahead, back = sums[:, atoms:], sums[:, : 2 * atoms]
    if flip:
        odd = lax.rem(lax.axis_index("region"), 2) == 1
        near_a[...] = jnp.where(odd, back, ahead)
        near_b[...] = jnp.where(odd, ahead, back)
    else:
        near_a[...] = ahead
        near_b[...] = back
    far[:, :atoms] = sums[:, :atoms]
    far[:, atoms:] = sums[:, 2 * atoms :]


def potential_kernel(
    comps, atoms, flip, own_ref, fa_ref, fb_ref, near_b_ref, near_a_ref, atom_ref,
    low_ref, high_ref, mom_ref, pot_ref,
):
    batches, points = pot_ref.shape
    near = 2 * low_ref.shape[0] // batches
    fields = [ref.at[n] for ref in (low_ref, high_ref) for n in range(ref.shape[0])]
    own = own_ref[...]
    near_a, near_b = near_a_ref[...], near_b_ref[...]
    if flip:
        odd = lax.rem(lax.axis_index("region"), 2) == 1
        low = jnp.where(odd, near_a, near_b)
        high = jnp.where(odd, near_b, near_a)
    else:
        low, high = near_a, near_b
    before = fa_ref[:, atoms:] + low[:, :atoms] + own[:, :atoms]
    here = low[:, atoms:] + own[:, atoms : 2 * atoms] + high[:, :atoms]
    after = own[:, 2 * atoms :] + high[:, atoms:] + fb_ref[:, :atoms]

    mine = mom_ref.shape[0]
    want = lax.broadcasted_iota(jnp.int32, (mine, atoms), 0) + lax.axis_index("dev") * mine
    keep = want == lax.broadcasted_iota(jnp.int32, (mine, atoms), 1)
    keep = keep.astype(jnp.float32).astype(jnp.bfloat16)
    taken = dot(keep, jnp.concatenate(split3(here), axis=0), NT)
    taken = taken[:, :ROWS] + taken[:, ROWS : 2 * ROWS] + taken[:, 2 * ROWS :]
    mom_ref[...] = taken[:, :comps]

    moments = jnp.concatenate([before, here, after], axis=1)
    row_id = lax.broadcasted_iota(jnp.int32, (3 * atoms, LANES), 0)
    pick = (row_id == atom_ref[...]).astype(jnp.float32).astype(jnp.bfloat16)
    got = dot(jnp.concatenate(split3(moments), axis=0), pick)
    chosen = got[:ROWS] + got[ROWS : 2 * ROWS] + got[2 * ROWS :]
    chosen = chosen[:comps]
    for b in range(batches):
        total = jnp.zeros((comps, points), jnp.float32)
        for i in range(near):
            column = chosen[:, b * SLOT + i : b * SLOT + i + 1]
            total = total + column * fields[b * near + i][...]
        pot_ref[b : b + 1, :] = jnp.sum(total, axis=0, keepdims=True)


def held_in_hbm(*values):
    return [pltpu.with_memory_space_constraint(value, pltpu.HBM) for value in values]


def crossed(value, axis, m):
    return lax.ppermute(value, axis, [(i, i ^ m) for i in range(lax.axis_size(axis))])


def turned(value, even, odd):
    count = lax.axis_size("dev")
    return lax.ppermute(value, "dev", [(i, i ^ (odd if i % 2 else even)) for i in range(count)])


def shifted(value, axis, step):
    count = lax.axis_size(axis)
    return lax.ppermute(value, axis, [(i, (i + step) % count) for i in range(count)])


def per_device(
    basis_values,
    density_rows,
    block_mask,
    window_start,
    batch_offsets,
    batch_sizes,
    atom_near,
    harmonics,
    partition,
    radius,
    radial_table,
):
    dev_count = lax.axis_size("dev")
    region_count = lax.axis_size("region")
    blocks_dev, band, width = density_rows.shape[:3]
    batches, near, comps, points = harmonics.shape
    near_blocks = basis_values.shape[1]
    mine = 16
    atoms = mine * dev_count
    f32, bf16 = jnp.float32, jnp.bfloat16

    work = pl.CostEstimate(flops=2_000_000_000, bytes_accessed=8_000_000, transcendentals=0)
    masked = pl.pallas_call(
        mask_kernel,
        out_shape=pltpu.VMEM(density_rows.shape, bf16),
        in_specs=[HBM, HBM],
        out_specs=VMEM,
        scratch_shapes=[
            pltpu.VMEM(block_mask.shape, jnp.int32),
            pltpu.VMEM(density_rows.shape, bf16),
            pltpu.SemaphoreType.DMA((blocks_dev + 1,)),
        ],
        compiler_params=PARAMS,
        cost_estimate=work,
        name="mask",
    )(*held_in_hbm(block_mask, density_rows))

    half = batches // 2

    def field(begin, after):
        return pl.pallas_call(
            functools.partial(field_kernel, begin),
            out_shape=pltpu.VMEM((half * near, comps, points), f32),
            in_specs=[HBM, VMEM] + [HBM] * 3,
            out_specs=VMEM,
            scratch_shapes=[
                pltpu.VMEM(radial_table.shape[::-1], f32),
                pltpu.VMEM((half,) + radius.shape[1:], f32),
                pltpu.VMEM((half,) + harmonics.shape[1:], bf16),
                pltpu.SemaphoreType.DMA((3,)),
            ],
            compiler_params=WIDE,
            cost_estimate=work,
            name="field",
        )(after, alive, *held_in_hbm(radial_table.T, radius, harmonics))

    def turned_basis(after):
        return pl.pallas_call(
            turn_kernel,
            out_shape=(
                pltpu.VMEM((batches, near_blocks, width, points), bf16),
                pltpu.VMEM(partition.shape, f32),
                pltpu.VMEM((batches * near, ROWS, points), bf16),
                pltpu.VMEM((1, LANES), jnp.int32),
                pltpu.VMEM((batches, points), f32),
            ),
            in_specs=[HBM, SMEM, SMEM] + [HBM] * 3,
            out_specs=(VMEM,) * 5,
            scratch_shapes=[
                pltpu.VMEM(basis_values.shape, bf16),
                pltpu.VMEM(harmonics.shape, bf16),
                pltpu.SemaphoreType.DMA((4,)),
            ],
            compiler_params=WIDE,
            cost_estimate=work,
            name="turn",
        )(after, atom_near.T, batch_sizes, *held_in_hbm(basis_values, partition, harmonics))

    def selected(even, odd, starts, rows):
        return pl.pallas_call(
            functools.partial(select_kernel, even, odd, dev_count),
            out_shape=pltpu.VMEM((2,) + density_rows.shape[1:], bf16),
            in_specs=[VMEM, VMEM],
            out_specs=VMEM,
            compiler_params=PARAMS,
            name="select",
        )(starts, rows)

    if dev_count == 8:
        opening = window_start[None]
        beside = crossed(opening, "dev", 1)
        beside, rows = lax.optimization_barrier((beside, masked))
        first = turned(rows, 4, 2)
        starts = turned(jnp.concatenate([opening, beside], axis=1), 2, 4)
        chosen = selected(0, 0, starts, masked)
        second = turned(chosen, 2, 4)
        first, later, _ = lax.optimization_barrier((first, masked, chosen))
        chosen = selected(4, 2, starts, first)
        third = turned(chosen, 2, 4)
        phit, weights, hpad, atom_rows, alive = turned_basis(chosen)
        second, phit = lax.optimization_barrier((second, phit))
        sent = (later, first, second, third)
        pieces = [piece for value in sent for piece in (value, crossed(value, "dev", 1))]
    else:
        phit, weights, hpad, atom_rows, alive = turned_basis(masked)
        pieces = [lax.all_gather(masked, "dev", axis=0)]

    density, terms = pl.pallas_call(
        density_kernel,
        out_shape=(
            pltpu.VMEM((batches, points), f32),
            pltpu.VMEM((ROWS, LANES), f32),
        ),
        in_specs=[SMEM] * 2 + [VMEM] * (5 + len(pieces)),
        out_specs=(VMEM, VMEM),
        scratch_shapes=[
            pltpu.VMEM((dev_count, band, width, width), bf16),
            pltpu.VMEM((LANES // SLOT, SLOT, points), f32),
        ],
        compiler_params=PARAMS,
        cost_estimate=pl.CostEstimate(flops=2_000_000_000, bytes_accessed=6_000_000, transcendentals=0),
        name="density",
    )(
        window_start, batch_offsets, atom_rows, alive, phit, weights, hpad,
        *pieces,
    )

    if dev_count == 8:
        both = jnp.stack([terms, crossed(terms, "dev", 1)])
        groups = [both] + [crossed(both, "dev", m) for m in (2, 4, 6)]
    else:
        groups = [lax.all_gather(terms, "dev", axis=0)]
    g_low = field(0, groups[0])
    *groups, g_low = lax.optimization_barrier((*groups, g_low))
    flip = region_count == 4
    own, near_a, near_b, far = pl.pallas_call(
        functools.partial(scatter_kernel, comps, atoms, flip),
        out_shape=tuple(jax.ShapeDtypeStruct((ROWS, n * atoms), f32) for n in (3, 2, 2, 2)),
        in_specs=[VMEM] * len(groups),
        out_specs=(VMEM,) * 4,
        compiler_params=PARAMS,
        name="scatter",
    )(*groups)
    g_high = field(half, own)
    if flip:
        far_a = far_b = crossed(far, "region", 2)
        near_b = crossed(near_b, "region", 3)
        near_a = crossed(near_a, "region", 1)
    else:
        far_a = shifted(far, "region", 2)
        far_b = shifted(far, "region", -2)
        near_a = shifted(near_a, "region", 1)
        near_b = shifted(near_b, "region", -1)

    far_a, far_b, near_b, near_a, g_high = lax.optimization_barrier(
        (far_a, far_b, near_b, near_a, g_high)
    )

    moments, potential = pl.pallas_call(
        functools.partial(potential_kernel, comps, atoms, flip),
        out_shape=(
            jax.ShapeDtypeStruct((mine, comps), f32),
            jax.ShapeDtypeStruct((batches, points), f32),
        ),
        in_specs=[VMEM] * 8,
        out_specs=(VMEM, VMEM),
        compiler_params=PARAMS,
        name="potential",
    )(own, far_a, far_b, near_b, near_a, atom_rows, g_low, g_high)
    return (density, moments.T, potential)


def solution(mesh):
    both = ("region", "dev")
    placed = (
        P(both, None, None, None),
        P(both, None, None, None),
        P(both, None),
        P(both),
        P(both, None),
        P(both, None),
        P(both, None),
        P(both, None, None, None),
        P(both, None, None),
        P(both, None, None),
        P(),
    )
    return jax.shard_map(
        per_device,
        mesh=mesh,
        in_specs=placed,
        out_specs=(P(both, None), P(None, both), P(both, None)),
        check_vma=False,
    )
```
